32 devices in a mesh: rows: 4 (over z), cols: 8 (over y, x, core).
Axes of the slice: x: 2, y: 2, z: 4, core: 2. Of those that a mesh axis runs over, the one named last changes fastest.
Arguments:
- slab: bfloat16 [8192, 8192], P('rows', 'cols'), may hold values from -6 to 6
- transforms: bfloat16 [8, 16384, 512], P('cols', 'rows'), may hold values from -0.25 to 0.25
- owners: int32 [2, 4], replicated, may hold values from 0 to 7, as said below
Outputs:
- updated: bfloat16 [8192, 8192], P('rows', 'cols')
The draws below stay inside these ranges and needn't reach their ends.
Inputs may be any that keep to these rules, and one draw needn't show every extreme that they name: For each row block, the owners of different rounds differ.
All inputs are finite; a program needn't handle non-finite values.
Results may differ from the reference program's by a relative error of at most 0.0063.
Values may be sent and summed in bfloat16 or wider, within the bound.
No kernel may reach another device: no remote copies, remote signals or barrier semaphores. Data moves between devices by JAX's collectives and lax.ppermute only.
A program may use at most 64 MiB of HBM per device.

```python
import jax
import jax.numpy as jnp
from jax import lax

W = 512
ROUNDS = 2
WINS = 4
STAGGER = 256
SLAB_ROWS = 8192
SLAB_COLS = 8192
POOL_ROWS = 16384
N_ROWS = 4
N_COLS = 8


def place_value(shuffled, value, position):
    found = jnp.argmax(shuffled == value)
    displaced = shuffled[position]
    return shuffled.at[found].set(displaced).at[position].set(value)


def draw_owners(key, part):
    base = jax.random.fold_in(key, 11)
    key_list = jax.random.split(base, N_ROWS + 4)
    shuffled = jnp.stack([jax.random.permutation(key_list[index], N_COLS) for index in range(N_ROWS)]).astype(jnp.int32)
    top_row = jax.random.randint(key_list[N_ROWS], (), 0, N_ROWS)
    low_row = (top_row + jax.random.randint(key_list[N_ROWS + 1], (), 1, N_ROWS)) % N_ROWS
    top_pos = jax.random.randint(key_list[N_ROWS + 2], (), 0, ROUNDS)
    low_pos = jax.random.randint(key_list[N_ROWS + 3], (), 0, ROUNDS)
    block_ids = jnp.arange(N_ROWS)[:, None]
    with_top = jax.vmap(lambda vector: place_value(vector, N_COLS - 1, top_pos))(shuffled)
    shuffled = jnp.where(block_ids == top_row, with_top, shuffled)
    with_low = jax.vmap(lambda vector: place_value(vector, 0, low_pos))(shuffled)
    shuffled = jnp.where(block_ids == low_row, with_low, shuffled)
    return shuffled[:, :ROUNDS].T.astype(jnp.int32)


def level_of(key, shape, cuts, low, high):
    loudness, own = 1.0, jax.random.fold_in(key, 6)
    for dim, shards_of in cuts:
        steps = jnp.exp(jax.random.uniform(jax.random.fold_in(own, dim), (shards_of,), jnp.float32, low / len(cuts), high / len(cuts)))
        loudness = loudness * jnp.repeat(steps, shape[dim] // shards_of).reshape([-1 if axis == dim else 1 for axis in range(len(shape))])
    return loudness


def centred(stream_key, dims, scale, bound, cuts=(), dtype=jnp.bfloat16):
    values = scale * jax.random.normal(stream_key, dims, jnp.float32)
    if cuts:
        values = values * level_of(stream_key, dims, cuts, -0.22, 0.18)
    return jnp.clip(values, -bound, bound).astype(dtype)


def setup_inputs(seed: int = 0) -> dict:
    key_of = jax.random.split(jax.random.key(seed), 4)
    return {
        "slab": centred(key_of[0], (SLAB_ROWS, SLAB_COLS), 1.0, 6.0, ((0, 4), (1, 8))),
        "transforms": centred(key_of[1], (N_COLS, POOL_ROWS, W), W ** -0.5, 0.25, ((0, 8), (1, 4))),
        "owners": draw_owners(jax.random.fold_in(key_of[3], 71), 0),
    }


def apply_pair(operands):
    transform, block_rows = operands
    product = lax.dot_general(transform, block_rows, (((0,), (0,)), ((), ())), preferred_element_type=jnp.float32)
    return product.astype(jnp.bfloat16)


def reference(slab, transforms, owners):
    span_rows = 2 * WINS * W
    total_windows = N_ROWS * WINS
    matrix = slab
    slab_width = slab.shape[1]
    for round_index in range(ROUNDS):
        pieces = []
        for row_block in range(N_ROWS):
            chosen = lax.dynamic_index_in_dim(transforms, owners[round_index, row_block].astype(jnp.int32), 0, keepdims=False)
            pieces.append(chosen[row_block * span_rows:(row_block + 1) * span_rows].reshape(2, WINS, W, W))
        stacked = jnp.stack(pieces)
        set_one = stacked[:, 0].reshape(total_windows, W, W)
        set_two = stacked[:, 1].reshape(total_windows, W, W)[:total_windows - 1]
        windows = matrix.reshape(total_windows, W, slab_width)
        matrix = lax.map(apply_pair, (set_one, windows)).reshape(matrix.shape)
        finish = STAGGER + (total_windows - 1) * W
        middle = matrix[STAGGER:finish].reshape(total_windows - 1, W, slab_width)
        middle = lax.map(apply_pair, (set_two, middle)).reshape(-1, slab_width)
        matrix = jnp.concatenate([matrix[:STAGGER], middle, matrix[finish:]], 0)
    return matrix
```

```python
import jax
import jax.numpy as jnp
from jax import lax
from jax.sharding import PartitionSpec as P


def shifted(value, axis, steps):
    count = lax.axis_size(axis)
    initial, last = (max(0, -steps), min(count, count - steps))
    return lax.ppermute(value, axis, [(source, source + steps) for source in range(initial, last)])


def flip(value, bits):
    count = lax.axis_size("cols")
    return lax.ppermute(value, "cols", [(d, d ^ (1 << bits[d & 1])) for d in range(count)])


class Spread:
    def __init__(self, slot, owners_here):
        count = lax.axis_size("cols")
        dims = count.bit_length() - 2
        self.me = lax.axis_index("cols")
        self.core = self.me & 1
        self.owners = owners_here
        self.cut = (1, dims)
        self.others = [(b, b - 1) for b in range(2, dims + 1)]
        self.slot = slot
        self.own = lax.dynamic_index_in_dim(slot, self.core, 1, keepdims=False)
        self.give = lax.dynamic_index_in_dim(slot, 1 - self.core, 1, keepdims=False)
        self.theirs = {}

    def bit(self, index, bits):
        return (index >> jnp.where(self.core == 0, bits[0], bits[1])) & 1

    def exchange(self, lo, hi):
        got = flip(self.give[lo:hi], (0, 0))
        for m in range(lo, hi):
            self.theirs[m] = got[m - lo]

    def begin(self, round_index, ms):
        owner = self.owners[round_index]
        own = jnp.stack([self.own[m] for m in ms])
        theirs = jnp.stack([self.theirs[m] for m in ms])
        data = jnp.where((owner & 1) == self.core, own, theirs)
        mine = self.bit(self.me, self.cut)
        out = lax.dynamic_index_in_dim(data, 1 - mine, 1, keepdims=False)
        hold = lax.dynamic_index_in_dim(data, mine, 1, keepdims=False)
        return owner, hold, flip(out, self.cut)

    def keep(self, state, bits):
        owner, hold, got = state
        same = self.bit(self.me, bits) == self.bit(owner, bits)
        return jnp.where(same, hold, got)

    def middle(self, state):
        bits = self.cut
        for other in self.others:
            hold = self.keep(state, bits)
            state = (state[0], hold, flip(hold, other))
            bits = other
        return state

    def last(self, state):
        hold = self.keep(state, self.others[-1])
        return hold, flip(hold, self.cut)

    def join(self, pair):
        hold, got = pair
        first = self.bit(self.me, self.cut) == 0
        half = jnp.stack([jnp.where(first, hold, got), jnp.where(first, got, hold)], 1)
        other = flip(half, (0, 0))
        core0 = self.core == 0
        whole = jnp.stack([jnp.where(core0, half, other), jnp.where(core0, other, half)], 1)
        n, _, _, rows, width = whole.shape
        return whole.reshape(n, 4 * rows, width)


def apply(q, x):
    product = lax.dot_general(q, x, (((0,), (0,)), ((), ())), preferred_element_type=jnp.float32)
    return product.astype(jnp.bfloat16)


def apply_many(q, x):
    product = jnp.einsum("nab,nac->nbc", q, x, preferred_element_type=jnp.float32)
    return product.astype(jnp.bfloat16)


def local(slab, transforms, owners):
    row_block = lax.axis_index("rows")
    last_block = lax.axis_size("rows") - 1
    window = transforms.shape[2]
    border = window // 2
    local_rows, local_cols = slab.shape
    wins = local_rows // window
    rounds = owners.shape[0]
    slot = transforms[0].reshape(2 * wins, 2, 2, window // 4, window)
    spread = Spread(slot, owners[:, row_block])
    spread.exchange(0, wins)
    spread.exchange(wins, 2 * wins)
    sets = [list(range(wins)), list(range(wins, 2 * wins))]

    streams = [(r, s) for r in range(rounds) for s in range(2)]
    states = {}
    for r, s in streams:
        states[r, s] = spread.begin(r, sets[s])
    for key in streams:
        states[key] = spread.middle(states[key])
    pairs = {key: spread.last(states[key]) for key in streams}

    matrix = slab
    for r in range(rounds):
        one = spread.join(pairs[r, 0])
        matrix = apply_many(one, matrix.reshape(wins, window, local_cols)).reshape(local_rows, local_cols)
        below = shifted(matrix[:border], "rows", -1)
        above = shifted(matrix[local_rows - border :], "rows", 1)
        two = spread.join(pairs[r, 1])
        prev = shifted(two[wins - 1, :, border:], "rows", 1)
        inner = apply_many(
            two[: wins - 1],
            matrix[border : local_rows - border].reshape(wins - 1, window, local_cols),
        ).reshape(local_rows - window, local_cols)
        low = apply(two[wins - 1, :, :border], jnp.concatenate([matrix[local_rows - border :], below], 0))
        low = jnp.where(row_block == last_block, matrix[local_rows - border :], low)
        top = apply(prev, jnp.concatenate([above, matrix[:border]], 0))
        top = jnp.where(row_block == 0, matrix[:border], top)
        matrix = jnp.concatenate([top, inner, low], 0)
    return matrix


def solution(mesh):
    return jax.shard_map(
        local,
        mesh=mesh,
        in_specs=(P("rows", "cols"), P("cols", "rows", None), P()),
        out_specs=P("rows", "cols"),
        check_vma=False,
    )
```

```python
import jax
import jax.numpy as jnp
from jax import lax
from jax.experimental import pallas as pl
from jax.experimental.pallas import tpu as pltpu
from jax.sharding import PartitionSpec as P


def shifted(value, axis, steps):
    count = lax.axis_size(axis)
    initial, last = (max(0, -steps), min(count, count - steps))
    return lax.ppermute(value, axis, [(source, source + steps) for source in range(initial, last)])


def flip(value, bits):
    count = lax.axis_size("cols")
    return lax.ppermute(value, "cols", [(d, d ^ (1 << bits[d & 1])) for d in range(count)])


def after(value, done):
    return lax.optimization_barrier((value, done))[0]


def place_kernel(cut, hold, got, other_hold, other_got, out, sems):
    me = lax.axis_index("cols")
    core = me & 1
    rows = hold.shape[1]
    bit0 = (me >> cut[0]) & 1
    bit1 = (me >> cut[1]) & 1
    mine = jnp.where(core == 0, bit0, bit1)
    other = jnp.where(core == 0, bit1, bit0)
    slots = (
        (hold, core * 2 + mine),
        (got, core * 2 + 1 - mine),
        (other_hold, (1 - core) * 2 + other),
        (other_got, (1 - core) * 2 + 1 - other),
    )
    copies = [
        pltpu.make_async_copy(
            piece, out.at[:, pl.ds(pl.multiple_of(at * rows, rows), rows), :], sems.at[k]
        )
        for k, (piece, at) in enumerate(slots)
    ]
    for copy in copies:
        copy.start()
    for copy in copies:
        copy.wait()


def place(cut, hold, got, other_hold, other_got):
    n, rows, width = hold.shape
    return pl.pallas_call(
        lambda *refs: place_kernel(cut, *refs),
        out_shape=jax.ShapeDtypeStruct((n, 4 * rows, width), hold.dtype),
        in_specs=[pl.BlockSpec(memory_space=pl.ANY)] * 4,
        out_specs=pl.BlockSpec(memory_space=pl.ANY),
        scratch_shapes=[pltpu.SemaphoreType.DMA((4,))],
        compiler_params=pltpu.CompilerParams(vmem_limit_bytes=1 << 20),
        cost_estimate=pl.CostEstimate(
            flops=0, bytes_accessed=2 * n * 4 * rows * width * 2, transcendentals=0
        ),
        name="place",
    )(hold, got, other_hold, other_got)


class Spread:
    def __init__(self, slot, owners_here):
        count = lax.axis_size("cols")
        dims = count.bit_length() - 2
        self.me = lax.axis_index("cols")
        self.core = self.me & 1
        self.owners = owners_here
        self.cut = (1, dims)
        self.others = [(b, b - 1) for b in range(2, dims + 1)]
        mine = self.bit(self.me, self.cut)
        other = (self.me >> jnp.where(self.core == 0, self.cut[1], self.cut[0])) & 1
        n, _, _, rows, width = slot.shape

        def take(half, piece):
            start = (0, half, piece, 0, 0)
            return lax.dynamic_slice(slot, start, (n, 1, 1, rows, width)).reshape(n, rows, width)

        self.own = take(self.core, 1 - mine), take(self.core, mine)
        self.give = take(1 - self.core, 1 - other), take(1 - self.core, other)
        self.theirs = {}

    def bit(self, index, bits):
        return (index >> jnp.where(self.core == 0, bits[0], bits[1])) & 1

    def exchange(self, lo, hi):
        got = [flip(give[lo:hi], (0, 0)) for give in self.give]
        for m in range(lo, hi):
            self.theirs[m] = [g[m - lo] for g in got]

    def begin(self, keys, first=None):
        data = []
        for part in range(2):
            data.append(
                jnp.stack(
                    [
                        jnp.where(
                            (self.owners[r] & 1) == self.core, self.own[part][m], self.theirs[m][part]
                        )
                        for r, m in keys
                    ]
                )
            )
        out = data[0] if first is None else after(data[0], first)
        return keys[0][0], data[1], flip(out, self.cut)

    def keep(self, state, bits):
        round_index, hold, got = state
        same = self.bit(self.me, bits) == self.bit(self.owners[round_index], bits)
        return jnp.where(same, hold, got)

    def middle(self, state):
        bits = self.cut
        for other in self.others:
            hold = self.keep(state, bits)
            state = (state[0], hold, flip(hold, other))
            bits = other
        return state

    def last(self, state):
        hold = self.keep(state, self.others[-1])
        return hold, flip(hold, self.cut)

    def join(self, hold, got):
        return place(self.cut, hold, got, flip(hold, (0, 0)), flip(got, (0, 0)))

    def join_above(self, hold, got):
        both = shifted(jnp.stack([hold, got]), "rows", 1)
        other = flip(both, (0, 0))
        return place(self.cut, both[:1], both[1:], other[:1], other[1:])[0]


def apply(q, x):
    product = lax.dot_general(q, x, (((0,), (0,)), ((), ())), preferred_element_type=jnp.float32)
    return product.astype(jnp.bfloat16)


def apply_many(q, x):
    product = jnp.einsum("nab,nac->nbc", q, x, preferred_element_type=jnp.float32)
    return product.astype(jnp.bfloat16)


def local(slab, transforms, owners):
    row_block = lax.axis_index("rows")
    last_block = lax.axis_size("rows") - 1
    window = transforms.shape[2]
    border = window // 2
    local_rows, local_cols = slab.shape
    wins = local_rows // window
    rounds = owners.shape[0]
    slot = transforms[0].reshape(2 * wins, 2, 2, window // 4, window)
    spread = Spread(slot, owners[:, row_block])
    spread.exchange(0, wins)
    spread.exchange(wins, 2 * wins)

    edge = [0, wins - 1, 2 * wins - 1]
    inside = [m for m in range(2 * wins) if m not in edge]
    plans = []
    for r in range(rounds):
        if r < rounds - 1:
            plans.append([(r, m) for m in range(wins)])
            plans.append([(r, m) for m in range(wins, 2 * wins)])
        else:
            plans.append([(r, m) for m in edge])
            plans.append([(r, m) for m in inside])
    states, pairs = {}, {}
    for k in range(0, len(plans), 2):
        if k == 0:
            states[k] = spread.begin(plans[k])
            states[k + 1] = spread.begin(plans[k + 1])
        else:
            states[k] = spread.begin(plans[k], states[k - 1][2])
            states[k + 1] = spread.begin(plans[k + 1], pairs[k - 2][1])
        pairs[k] = spread.last(spread.middle(states[k]))
        pairs[k + 1] = spread.last(spread.middle(states[k + 1]))

    matrix = slab
    for r in range(rounds):
        head, tail = pairs[2 * r], pairs[2 * r + 1]
        if r < rounds - 1:
            one = spread.join(*head)
            matrix = apply_many(one, matrix.reshape(wins, window, local_cols)).reshape(local_rows, local_cols)
            begin, end = matrix[:border], matrix[local_rows - border :]
            below = shifted(begin, "rows", -1)
            above = shifted(end, "rows", 1)
            prev = spread.join_above(tail[0][-1, :, border:], tail[1][-1, :, border:])
            two = spread.join(*tail)
            cross = two[wins - 1]
            two = two[: wins - 1]
            centre = matrix[border : local_rows - border]
        else:
            edges = spread.join(*head)
            cross = edges[2]
            head_rows = apply(edges[0], matrix[:window])
            tail_rows = apply(edges[1], matrix[local_rows - window :])
            begin, end = head_rows[:border], tail_rows[border:]
            below = shifted(begin, "rows", -1)
            above = shifted(end, "rows", 1)
            prev = spread.join_above(head[0][-1, :, border:], head[1][-1, :, border:])
            rest = spread.join(*tail)
            mid = apply_many(
                rest[: wins - 2],
                matrix[window : local_rows - window].reshape(wins - 2, window, local_cols),
            ).reshape(local_rows - 2 * window, local_cols)
            two = rest[wins - 2 :]
            centre = jnp.concatenate([head_rows[border:], mid, tail_rows[:border]], 0)
        inner = apply_many(two, centre.reshape(wins - 1, window, local_cols)).reshape(
            local_rows - window, local_cols
        )
        low = apply(cross[:, :border], jnp.concatenate([end, below], 0))
        low = jnp.where(row_block == last_block, end, low)
        top = apply(prev, jnp.concatenate([above, begin], 0))
        top = jnp.where(row_block == 0, begin, top)
        matrix = jnp.concatenate([top, inner, low], 0)
    return matrix


def solution(mesh):
    return jax.shard_map(
        local,
        mesh=mesh,
        in_specs=(P("rows", "cols"), P("cols", "rows", None), P()),
        out_specs=P("rows", "cols"),
        check_vma=False,
    )
```

```python
import jax
import jax.numpy as jnp
from jax import lax
from jax.experimental import pallas as pl
from jax.experimental.pallas import tpu as pltpu
from jax.sharding import PartitionSpec as P


def shifted(value, axis, steps):
    count = lax.axis_size(axis)
    initial, last = (max(0, -steps), min(count, count - steps))
    return lax.ppermute(value, axis, [(source, source + steps) for source in range(initial, last)])


def flip(value, bits):
    count = lax.axis_size("cols")
    return lax.ppermute(value, "cols", [(d, d ^ (1 << bits[d & 1])) for d in range(count)])


def copy_all(copies):
    for copy in copies:
        copy.start()
    for copy in copies:
        copy.wait()


def small(flops=0, bytes_accessed=0):
    return dict(
        compiler_params=pltpu.CompilerParams(vmem_limit_bytes=1 << 20),
        cost_estimate=pl.CostEstimate(
            flops=flops, bytes_accessed=bytes_accessed, transcendentals=0
        ),
    )


ANY = pl.BlockSpec(memory_space=pl.ANY)


def after(value, done):
    def kernel(source, _, out, sem):
        copy_all([pltpu.make_async_copy(source, out, sem)])

    return pl.pallas_call(
        kernel,
        out_shape=jax.ShapeDtypeStruct(value.shape, value.dtype),
        in_specs=[ANY, ANY],
        out_specs=ANY,
        scratch_shapes=[pltpu.SemaphoreType.DMA],
        name="after",
        **small(bytes_accessed=4 * value.size),
    )(value, done)


def runs(ms):
    found = []
    for at, m in enumerate(ms):
        if found and found[-1][0] + found[-1][2] == m:
            found[-1][2] += 1
        else:
            found.append([m, at, 1])
    return found


def cut_slot(cut, groups, slot):
    _, _, _, rows, width = slot.shape
    pieces = [(group, k) for group in groups for k in range(4)]
    shapes = [jax.ShapeDtypeStruct((len(group), rows, width), slot.dtype) for group, _ in pieces]
    count = sum(len(runs(group)) for group, _ in pieces)

    def kernel(source, *refs):
        outs, sems = refs[:-1], refs[-1]
        me = lax.axis_index("cols")
        core = me & 1
        bit0 = (me >> cut[0]) & 1
        bit1 = (me >> cut[1]) & 1
        mine = jnp.where(core == 0, bit0, bit1)
        other = jnp.where(core == 0, bit1, bit0)
        places = ((1 - core, 1 - other), (core, 1 - mine), (1 - core, other), (core, mine))
        copies = []
        for (group, k), out in zip(pieces, outs):
            half, piece = places[k]
            for first, at, n in runs(group):
                copies.append(
                    pltpu.make_async_copy(
                        source.at[pl.ds(first, n), half, piece],
                        out.at[pl.ds(at, n)],
                        sems.at[len(copies)],
                    )
                )
        copy_all(copies)

    outs = pl.pallas_call(
        kernel,
        out_shape=shapes,
        in_specs=[ANY],
        out_specs=[ANY] * len(shapes),
        scratch_shapes=[pltpu.SemaphoreType.DMA((count,))],
        name="cut_slot",
        **small(bytes_accessed=4 * slot.size),
    )(slot)
    return [outs[4 * g : 4 * g + 4] for g in range(len(groups))]


def place_kernel(cut, hold, got, other_hold, other_got, out, sems):
    me = lax.axis_index("cols")
    core = me & 1
    rows = hold.shape[1]
    bit0 = (me >> cut[0]) & 1
    bit1 = (me >> cut[1]) & 1
    mine = jnp.where(core == 0, bit0, bit1)
    other = jnp.where(core == 0, bit1, bit0)
    slots = (
        (hold, core * 2 + mine),
        (got, core * 2 + 1 - mine),
        (other_hold, (1 - core) * 2 + other),
        (other_got, (1 - core) * 2 + 1 - other),
    )
    copies = [
        pltpu.make_async_copy(
            piece, out.at[:, pl.ds(pl.multiple_of(at * rows, rows), rows), :], sems.at[k]
        )
        for k, (piece, at) in enumerate(slots)
    ]
    copy_all(copies)


def place(cut, hold, got, other_hold, other_got):
    n, rows, width = hold.shape
    return pl.pallas_call(
        lambda *refs: place_kernel(cut, *refs),
        out_shape=jax.ShapeDtypeStruct((n, 4 * rows, width), hold.dtype),
        in_specs=[ANY] * 4,
        out_specs=ANY,
        scratch_shapes=[pltpu.SemaphoreType.DMA((4,))],
        name="place",
        **small(bytes_accessed=2 * n * 4 * rows * width * 2),
    )(hold, got, other_hold, other_got)


class Spread:
    def __init__(self, slot, owners_here, groups):
        count = lax.axis_size("cols")
        dims = count.bit_length() - 2
        self.me = lax.axis_index("cols")
        self.core = self.me & 1
        self.owners = owners_here
        self.cut = (1, dims)
        self.others = [(b, b - 1) for b in range(2, dims + 1)]
        self.own, self.theirs = [], []
        for give_out, own_out, give_hold, own_hold in cut_slot(self.cut, groups, slot):
            self.own.append((own_out, own_hold))
            self.theirs.append((flip(give_out, (0, 0)), flip(give_hold, (0, 0))))

    def bit(self, index, bits):
        return (index >> jnp.where(self.core == 0, bits[0], bits[1])) & 1

    def begin(self, round_index, group, first=None):
        here = (self.owners[round_index] & 1) == self.core
        out, hold = [
            jnp.where(here, own, theirs)
            for own, theirs in zip(self.own[group], self.theirs[group])
        ]
        if first is not None:
            out = after(out, first)
        return round_index, hold, flip(out, self.cut)

    def keep(self, state, bits):
        round_index, hold, got = state
        same = self.bit(self.me, bits) == self.bit(self.owners[round_index], bits)
        return jnp.where(same, hold, got)

    def middle(self, state):
        bits = self.cut
        for other in self.others:
            hold = self.keep(state, bits)
            state = (state[0], hold, flip(hold, other))
            bits = other
        return state

    def last(self, state):
        hold = self.keep(state, self.others[-1])
        return hold, flip(hold, self.cut)

    def join(self, hold, got):
        return place(self.cut, hold, got, flip(hold, (0, 0)), flip(got, (0, 0)))

    def join_above(self, hold, got):
        both = shifted(jnp.stack([hold, got]), "rows", 1)
        other = flip(both, (0, 0))
        return place(self.cut, both[:1], both[1:], other[:1], other[1:])[0]


def apply(q, x):
    product = lax.dot_general(q, x, (((0,), (0,)), ((), ())), preferred_element_type=jnp.float32)
    return product.astype(jnp.bfloat16)


def apply_many(q, x):
    product = jnp.einsum("nab,nac->nbc", q, x, preferred_element_type=jnp.float32)
    return product.astype(jnp.bfloat16)


def local(slab, transforms, owners):
    row_block = lax.axis_index("rows")
    last_block = lax.axis_size("rows") - 1
    window = transforms.shape[2]
    border = window // 2
    local_rows, local_cols = slab.shape
    wins = local_rows // window
    rounds = owners.shape[0]
    slot = transforms[0].reshape(2 * wins, 2, 2, window // 4, window)
    edge = [0, wins - 1, 2 * wins - 1]
    inside = [m for m in range(2 * wins) if m not in edge]
    spread = Spread(slot, owners[:, row_block], (edge, inside))

    states, pairs = {}, {}
    for r in range(rounds):
        for g in range(2):
            first = None if r == 0 else (states[r - 1, 1][2] if g == 0 else pairs[r - 1, 0][1])
            states[r, g] = spread.middle(spread.begin(r, g, first))
        for g in range(2):
            pairs[r, g] = spread.last(states[r, g])

    matrix = slab
    for r in range(rounds):
        head, tail = pairs[r, 0], pairs[r, 1]
        edges = spread.join(*head)
        head_rows = apply(edges[0], matrix[:window])
        tail_rows = apply(edges[1], matrix[local_rows - window :])
        begin, end = head_rows[:border], tail_rows[border:]
        below = shifted(begin, "rows", -1)
        above = shifted(end, "rows", 1)
        prev = spread.join_above(head[0][-1, :, border:], head[1][-1, :, border:])
        rest = spread.join(*tail)
        mid = apply_many(
            rest[: wins - 2],
            matrix[window : local_rows - window].reshape(wins - 2, window, local_cols),
        ).reshape(local_rows - 2 * window, local_cols)
        centre = jnp.concatenate([head_rows[border:], mid, tail_rows[:border]], 0)
        inner = apply_many(rest[wins - 2 :], centre.reshape(wins - 1, window, local_cols)).reshape(
            local_rows - window, local_cols
        )
        low = apply(edges[2, :, :border], jnp.concatenate([end, below], 0))
        low = jnp.where(row_block == last_block, end, low)
        top = apply(prev, jnp.concatenate([above, begin], 0))
        top = jnp.where(row_block == 0, begin, top)
        matrix = jnp.concatenate([top, inner, low], 0)
    return matrix


def solution(mesh):
    return jax.shard_map(
        local,
        mesh=mesh,
        in_specs=(P("rows", "cols"), P("cols", "rows", None), P()),
        out_specs=P("rows", "cols"),
        check_vma=False,
    )
```

```python
import jax
import jax.numpy as jnp
from jax import lax
from jax.experimental import pallas as pl
from jax.experimental.pallas import tpu as pltpu
from jax.sharding import PartitionSpec as P


def shifted(value, axis, steps):
    count = lax.axis_size(axis)
    initial, last = (max(0, -steps), min(count, count - steps))
    return lax.ppermute(value, axis, [(source, source + steps) for source in range(initial, last)])


def flip(value, bits):
    count = lax.axis_size("cols")
    return lax.ppermute(value, "cols", [(d, d ^ (1 << bits[d & 1])) for d in range(count)])


def copy_all(copies):
    for copy in copies:
        copy.start()
    for copy in copies:
        copy.wait()


def small(flops=0, bytes_accessed=0, limit=1 << 20):
    return dict(
        compiler_params=pltpu.CompilerParams(vmem_limit_bytes=limit),
        cost_estimate=pl.CostEstimate(
            flops=flops, bytes_accessed=bytes_accessed, transcendentals=0
        ),
    )


ANY = pl.BlockSpec(memory_space=pl.ANY)


def after(value, done):
    def kernel(source, _, out, sem):
        copy_all([pltpu.make_async_copy(source, out, sem)])

    return pl.pallas_call(
        kernel,
        out_shape=jax.ShapeDtypeStruct(value.shape, value.dtype),
        in_specs=[ANY, ANY],
        out_specs=ANY,
        scratch_shapes=[pltpu.SemaphoreType.DMA],
        name="after",
        **small(bytes_accessed=4 * value.size),
    )(value, done)


def runs(ms):
    found = []
    for at, m in enumerate(ms):
        if found and found[-1][0] + found[-1][2] == m:
            found[-1][2] += 1
        else:
            found.append([m, at, 1])
    return found


def cut_slot(cut, order, kinds, slot):
    _, _, _, rows, width = slot.shape
    shapes = [jax.ShapeDtypeStruct((len(order), rows, width), slot.dtype) for _ in kinds]
    spans = runs(order)

    def kernel(source, *refs):
        outs, sems = refs[:-1], refs[-1]
        me = lax.axis_index("cols")
        core = me & 1
        bit0 = (me >> cut[0]) & 1
        bit1 = (me >> cut[1]) & 1
        mine = jnp.where(core == 0, bit0, bit1)
        other = jnp.where(core == 0, bit1, bit0)
        copies = []
        for (own, hold), out in zip(kinds, outs):
            half = core if own else 1 - core
            piece = mine if own else other
            piece = piece if hold else 1 - piece
            for first, at, n in spans:
                copies.append(
                    pltpu.make_async_copy(
                        source.at[pl.ds(first, n), half, piece],
                        out.at[pl.ds(at, n)],
                        sems.at[len(copies)],
                    )
                )
        copy_all(copies)

    return pl.pallas_call(
        kernel,
        out_shape=shapes,
        in_specs=[pl.BlockSpec(memory_space=pltpu.HBM)],
        out_specs=[ANY] * len(shapes),
        scratch_shapes=[pltpu.SemaphoreType.DMA((len(spans) * len(kinds),))],
        name="cut_slot",
        **small(bytes_accessed=len(kinds) * slot.size, limit=(60 if len(kinds) == 1 else 1) << 20),
    )(slot)


def place_kernel(cut, hold, got, other_hold, other_got, out, sems):
    me = lax.axis_index("cols")
    core = me & 1
    rows = hold.shape[1]
    bit0 = (me >> cut[0]) & 1
    bit1 = (me >> cut[1]) & 1
    mine = jnp.where(core == 0, bit0, bit1)
    other = jnp.where(core == 0, bit1, bit0)
    slots = (
        (hold, core * 2 + mine),
        (got, core * 2 + 1 - mine),
        (other_hold, (1 - core) * 2 + other),
        (other_got, (1 - core) * 2 + 1 - other),
    )
    copies = [
        pltpu.make_async_copy(
            piece, out.at[:, pl.ds(pl.multiple_of(at * rows, rows), rows), :], sems.at[k]
        )
        for k, (piece, at) in enumerate(slots)
    ]
    copy_all(copies)


def place(cut, hold, got, other_hold, other_got):
    n, rows, width = hold.shape
    return pl.pallas_call(
        lambda *refs: place_kernel(cut, *refs),
        out_shape=jax.ShapeDtypeStruct((n, 4 * rows, width), hold.dtype),
        in_specs=[ANY] * 4,
        out_specs=ANY,
        scratch_shapes=[pltpu.SemaphoreType.DMA((4,))],
        name="place",
        **small(bytes_accessed=2 * n * 4 * rows * width * 2),
    )(hold, got, other_hold, other_got)


class Spread:
    def __init__(self, slot, owners_here, groups):
        count = lax.axis_size("cols")
        dims = count.bit_length() - 2
        self.me = lax.axis_index("cols")
        self.core = self.me & 1
        self.owners = owners_here
        self.cut = (1, dims)
        self.others = [(b, b - 1) for b in range(2, dims + 1)]
        order = [m for group in groups for m in group]
        self.spans, at = [], 0
        for group in groups:
            self.spans.append(slice(at, at + len(group)))
            at += len(group)
        (give_out,) = cut_slot(self.cut, order, [(False, False)], slot)
        own_out, give_hold, own_hold = cut_slot(
            self.cut, order, [(True, False), (False, True), (True, True)], slot
        )
        self.own = own_out, own_hold
        self.theirs = flip(give_out, (0, 0)), flip(give_hold, (0, 0))

    def bit(self, index, bits):
        return (index >> jnp.where(self.core == 0, bits[0], bits[1])) & 1

    def begin(self, round_index, group, first=None):
        here = (self.owners[round_index] & 1) == self.core
        out, hold = [
            jnp.where(here, own[self.spans[group]], theirs[self.spans[group]])
            for own, theirs in zip(self.own, self.theirs)
        ]
        if first is not None:
            out = after(out, first)
        return round_index, hold, flip(out, self.cut)

    def keep(self, state, bits):
        round_index, hold, got = state
        same = self.bit(self.me, bits) == self.bit(self.owners[round_index], bits)
        return jnp.where(same, hold, got)

    def middle(self, state):
        bits = self.cut
        for other in self.others:
            hold = self.keep(state, bits)
            state = (state[0], hold, flip(hold, other))
            bits = other
        return state

    def last(self, state):
        hold = self.keep(state, self.others[-1])
        return hold, flip(hold, self.cut)

    def join(self, hold, got):
        return place(self.cut, hold, got, flip(hold, (0, 0)), flip(got, (0, 0)))

    def join_above(self, hold, got):
        both = shifted(jnp.stack([hold, got]), "rows", 1)
        other = flip(both, (0, 0))
        return place(self.cut, both[:1], both[1:], other[:1], other[1:])[0]


def apply(q, x):
    product = lax.dot_general(q, x, (((0,), (0,)), ((), ())), preferred_element_type=jnp.float32)
    return product.astype(jnp.bfloat16)


def apply_many(q, x):
    product = jnp.einsum("nab,nac->nbc", q, x, preferred_element_type=jnp.float32)
    return product.astype(jnp.bfloat16)


def local(slab, transforms, owners):
    row_block = lax.axis_index("rows")
    last_block = lax.axis_size("rows") - 1
    window = transforms.shape[2]
    border = window // 2
    local_rows, local_cols = slab.shape
    wins = local_rows // window
    rounds = owners.shape[0]
    slot = transforms[0].reshape(2 * wins, 2, 2, window // 4, window)
    edge = [0, wins - 1, 2 * wins - 1]
    inside = [m for m in range(2 * wins) if m not in edge]
    spread = Spread(slot, owners[:, row_block], (edge, inside))

    states, pairs = {}, {}
    for r in range(rounds):
        for g in range(2):
            first = None if r == 0 else pairs[r - 1, g][1]
            states[r, g] = spread.middle(spread.begin(r, g, first))
        for g in range(2):
            pairs[r, g] = spread.last(states[r, g])

    matrix = slab
    for r in range(rounds):
        head, tail = pairs[r, 0], pairs[r, 1]
        edges = spread.join(*head)
        head_rows = apply(edges[0], matrix[:window])
        tail_rows = apply(edges[1], matrix[local_rows - window :])
        begin, end = head_rows[:border], tail_rows[border:]
        below = shifted(begin, "rows", -1)
        above = shifted(end, "rows", 1)
        prev = spread.join_above(head[0][-1, :, border:], head[1][-1, :, border:])
        rest = spread.join(*tail)
        mid = apply_many(
            rest[: wins - 2],
            matrix[window : local_rows - window].reshape(wins - 2, window, local_cols),
        ).reshape(local_rows - 2 * window, local_cols)
        centre = jnp.concatenate([head_rows[border:], mid, tail_rows[:border]], 0)
        inner = apply_many(rest[wins - 2 :], centre.reshape(wins - 1, window, local_cols)).reshape(
            local_rows - window, local_cols
        )
        low = apply(edges[2, :, :border], jnp.concatenate([end, below], 0))
        low = jnp.where(row_block == last_block, end, low)
        top = apply(prev, jnp.concatenate([above, begin], 0))
        top = jnp.where(row_block == 0, begin, top)
        matrix = jnp.concatenate([top, inner, low], 0)
    return matrix


def solution(mesh):
    return jax.shard_map(
        local,
        mesh=mesh,
        in_specs=(P("rows", "cols"), P("cols", "rows", None), P()),
        out_specs=P("rows", "cols"),
        check_vma=False,
    )
```

```python
import jax
import jax.numpy as jnp
from jax import lax
from jax.experimental import pallas as pl
from jax.experimental.pallas import tpu as pltpu
from jax.sharding import PartitionSpec as P


def shifted(value, axis, steps):
    count = lax.axis_size(axis)
    initial, last = (max(0, -steps), min(count, count - steps))
    return lax.ppermute(value, axis, [(source, source + steps) for source in range(initial, last)])


def copy_all(copies):
    for copy in copies:
        copy.start()
    for copy in copies:
        copy.wait()


def small(flops=0, bytes_accessed=0):
    return dict(
        compiler_params=pltpu.CompilerParams(vmem_limit_bytes=1 << 20),
        cost_estimate=pl.CostEstimate(
            flops=flops, bytes_accessed=bytes_accessed, transcendentals=0
        ),
    )


ANY = pl.BlockSpec(memory_space=pl.ANY)


def runs(ms):
    found = []
    for at, m in enumerate(ms):
        if found and found[-1][0] + found[-1][2] == m:
            found[-1][2] += 1
        else:
            found.append([m, at, 1])
    return found


def take_half(order, own, slot):
    _, _, rows, width = slot.shape
    spans = runs(order)

    def kernel(source, out, sems):
        core = lax.axis_index("cols") & 1
        half = core if own else 1 - core
        copy_all(
            [
                pltpu.make_async_copy(source.at[pl.ds(first, n), half], out.at[pl.ds(at, n)], sems.at[k])
                for k, (first, at, n) in enumerate(spans)
            ]
        )

    return pl.pallas_call(
        kernel,
        out_shape=jax.ShapeDtypeStruct((len(order), rows, width), slot.dtype),
        in_specs=[ANY],
        out_specs=ANY,
        scratch_shapes=[pltpu.SemaphoreType.DMA((len(spans),))],
        name="take_half",
        **small(bytes_accessed=2 * slot.size),
    )(slot)


def place(half, other):
    n, rows, width = half.shape

    def kernel(mine, theirs, out, sems):
        core = lax.axis_index("cols") & 1
        copy_all(
            [
                pltpu.make_async_copy(
                    piece, out.at[:, pl.ds(pl.multiple_of(at * rows, rows), rows), :], sems.at[k]
                )
                for k, (piece, at) in enumerate(((mine, core), (theirs, 1 - core)))
            ]
        )

    return pl.pallas_call(
        kernel,
        out_shape=jax.ShapeDtypeStruct((n, 2 * rows, width), half.dtype),
        in_specs=[ANY] * 2,
        out_specs=ANY,
        scratch_shapes=[pltpu.SemaphoreType.DMA((2,))],
        name="place",
        **small(bytes_accessed=8 * n * rows * width),
    )(half, other)


def swap_cores(value):
    count = lax.axis_size("cols")
    return lax.ppermute(value, "cols", [(d, d ^ 1) for d in range(count)])


class Spread:
    def __init__(self, slot, owners_here, groups):
        count = lax.axis_size("cols")
        self.me = lax.axis_index("cols")
        self.core = self.me & 1
        self.owners = owners_here
        order = [m for group in groups for m in group]
        self.spans, at = [], 0
        for group in groups:
            self.spans.append(slice(at, at + len(group)))
            at += len(group)
        self.theirs = swap_cores(take_half(order, False, slot))
        self.own = take_half(order, True, slot)
        chips = [k ^ (k >> 1) for k in range(count // 2)]
        self.rings = [[2 * chip + core for chip in chips] for core in range(2)]
        self.sums = 0

    def sum(self, round_index, group):
        owner = self.owners[round_index]
        span = self.spans[group]
        value = jnp.where((owner & 1) == self.core, self.own[span], self.theirs[span])
        value = jnp.where((owner >> 1) == (self.me >> 1), value, jnp.zeros_like(value))
        turn = self.sums % len(self.rings[0])
        self.sums += 1
        return lax.psum(value, "cols", axis_index_groups=[ring[turn:] + ring[:turn] for ring in self.rings])

    def join(self, half):
        return place(half, swap_cores(half))

    def join_above(self, half):
        both = shifted(half, "rows", 1)
        return place(both[None], swap_cores(both)[None])[0]


def apply(q, x):
    product = lax.dot_general(q, x, (((0,), (0,)), ((), ())), preferred_element_type=jnp.float32)
    return product.astype(jnp.bfloat16)


def apply_many(q, x):
    product = jnp.einsum("nab,nac->nbc", q, x, preferred_element_type=jnp.float32)
    return product.astype(jnp.bfloat16)


def local(slab, transforms, owners):
    row_block = lax.axis_index("rows")
    last_block = lax.axis_size("rows") - 1
    window = transforms.shape[2]
    border = window // 2
    local_rows, local_cols = slab.shape
    wins = local_rows // window
    rounds = owners.shape[0]
    slot = transforms[0].reshape(2 * wins, 2, border, window)
    edge = [0, wins - 1, 2 * wins - 1]
    inside = [m for m in range(2 * wins) if m not in edge]
    spread = Spread(slot, owners[:, row_block], (edge, inside))

    halves = [[spread.sum(r, g) for g in range(2)] for r in range(rounds)]

    matrix = slab
    for r in range(rounds):
        head, tail = halves[r]
        edges = spread.join(head)
        head_rows = apply(edges[0], matrix[:window])
        tail_rows = apply(edges[1], matrix[local_rows - window :])
        begin, end = head_rows[:border], tail_rows[border:]
        below = shifted(begin, "rows", -1)
        above = shifted(end, "rows", 1)
        prev = spread.join_above(head[-1, :, border:])
        rest = spread.join(tail)
        mid = apply_many(
            rest[: wins - 2],
            matrix[window : local_rows - window].reshape(wins - 2, window, local_cols),
        ).reshape(local_rows - 2 * window, local_cols)
        centre = jnp.concatenate([head_rows[border:], mid, tail_rows[:border]], 0)
        inner = apply_many(rest[wins - 2 :], centre.reshape(wins - 1, window, local_cols)).reshape(
            local_rows - window, local_cols
        )
        low = apply(edges[2, :, :border], jnp.concatenate([end, below], 0))
        low = jnp.where(row_block == last_block, end, low)
        top = apply(prev, jnp.concatenate([above, begin], 0))
        top = jnp.where(row_block == 0, begin, top)
        matrix = jnp.concatenate([top, inner, low], 0)
    return matrix


def solution(mesh):
    return jax.shard_map(
        local,
        mesh=mesh,
        in_specs=(P("rows", "cols"), P("cols", "rows", None), P()),
        out_specs=P("rows", "cols"),
        check_vma=False,
    )
```

```python
import jax
import jax.numpy as jnp
from jax import lax
from jax.experimental import pallas as pl
from jax.experimental.pallas import tpu as pltpu
from jax.sharding import PartitionSpec as P


def shifted(value, axis, steps):
    count = lax.axis_size(axis)
    initial, last = (max(0, -steps), min(count, count - steps))
    return lax.ppermute(value, axis, [(source, source + steps) for source in range(initial, last)])


def swap_rows(up, down):
    count = lax.axis_size("rows")
    even = (lax.axis_index("rows") & 1) == 0

    def swap(value, start):
        pairs = [(low, low + 1) for low in range(start, count - 1, 2)]
        return lax.ppermute(value, "rows", pairs + [(b, a) for a, b in pairs])

    first = swap(jnp.where(even, down, up), 0)
    second = swap(jnp.where(even, up, down), 1)
    return jnp.where(even, second, first), jnp.where(even, first, second)


def flip(value, bits):
    count = lax.axis_size("cols")
    return lax.ppermute(value, "cols", [(d, d ^ (1 << bits[d & 1])) for d in range(count)])


def copy_all(copies):
    for copy in copies:
        copy.start()
    for copy in copies:
        copy.wait()


def small(flops=0, bytes_accessed=0, limit=1 << 20):
    return dict(
        compiler_params=pltpu.CompilerParams(vmem_limit_bytes=limit),
        cost_estimate=pl.CostEstimate(
            flops=flops, bytes_accessed=bytes_accessed, transcendentals=0
        ),
    )


ANY = pl.BlockSpec(memory_space=pl.ANY)


def after(value, done):
    def kernel(source, _, out, sem):
        copy_all([pltpu.make_async_copy(source, out, sem)])

    return pl.pallas_call(
        kernel,
        out_shape=jax.ShapeDtypeStruct(value.shape, value.dtype),
        in_specs=[ANY, ANY],
        out_specs=ANY,
        scratch_shapes=[pltpu.SemaphoreType.DMA],
        name="after",
        **small(bytes_accessed=4 * value.size),
    )(value, done)


def runs(ms):
    found = []
    for at, m in enumerate(ms):
        if found and found[-1][0] + found[-1][2] == m:
            found[-1][2] += 1
        else:
            found.append([m, at, 1])
    return found


def cut_slot(cut, order, kinds, slot):
    _, _, _, rows, width = slot.shape
    shapes = [jax.ShapeDtypeStruct((len(order), rows, width), slot.dtype) for _ in kinds]
    spans = runs(order)

    def kernel(source, *refs):
        outs, sems = refs[:-1], refs[-1]
        me = lax.axis_index("cols")
        core = me & 1
        bit0 = (me >> cut[0]) & 1
        bit1 = (me >> cut[1]) & 1
        mine = jnp.where(core == 0, bit0, bit1)
        other = jnp.where(core == 0, bit1, bit0)
        copies = []
        for (own, hold), out in zip(kinds, outs):
            half = core if own else 1 - core
            piece = mine if own else other
            piece = piece if hold else 1 - piece
            for first, at, n in spans:
                copies.append(
                    pltpu.make_async_copy(
                        source.at[pl.ds(first, n), half, piece],
                        out.at[pl.ds(at, n)],
                        sems.at[len(copies)],
                    )
                )
        copy_all(copies)

    return pl.pallas_call(
        kernel,
        out_shape=shapes,
        in_specs=[pl.BlockSpec(memory_space=pltpu.HBM)],
        out_specs=[ANY] * len(shapes),
        scratch_shapes=[pltpu.SemaphoreType.DMA((len(spans) * len(kinds),))],
        name="cut_slot",
        **small(bytes_accessed=len(kinds) * slot.size, limit=(48 if len(kinds) == 1 else 1) << 20),
    )(slot)


def place_kernel(cut, hold, got, other_hold, other_got, out, sems):
    me = lax.axis_index("cols")
    core = me & 1
    rows = hold.shape[1]
    bit0 = (me >> cut[0]) & 1
    bit1 = (me >> cut[1]) & 1
    mine = jnp.where(core == 0, bit0, bit1)
    other = jnp.where(core == 0, bit1, bit0)
    slots = (
        (hold, core * 2 + mine),
        (got, core * 2 + 1 - mine),
        (other_hold, (1 - core) * 2 + other),
        (other_got, (1 - core) * 2 + 1 - other),
    )
    copies = [
        pltpu.make_async_copy(
            piece, out.at[:, pl.ds(pl.multiple_of(at * rows, rows), rows), :], sems.at[k]
        )
        for k, (piece, at) in enumerate(slots)
    ]
    copy_all(copies)


def place(cut, hold, got, other_hold, other_got):
    n, rows, width = hold.shape
    return pl.pallas_call(
        lambda *refs: place_kernel(cut, *refs),
        out_shape=jax.ShapeDtypeStruct((n, 4 * rows, width), hold.dtype),
        in_specs=[ANY] * 4,
        out_specs=ANY,
        scratch_shapes=[pltpu.SemaphoreType.DMA((4,))],
        name="place",
        **small(bytes_accessed=2 * n * 4 * rows * width * 2),
    )(hold, got, other_hold, other_got)


class Spread:
    def __init__(self, slot, owners_here, groups):
        count = lax.axis_size("cols")
        dims = count.bit_length() - 2
        self.me = lax.axis_index("cols")
        self.core = self.me & 1
        self.owners = owners_here
        self.cut = (1, dims)
        self.others = [(b, b - 1) for b in range(2, dims + 1)]
        order = [m for group in groups for m in group]
        self.spans, at = [], 0
        for group in groups:
            self.spans.append(slice(at, at + len(group)))
            at += len(group)
        (give_out,) = cut_slot(self.cut, order, [(False, False)], slot)
        own_out, give_hold, own_hold = cut_slot(
            self.cut, order, [(True, False), (False, True), (True, True)], slot
        )
        self.own = own_out, own_hold
        self.theirs = flip(give_out, (0, 0)), flip(give_hold, (0, 0))

    def bit(self, index, bits):
        return (index >> jnp.where(self.core == 0, bits[0], bits[1])) & 1

    def begin(self, round_index, group, first=None):
        here = (self.owners[round_index] & 1) == self.core
        out, hold = [
            jnp.where(here, own[self.spans[group]], theirs[self.spans[group]])
            for own, theirs in zip(self.own, self.theirs)
        ]
        if first is not None:
            out = after(out, first)
        return round_index, hold, flip(out, self.cut)

    def keep(self, state, bits):
        round_index, hold, got = state
        same = self.bit(self.me, bits) == self.bit(self.owners[round_index], bits)
        return jnp.where(same, hold, got)

    def middle(self, state):
        bits = self.cut
        for other in self.others:
            hold = self.keep(state, bits)
            state = (state[0], hold, flip(hold, other))
            bits = other
        return state

    def last(self, state):
        hold = self.keep(state, self.others[-1])
        return hold, flip(hold, self.cut)

    def join(self, hold, got):
        return place(self.cut, hold, got, flip(hold, (0, 0)), flip(got, (0, 0)))

    def join_above(self, hold, got):
        both = shifted(jnp.stack([hold, got]), "rows", 1)
        other = flip(both, (0, 0))
        return place(self.cut, both[:1], both[1:], other[:1], other[1:])[0]


def apply(q, x):
    product = lax.dot_general(q, x, (((0,), (0,)), ((), ())), preferred_element_type=jnp.float32)
    return product.astype(jnp.bfloat16)


def apply_many(q, x):
    product = jnp.einsum("nab,nac->nbc", q, x, preferred_element_type=jnp.float32)
    return product.astype(jnp.bfloat16)


def local(slab, transforms, owners):
    row_block = lax.axis_index("rows")
    last_block = lax.axis_size("rows") - 1
    window = transforms.shape[2]
    border = window // 2
    local_rows, local_cols = slab.shape
    wins = local_rows // window
    rounds = owners.shape[0]
    slot = transforms[0].reshape(2 * wins, 2, 2, window // 4, window)
    edge = [0, wins - 1, 2 * wins - 1]
    inside = [m for m in range(2 * wins) if m not in edge]
    spread = Spread(slot, owners[:, row_block], (edge, inside))

    states, pairs = {}, {}
    for r in range(rounds):
        for g in range(2):
            first = None if r == 0 else (states[r - 1, 0][2] if g == 0 else pairs[r - 1, 0][1])
            states[r, g] = spread.middle(spread.begin(r, g, first))
        for g in range(2):
            pairs[r, g] = spread.last(states[r, g])

    matrix = slab
    for r in range(rounds):
        head, tail = pairs[r, 0], pairs[r, 1]
        edges = spread.join(*head)
        head_rows = apply(edges[0], matrix[:window])
        tail_rows = apply(edges[1], matrix[local_rows - window :])
        begin, end = head_rows[:border], tail_rows[border:]
        above, below = swap_rows(begin, end)
        prev = spread.join_above(head[0][-1, :, border:], head[1][-1, :, border:])
        rest = spread.join(*tail)
        mid = apply_many(
            rest[: wins - 2],
            matrix[window : local_rows - window].reshape(wins - 2, window, local_cols),
        ).reshape(local_rows - 2 * window, local_cols)
        centre = jnp.concatenate([head_rows[border:], mid, tail_rows[:border]], 0)
        inner = apply_many(rest[wins - 2 :], centre.reshape(wins - 1, window, local_cols)).reshape(
            local_rows - window, local_cols
        )
        low = apply(edges[2, :, :border], jnp.concatenate([end, below], 0))
        low = jnp.where(row_block == last_block, end, low)
        top = apply(prev, jnp.concatenate([above, begin], 0))
        top = jnp.where(row_block == 0, begin, top)
        matrix = jnp.concatenate([top, inner, low], 0)
    return matrix


def solution(mesh):
    return jax.shard_map(
        local,
        mesh=mesh,
        in_specs=(P("rows", "cols"), P("cols", "rows", None), P()),
        out_specs=P("rows", "cols"),
        check_vma=False,
    )
```

```python
import jax
import jax.numpy as jnp
from jax import lax
from jax.experimental import pallas as pl
from jax.experimental.pallas import tpu as pltpu
from jax.sharding import PartitionSpec as P


def shifted(value, axis, steps):
    count = lax.axis_size(axis)
    initial, last = (max(0, -steps), min(count, count - steps))
    return lax.ppermute(value, axis, [(source, source + steps) for source in range(initial, last)])


def swap_rows(up, down):
    count = lax.axis_size("rows")
    even = (lax.axis_index("rows") & 1) == 0

    def swap(value, start):
        pairs = [(low, low + 1) for low in range(start, count - 1, 2)]
        return lax.ppermute(value, "rows", pairs + [(b, a) for a, b in pairs])

    first = swap(jnp.where(even, down, up), 0)
    second = swap(jnp.where(even, up, down), 1)
    return jnp.where(even, second, first), jnp.where(even, first, second)


def flip(value, bits):
    count = lax.axis_size("cols")
    return lax.ppermute(value, "cols", [(d, d ^ (1 << bits[d & 1])) for d in range(count)])


def copy_all(copies):
    for copy in copies:
        copy.start()
    for copy in copies:
        copy.wait()


def small(flops=0, bytes_accessed=0, limit=1 << 20):
    return dict(
        compiler_params=pltpu.CompilerParams(vmem_limit_bytes=limit),
        cost_estimate=pl.CostEstimate(
            flops=flops, bytes_accessed=bytes_accessed, transcendentals=0
        ),
    )


ANY = pl.BlockSpec(memory_space=pl.ANY)


def after(value, *done):
    def kernel(source, *refs):
        copy_all([pltpu.make_async_copy(source, refs[-2], refs[-1])])

    return pl.pallas_call(
        kernel,
        out_shape=jax.ShapeDtypeStruct(value.shape, value.dtype),
        in_specs=[ANY] * (1 + len(done)),
        out_specs=ANY,
        scratch_shapes=[pltpu.SemaphoreType.DMA],
        name="after",
        **small(bytes_accessed=4 * value.size),
    )(value, *done)


def runs(ms):
    found = []
    for at, m in enumerate(ms):
        if found and found[-1][0] + found[-1][2] == m:
            found[-1][2] += 1
        else:
            found.append([m, at, 1])
    return found


def cut_slot(cut, order, kinds, slot):
    _, _, _, rows, width = slot.shape
    shapes = [jax.ShapeDtypeStruct((len(order), rows, width), slot.dtype) for _ in kinds]
    spans = runs(order)

    def kernel(source, *refs):
        outs, sems = refs[:-1], refs[-1]
        me = lax.axis_index("cols")
        core = me & 1
        bit0 = (me >> cut[0]) & 1
        bit1 = (me >> cut[1]) & 1
        mine = jnp.where(core == 0, bit0, bit1)
        other = jnp.where(core == 0, bit1, bit0)
        copies = []
        for (own, hold), out in zip(kinds, outs):
            half = core if own else 1 - core
            piece = mine if own else other
            piece = piece if hold else 1 - piece
            for first, at, n in spans:
                copies.append(
                    pltpu.make_async_copy(
                        source.at[pl.ds(first, n), half, piece],
                        out.at[pl.ds(at, n)],
                        sems.at[len(copies)],
                    )
                )
        copy_all(copies)

    return pl.pallas_call(
        kernel,
        out_shape=shapes,
        in_specs=[pl.BlockSpec(memory_space=pltpu.HBM)],
        out_specs=[ANY] * len(shapes),
        scratch_shapes=[pltpu.SemaphoreType.DMA((len(spans) * len(kinds),))],
        name="cut_slot",
        **small(bytes_accessed=len(kinds) * slot.size, limit=(48 if len(kinds) == 1 else 1) << 20),
    )(slot)


def place_kernel(cut, hold, got, other_hold, other_got, out, sems):
    me = lax.axis_index("cols")
    core = me & 1
    rows = hold.shape[1]
    bit0 = (me >> cut[0]) & 1
    bit1 = (me >> cut[1]) & 1
    mine = jnp.where(core == 0, bit0, bit1)
    other = jnp.where(core == 0, bit1, bit0)
    slots = (
        (hold, core * 2 + mine),
        (got, core * 2 + 1 - mine),
        (other_hold, (1 - core) * 2 + other),
        (other_got, (1 - core) * 2 + 1 - other),
    )
    copies = [
        pltpu.make_async_copy(
            piece, out.at[:, pl.ds(pl.multiple_of(at * rows, rows), rows), :], sems.at[k]
        )
        for k, (piece, at) in enumerate(slots)
    ]
    copy_all(copies)


def place(cut, hold, got, other_hold, other_got):
    n, rows, width = hold.shape
    return pl.pallas_call(
        lambda *refs: place_kernel(cut, *refs),
        out_shape=jax.ShapeDtypeStruct((n, 4 * rows, width), hold.dtype),
        in_specs=[ANY] * 4,
        out_specs=ANY,
        scratch_shapes=[pltpu.SemaphoreType.DMA((4,))],
        name="place",
        **small(bytes_accessed=2 * n * 4 * rows * width * 2),
    )(hold, got, other_hold, other_got)


class Spread:
    def __init__(self, slot, owners_here, order):
        count = lax.axis_size("cols")
        dims = count.bit_length() - 2
        self.me = lax.axis_index("cols")
        self.core = self.me & 1
        self.owners = owners_here
        self.cut = (1, dims)
        self.others = [(b, b - 1) for b in range(2, dims + 1)]
        (give_out,) = cut_slot(self.cut, order, [(False, False)], slot)
        own_out, give_hold, own_hold = cut_slot(
            self.cut, order, [(True, False), (False, True), (True, True)], slot
        )
        self.own = own_out, own_hold
        self.theirs = flip(give_out, (0, 0)), flip(give_hold, (0, 0))

    def bit(self, index, bits):
        return (index >> jnp.where(self.core == 0, bits[0], bits[1])) & 1

    def choose(self, rounds, test, yes, no):
        holds = [test(self.owners[r]) for r in rounds]
        mask = holds[0]
        for at in range(1, len(rounds)):
            if rounds[at] != rounds[at - 1]:
                row = lax.broadcasted_iota(jnp.int32, yes.shape, 0)
                mask = jnp.where(row < at, mask, holds[at])
        return jnp.where(mask, yes, no)

    def begin(self, rounds, rows, *first):
        out, hold = [
            self.choose(rounds, lambda owner: (owner & 1) == self.core, own[rows], theirs[rows])
            for own, theirs in zip(self.own, self.theirs)
        ]
        if first:
            out = after(out, *first)
        return rounds, hold, flip(out, self.cut)

    def keep(self, state, bits):
        rounds, hold, got = state
        mine = self.bit(self.me, bits)
        return self.choose(rounds, lambda owner: mine == self.bit(owner, bits), hold, got)

    def middle(self, state, *first):
        bits = self.cut
        for other in self.others:
            hold = self.keep(state, bits)
            if first:
                hold = after(hold, *first)
                first = ()
            state = (state[0], hold, flip(hold, other))
            bits = other
        return state

    def last(self, state, *first):
        hold = self.keep(state, self.others[-1])
        if first:
            hold = after(hold, *first)
        return hold, flip(hold, self.cut)

    def join(self, hold, got):
        return place(self.cut, hold, got, flip(hold, (0, 0)), flip(got, (0, 0)))

    def join_above(self, hold, got):
        both = shifted(jnp.stack([hold, got]), "rows", 1)
        other = flip(both, (0, 0))
        return place(self.cut, both[0], both[1], other[0], other[1])


def apply(q, x):
    product = lax.dot_general(q, x, (((0,), (0,)), ((), ())), preferred_element_type=jnp.float32)
    return product.astype(jnp.bfloat16)


def apply_many(q, x):
    product = jnp.einsum("nab,nac->nbc", q, x, preferred_element_type=jnp.float32)
    return product.astype(jnp.bfloat16)


def local(slab, transforms, owners):
    row_block = lax.axis_index("rows")
    last_block = lax.axis_size("rows") - 1
    window = transforms.shape[2]
    border = window // 2
    local_rows, local_cols = slab.shape
    wins = local_rows // window
    rounds = owners.shape[0]
    slot = transforms[0].reshape(2 * wins, 2, 2, window // 4, window)
    crossing = 2 * wins - 1
    inside = [m for m in range(crossing) if m not in (0, wins - 1)]
    spread = Spread(slot, owners[:, row_block], [0, wins - 1, crossing, crossing] + inside)

    heads, tails = [], []
    for r in range(rounds):
        across = ([r] if r == 0 else []) + ([r + 1] if r + 1 < rounds else [])
        edge_rounds = [r, r] + across
        edge_rows = slice(0, len(edge_rounds))
        rest_rounds = [r] * len(inside)
        rest_rows = slice(4, 4 + len(inside))
        if r == 0:
            head = spread.middle(spread.begin(edge_rounds, edge_rows))
            tail_one = spread.begin(rest_rounds, rest_rows)
            tail_two = spread.middle(tail_one)
            head_end = spread.last(head)
            tail_end = spread.last(tail_two)
        else:
            head_one = spread.begin(edge_rounds, edge_rows, tail_one[2])
            head_two = spread.middle(head_one, tail_two[2])
            tail_one = spread.begin(rest_rounds, rest_rows, head_end[1])
            tail_two = spread.middle(tail_one)
            head_end = spread.last(head_two, tail_end[1], tail_one[2])
            tail_end = spread.last(tail_two)
        heads.append(head_end)
        tails.append(tail_end)

    matrix = slab
    crosses, above_crosses = [], []
    for r in range(rounds):
        head, tail = heads[r], tails[r]
        edges = spread.join(*head)
        crosses += [edges[k] for k in range(2, edges.shape[0])]
        if edges.shape[0] > 2:
            from_above = spread.join_above(head[0][2:, :, border:], head[1][2:, :, border:])
            above_crosses += [from_above[k] for k in range(from_above.shape[0])]
        prev, cross = above_crosses[r], crosses[r]
        head_rows = apply(edges[0], matrix[:window])
        tail_rows = apply(edges[1], matrix[local_rows - window :])
        begin, end = head_rows[:border], tail_rows[border:]
        above, below = swap_rows(begin, end)
        rest = spread.join(*tail)
        mid = apply_many(
            rest[: wins - 2],
            matrix[window : local_rows - window].reshape(wins - 2, window, local_cols),
        ).reshape(local_rows - 2 * window, local_cols)
        centre = jnp.concatenate([head_rows[border:], mid, tail_rows[:border]], 0)
        inner = apply_many(rest[wins - 2 :], centre.reshape(wins - 1, window, local_cols)).reshape(
            local_rows - window, local_cols
        )
        low = apply(cross[:, :border], jnp.concatenate([end, below], 0))
        low = jnp.where(row_block == last_block, end, low)
        top = apply(prev, jnp.concatenate([above, begin], 0))
        top = jnp.where(row_block == 0, begin, top)
        matrix = jnp.concatenate([top, inner, low], 0)
    return matrix


def solution(mesh):
    return jax.shard_map(
        local,
        mesh=mesh,
        in_specs=(P("rows", "cols"), P("cols", "rows", None), P()),
        out_specs=P("rows", "cols"),
        check_vma=False,
    )
```

```python
import jax
import jax.numpy as jnp
from jax import lax
from jax.experimental import pallas as pl
from jax.experimental.pallas import tpu as pltpu
from jax.sharding import PartitionSpec as P


def shifted(value, axis, steps):
    count = lax.axis_size(axis)
    initial, last = (max(0, -steps), min(count, count - steps))
    return lax.ppermute(value, axis, [(source, source + steps) for source in range(initial, last)])


def swap_rows(up, down):
    count = lax.axis_size("rows")
    even = (lax.axis_index("rows") & 1) == 0

    def swap(value, start):
        pairs = [(low, low + 1) for low in range(start, count - 1, 2)]
        return lax.ppermute(value, "rows", pairs + [(b, a) for a, b in pairs])

    first = swap(jnp.where(even, down, up), 0)
    second = swap(jnp.where(even, up, down), 1)
    return jnp.where(even, second, first), jnp.where(even, first, second)


def flip(value, bits):
    count = lax.axis_size("cols")
    return lax.ppermute(value, "cols", [(d, d ^ (1 << bits[d & 1])) for d in range(count)])


def copy_all(copies):
    for copy in copies:
        copy.start()
    for copy in copies:
        copy.wait()


def small(flops=0, bytes_accessed=0, limit=1 << 20):
    return dict(
        compiler_params=pltpu.CompilerParams(vmem_limit_bytes=limit),
        cost_estimate=pl.CostEstimate(
            flops=flops, bytes_accessed=bytes_accessed, transcendentals=0
        ),
    )


ANY = pl.BlockSpec(memory_space=pl.ANY)


def after(value, *done):
    def kernel(source, *refs):
        copy_all([pltpu.make_async_copy(source, refs[-2], refs[-1])])

    return pl.pallas_call(
        kernel,
        out_shape=jax.ShapeDtypeStruct(value.shape, value.dtype),
        in_specs=[ANY] * (1 + len(done)),
        out_specs=ANY,
        scratch_shapes=[pltpu.SemaphoreType.DMA],
        name="after",
        **small(bytes_accessed=4 * value.size),
    )(value, *done)


def runs(ms):
    found = []
    for at, m in enumerate(ms):
        if found and found[-1][0] + found[-1][2] == m:
            found[-1][2] += 1
        else:
            found.append([m, at, 1])
    return found


def cut_slot(cut, order, kinds, slot):
    _, _, _, rows, width = slot.shape
    shapes = [jax.ShapeDtypeStruct((len(order), rows, width), slot.dtype) for _ in kinds]
    spans = runs(order)

    def kernel(source, *refs):
        outs, sems = refs[:-1], refs[-1]
        me = lax.axis_index("cols")
        core = me & 1
        bit0 = (me >> cut[0]) & 1
        bit1 = (me >> cut[1]) & 1
        mine = jnp.where(core == 0, bit0, bit1)
        other = jnp.where(core == 0, bit1, bit0)
        copies = []
        for (own, hold), out in zip(kinds, outs):
            half = core if own else 1 - core
            piece = mine if own else other
            piece = piece if hold else 1 - piece
            for first, at, n in spans:
                copies.append(
                    pltpu.make_async_copy(
                        source.at[pl.ds(first, n), half, piece],
                        out.at[pl.ds(at, n)],
                        sems.at[len(copies)],
                    )
                )
        copy_all(copies)

    return pl.pallas_call(
        kernel,
        out_shape=shapes,
        in_specs=[pl.BlockSpec(memory_space=pltpu.HBM)],
        out_specs=[ANY] * len(shapes),
        scratch_shapes=[pltpu.SemaphoreType.DMA((len(spans) * len(kinds),))],
        name="cut_slot",
        **small(bytes_accessed=len(kinds) * slot.size, limit=(48 if len(kinds) == 1 else 1) << 20),
    )(slot)


def place_kernel(cut, hold, got, other_hold, other_got, out, sems):
    me = lax.axis_index("cols")
    core = me & 1
    rows = hold.shape[1]
    bit0 = (me >> cut[0]) & 1
    bit1 = (me >> cut[1]) & 1
    mine = jnp.where(core == 0, bit0, bit1)
    other = jnp.where(core == 0, bit1, bit0)
    slots = (
        (hold, core * 2 + mine),
        (got, core * 2 + 1 - mine),
        (other_hold, (1 - core) * 2 + other),
        (other_got, (1 - core) * 2 + 1 - other),
    )
    copies = [
        pltpu.make_async_copy(
            piece, out.at[:, pl.ds(pl.multiple_of(at * rows, rows), rows), :], sems.at[k]
        )
        for k, (piece, at) in enumerate(slots)
    ]
    copy_all(copies)


def place(cut, hold, got, other_hold, other_got):
    n, rows, width = hold.shape
    return pl.pallas_call(
        lambda *refs: place_kernel(cut, *refs),
        out_shape=jax.ShapeDtypeStruct((n, 4 * rows, width), hold.dtype),
        in_specs=[ANY] * 4,
        out_specs=ANY,
        scratch_shapes=[pltpu.SemaphoreType.DMA((4,))],
        name="place",
        **small(bytes_accessed=2 * n * 4 * rows * width * 2),
    )(hold, got, other_hold, other_got)


class Spread:
    def __init__(self, slot, owners_here, order):
        count = lax.axis_size("cols")
        dims = count.bit_length() - 2
        self.me = lax.axis_index("cols")
        self.core = self.me & 1
        self.owners = owners_here
        self.cut = (1, dims)
        self.others = [(b, b - 1) for b in range(2, dims + 1)]
        (give_out,) = cut_slot(self.cut, order, [(False, False)], slot)
        own_out, give_hold, own_hold = cut_slot(
            self.cut, order, [(True, False), (False, True), (True, True)], slot
        )
        self.own = own_out, own_hold
        self.theirs = flip(give_out, (0, 0)), flip(give_hold, (0, 0))

    def bit(self, index, bits):
        return (index >> jnp.where(self.core == 0, bits[0], bits[1])) & 1

    def choose(self, rounds, test, yes, no):
        holds = [test(self.owners[r]) for r in rounds]
        mask = holds[0]
        for at in range(1, len(rounds)):
            if rounds[at] != rounds[at - 1]:
                row = lax.broadcasted_iota(jnp.int32, yes.shape, 0)
                mask = jnp.where(row < at, mask, holds[at])
        return jnp.where(mask, yes, no)

    def begin(self, rounds, rows, *first):
        out, hold = [
            self.choose(rounds, lambda owner: (owner & 1) == self.core, own[rows], theirs[rows])
            for own, theirs in zip(self.own, self.theirs)
        ]
        if first:
            out = after(out, *first)
        return rounds, hold, flip(out, self.cut)

    def keep(self, state, bits):
        rounds, hold, got = state
        mine = self.bit(self.me, bits)
        return self.choose(rounds, lambda owner: mine == self.bit(owner, bits), hold, got)

    def middle(self, state, *first):
        bits = self.cut
        for other in self.others:
            hold = self.keep(state, bits)
            if first:
                hold = after(hold, *first)
                first = ()
            state = (state[0], hold, flip(hold, other))
            bits = other
        return state

    def last(self, state, *first):
        hold = self.keep(state, self.others[-1])
        if first:
            hold = after(hold, *first)
        return hold, flip(hold, self.cut)

    def join(self, hold, got):
        return place(self.cut, hold, got, flip(hold, (0, 0)), flip(got, (0, 0)))

    def join_above(self, hold, got):
        both = shifted(jnp.stack([hold, got]), "rows", 1)
        other = flip(both, (0, 0))
        return place(self.cut, both[0], both[1], other[0], other[1])


def apply(q, x):
    product = lax.dot_general(q, x, (((0,), (0,)), ((), ())), preferred_element_type=jnp.float32)
    return product.astype(jnp.bfloat16)


def apply_many(q, x):
    product = jnp.einsum("nab,nac->nbc", q, x, preferred_element_type=jnp.float32)
    return product.astype(jnp.bfloat16)


def local(slab, transforms, owners):
    row_block = lax.axis_index("rows")
    last_block = lax.axis_size("rows") - 1
    window = transforms.shape[2]
    border = window // 2
    local_rows, local_cols = slab.shape
    wins = local_rows // window
    rounds = owners.shape[0]
    slot = transforms[0].reshape(2 * wins, 2, 2, window // 4, window)
    crossing = 2 * wins - 1
    middle_one, middle_two = list(range(1, wins - 1)), list(range(wins, crossing))
    order = [crossing, crossing, 0, wins - 1] + middle_one + middle_two
    spread = Spread(slot, owners[:, row_block], order)
    cut_one, cut_two = 4 + len(middle_one), len(order)

    heads, tails = [], []
    for r in range(rounds):
        across = ([r + 1] if r + 1 < rounds else []) + ([r] if r == 0 else [])
        if r == 0:
            head = spread.begin(across + [r, r], slice(2 - len(across), 4))
            tail = spread.begin([r] * (cut_two - 4), slice(4, cut_two))
        else:
            head = spread.begin(across + [r] * wins, slice(2 - len(across), cut_one), head[2])
            tail = spread.begin([r] * (cut_two - cut_one), slice(cut_one, cut_two), tail[2])
        head, tail = spread.middle(head), spread.middle(tail)
        heads.append(spread.last(head))
        tails.append(spread.last(tail))

    matrix = slab
    crosses, above_crosses = {}, {}
    for r in range(rounds):
        head, tail = heads[r], tails[r]
        edges = spread.join(*head)
        across = ([r + 1] if r + 1 < rounds else []) + ([r] if r == 0 else [])
        if across:
            n = len(across)
            from_above = spread.join_above(head[0][:n, :, border:], head[1][:n, :, border:])
            for k, q in enumerate(across):
                crosses[q], above_crosses[q] = edges[k], from_above[k]
            edges = edges[n:]
        prev, cross = above_crosses[r], crosses[r]
        head_rows = apply(edges[0], matrix[:window])
        tail_rows = apply(edges[1], matrix[local_rows - window :])
        begin, end = head_rows[:border], tail_rows[border:]
        above, below = swap_rows(begin, end)
        rest = spread.join(*tail)
        if r == 0:
            ones, twos = rest[: wins - 2], rest[wins - 2 :]
        else:
            ones, twos = edges[2:], rest
        mid = apply_many(
            ones,
            matrix[window : local_rows - window].reshape(wins - 2, window, local_cols),
        ).reshape(local_rows - 2 * window, local_cols)
        centre = jnp.concatenate([head_rows[border:], mid, tail_rows[:border]], 0)
        inner = apply_many(twos, centre.reshape(wins - 1, window, local_cols)).reshape(
            local_rows - window, local_cols
        )
        low = apply(cross[:, :border], jnp.concatenate([end, below], 0))
        low = jnp.where(row_block == last_block, end, low)
        top = apply(prev, jnp.concatenate([above, begin], 0))
        top = jnp.where(row_block == 0, begin, top)
        matrix = jnp.concatenate([top, inner, low], 0)
    return matrix


def solution(mesh):
    return jax.shard_map(
        local,
        mesh=mesh,
        in_specs=(P("rows", "cols"), P("cols", "rows", None), P()),
        out_specs=P("rows", "cols"),
        check_vma=False,
    )
```

```python
import jax
import jax.numpy as jnp
from jax import lax
from jax.experimental import pallas as pl
from jax.experimental.pallas import tpu as pltpu
from jax.sharding import PartitionSpec as P


def shifted(value, axis, steps):
    count = lax.axis_size(axis)
    initial, last = (max(0, -steps), min(count, count - steps))
    return lax.ppermute(value, axis, [(source, source + steps) for source in range(initial, last)])


def swap_rows(up, down):
    count = lax.axis_size("rows")
    even = (lax.axis_index("rows") & 1) == 0

    def swap(value, start):
        pairs = [(low, low + 1) for low in range(start, count - 1, 2)]
        return lax.ppermute(value, "rows", pairs + [(b, a) for a, b in pairs])

    first = swap(jnp.where(even, down, up), 0)
    second = swap(jnp.where(even, up, down), 1)
    return (jnp.where(even, second, first), jnp.where(even, first, second)), (first, second)


def flip(value, bits):
    count = lax.axis_size("cols")
    return lax.ppermute(value, "cols", [(d, d ^ (1 << bits[d & 1])) for d in range(count)])


def copy_all(copies):
    for copy in copies:
        copy.start()
    for copy in copies:
        copy.wait()


def small(flops=0, bytes_accessed=0, limit=1 << 20):
    return dict(
        compiler_params=pltpu.CompilerParams(vmem_limit_bytes=limit),
        cost_estimate=pl.CostEstimate(
            flops=flops, bytes_accessed=bytes_accessed, transcendentals=0
        ),
    )


ANY = pl.BlockSpec(memory_space=pl.ANY)


def after(value, *done, rows=None):
    start, count = (0, value.shape[0]) if rows is None else (rows.start, rows.stop - rows.start)

    def kernel(source, *refs):
        copy_all([pltpu.make_async_copy(source.at[pl.ds(start, count)], refs[-2], refs[-1])])

    return pl.pallas_call(
        kernel,
        out_shape=jax.ShapeDtypeStruct((count,) + value.shape[1:], value.dtype),
        in_specs=[ANY] * (1 + len(done)),
        out_specs=ANY,
        scratch_shapes=[pltpu.SemaphoreType.DMA],
        name="after",
        **small(bytes_accessed=4 * value.size),
    )(value, *done)


def runs(ms):
    found = []
    for at, m in enumerate(ms):
        if found and found[-1][0] + found[-1][2] == m:
            found[-1][2] += 1
        else:
            found.append([m, at, 1])
    return found


def cut_slot(cut, order, kinds, slot):
    _, _, _, rows, width = slot.shape
    shapes = [jax.ShapeDtypeStruct((len(order), rows, width), slot.dtype) for _ in kinds]
    spans = runs(order)

    def kernel(source, *refs):
        outs, sems = refs[:-1], refs[-1]
        me = lax.axis_index("cols")
        core = me & 1
        bit0 = (me >> cut[0]) & 1
        bit1 = (me >> cut[1]) & 1
        mine = jnp.where(core == 0, bit0, bit1)
        other = jnp.where(core == 0, bit1, bit0)
        copies = []
        for (own, hold), out in zip(kinds, outs):
            half = core if own else 1 - core
            piece = mine if own else other
            piece = piece if hold else 1 - piece
            for first, at, n in spans:
                copies.append(
                    pltpu.make_async_copy(
                        source.at[pl.ds(first, n), half, piece],
                        out.at[pl.ds(at, n)],
                        sems.at[len(copies)],
                    )
                )
        copy_all(copies)

    return pl.pallas_call(
        kernel,
        out_shape=shapes,
        in_specs=[pl.BlockSpec(memory_space=pltpu.HBM)],
        out_specs=[ANY] * len(shapes),
        scratch_shapes=[pltpu.SemaphoreType.DMA((len(spans) * len(kinds),))],
        name="cut_slot",
        **small(bytes_accessed=len(kinds) * slot.size, limit=(48 if len(kinds) == 1 else 1) << 20),
    )(slot)


def place_kernel(cut, hold, got, other_hold, other_got, out, sems):
    me = lax.axis_index("cols")
    core = me & 1
    rows = hold.shape[1]
    bit0 = (me >> cut[0]) & 1
    bit1 = (me >> cut[1]) & 1
    mine = jnp.where(core == 0, bit0, bit1)
    other = jnp.where(core == 0, bit1, bit0)
    slots = (
        (hold, core * 2 + mine),
        (got, core * 2 + 1 - mine),
        (other_hold, (1 - core) * 2 + other),
        (other_got, (1 - core) * 2 + 1 - other),
    )
    copies = [
        pltpu.make_async_copy(
            piece, out.at[:, pl.ds(pl.multiple_of(at * rows, rows), rows), :], sems.at[k]
        )
        for k, (piece, at) in enumerate(slots)
    ]
    copy_all(copies)


def place(cut, hold, got, other_hold, other_got):
    n, rows, width = hold.shape
    return pl.pallas_call(
        lambda *refs: place_kernel(cut, *refs),
        out_shape=jax.ShapeDtypeStruct((n, 4 * rows, width), hold.dtype),
        in_specs=[ANY] * 4,
        out_specs=ANY,
        scratch_shapes=[pltpu.SemaphoreType.DMA((4,))],
        name="place",
        **small(bytes_accessed=2 * n * 4 * rows * width * 2),
    )(hold, got, other_hold, other_got)


class Spread:
    def __init__(self, slot, owners_here, order):
        count = lax.axis_size("cols")
        dims = count.bit_length() - 2
        self.me = lax.axis_index("cols")
        self.core = self.me & 1
        self.owners = owners_here
        self.cut = (1, dims)
        self.others = [(b, b - 1) for b in range(2, dims + 1)]
        (give_out,) = cut_slot(self.cut, order, [(False, False)], slot)
        own_out, give_hold, own_hold = cut_slot(
            self.cut, order, [(True, False), (False, True), (True, True)], slot
        )
        self.own = own_out, own_hold
        self.theirs = flip(give_out, (0, 0)), flip(give_hold, (0, 0))

    def bit(self, index, bits):
        return (index >> jnp.where(self.core == 0, bits[0], bits[1])) & 1

    def choose(self, rounds, test, yes, no):
        holds = [test(self.owners[r]) for r in rounds]
        mask = holds[0]
        for at in range(1, len(rounds)):
            if rounds[at] != rounds[at - 1]:
                row = lax.broadcasted_iota(jnp.int32, yes.shape, 0)
                mask = jnp.where(row < at, mask, holds[at])
        return jnp.where(mask, yes, no)

    def begin(self, rounds, rows, *first):
        parts = []
        for own, theirs in zip(self.own, self.theirs):
            theirs = after(theirs, *first, rows=rows) if first else theirs[rows]
            parts.append(
                self.choose(rounds, lambda owner: (owner & 1) == self.core, own[rows], theirs)
            )
        return rounds, parts[1], flip(parts[0], self.cut)

    def keep(self, state, bits):
        rounds, hold, got = state
        mine = self.bit(self.me, bits)
        return self.choose(rounds, lambda owner: mine == self.bit(owner, bits), hold, got)

    def middle(self, state, *first):
        bits = self.cut
        for other in self.others:
            hold = self.keep(state, bits)
            if first:
                hold = after(hold, *first)
                first = ()
            state = (state[0], hold, flip(hold, other))
            bits = other
        return state

    def last(self, state, *first):
        hold = self.keep(state, self.others[-1])
        if first:
            hold = after(hold, *first)
        return hold, flip(hold, self.cut)

    def join(self, hold, got):
        return place(self.cut, hold, got, flip(hold, (0, 0)), flip(got, (0, 0)))

    def join_above(self, hold, got):
        both = shifted(jnp.stack([hold, got]), "rows", 1)
        other = flip(both, (0, 0))
        return place(self.cut, both[0], both[1], other[0], other[1])


def apply(q, x):
    product = lax.dot_general(q, x, (((0,), (0,)), ((), ())), preferred_element_type=jnp.float32)
    return product.astype(jnp.bfloat16)


def apply_many(q, x):
    product = jnp.einsum("nab,nac->nbc", q, x, preferred_element_type=jnp.float32)
    return product.astype(jnp.bfloat16)


def local(slab, transforms, owners):
    row_block = lax.axis_index("rows")
    last_block = lax.axis_size("rows") - 1
    window = transforms.shape[2]
    border = window // 2
    local_rows, local_cols = slab.shape
    wins = local_rows // window
    rounds = owners.shape[0]
    slot = transforms[0].reshape(2 * wins, 2, 2, window // 4, window)
    crossing = 2 * wins - 1
    middle_one, middle_two = list(range(1, wins - 1)), list(range(wins, crossing))
    order = [crossing, crossing, 0, wins - 1] + middle_one + middle_two
    spread = Spread(slot, owners[:, row_block], order)
    cut_one, cut_two = 4 + len(middle_one), len(order)

    matrix = slab
    crosses, above_crosses = {}, {}
    for r in range(rounds):
        across = ([r + 1] if r + 1 < rounds else []) + ([r] if r == 0 else [])
        n = len(across)
        if r == 0:
            head = spread.middle(spread.begin(across + [r, r], slice(2 - n, 4)))
            tail = spread.middle(spread.begin([r] * (cut_two - 4), slice(4, cut_two)))
            head_pair, tail_pair = spread.last(head), spread.last(tail)
        else:
            head = spread.begin(across + [r] * wins, slice(2 - n, cut_one), head[2])
            tail = spread.begin([r] * (cut_two - cut_one), slice(cut_one, cut_two), tail[2])
            head, tail = spread.middle(head, head_rows, tail_rows), spread.middle(tail)
            head_pair, tail_pair = spread.last(head), spread.last(tail, *swapped)
        edges = spread.join(*head_pair)
        if n:
            from_above = spread.join_above(
                head_pair[0][:n, :, border:], head_pair[1][:n, :, border:]
            )
            for k, q in enumerate(across):
                crosses[q], above_crosses[q] = edges[k], from_above[k]
            edges = edges[n:]
        prev, cross = above_crosses[r], crosses[r]
        head_rows = apply(edges[0], matrix[:window])
        tail_rows = apply(edges[1], matrix[local_rows - window :])
        begin, end = head_rows[:border], tail_rows[border:]
        (above, below), swapped = swap_rows(begin, end)
        rest = spread.join(*tail_pair)
        if r == 0:
            ones, twos = rest[: wins - 2], rest[wins - 2 :]
        else:
            ones, twos = edges[2:], rest
        mid = apply_many(
            ones,
            matrix[window : local_rows - window].reshape(wins - 2, window, local_cols),
        ).reshape(local_rows - 2 * window, local_cols)
        centre = jnp.concatenate([head_rows[border:], mid, tail_rows[:border]], 0)
        inner = apply_many(twos, centre.reshape(wins - 1, window, local_cols)).reshape(
            local_rows - window, local_cols
        )
        low = apply(cross[:, :border], jnp.concatenate([end, below], 0))
        low = jnp.where(row_block == last_block, end, low)
        top = apply(prev, jnp.concatenate([above, begin], 0))
        top = jnp.where(row_block == 0, begin, top)
        matrix = jnp.concatenate([top, inner, low], 0)
    return matrix


def solution(mesh):
    return jax.shard_map(
        local,
        mesh=mesh,
        in_specs=(P("rows", "cols"), P("cols", "rows", None), P()),
        out_specs=P("rows", "cols"),
        check_vma=False,
    )
```

```python
import jax
import jax.numpy as jnp
from jax import lax
from jax.experimental import pallas as pl
from jax.experimental.pallas import tpu as pltpu
from jax.sharding import PartitionSpec as P


def shifted(value, axis, steps):
    count = lax.axis_size(axis)
    initial, last = (max(0, -steps), min(count, count - steps))
    return lax.ppermute(value, axis, [(source, source + steps) for source in range(initial, last)])


def swap_rows(up, down):
    count = lax.axis_size("rows")
    even = (lax.axis_index("rows") & 1) == 0

    def swap(value, start):
        pairs = [(low, low + 1) for low in range(start, count - 1, 2)]
        return lax.ppermute(value, "rows", pairs + [(b, a) for a, b in pairs])

    first = swap(jnp.where(even, down, up), 0)
    second = swap(jnp.where(even, up, down), 1)
    return jnp.where(even, second, first), jnp.where(even, first, second)


def flip(value, bits):
    count = lax.axis_size("cols")
    return lax.ppermute(value, "cols", [(d, d ^ (1 << bits[d & 1])) for d in range(count)])


def copy_all(copies):
    for copy in copies:
        copy.start()
    for copy in copies:
        copy.wait()


def small(flops=0, bytes_accessed=0, limit=1 << 20):
    return dict(
        compiler_params=pltpu.CompilerParams(vmem_limit_bytes=limit),
        cost_estimate=pl.CostEstimate(
            flops=flops, bytes_accessed=bytes_accessed, transcendentals=0
        ),
    )


ANY = pl.BlockSpec(memory_space=pl.ANY)


def after(value, *done):
    def kernel(source, *refs):
        copy_all([pltpu.make_async_copy(source, refs[-2], refs[-1])])

    return pl.pallas_call(
        kernel,
        out_shape=jax.ShapeDtypeStruct(value.shape, value.dtype),
        in_specs=[ANY] * (1 + len(done)),
        out_specs=ANY,
        scratch_shapes=[pltpu.SemaphoreType.DMA],
        name="after",
        **small(bytes_accessed=4 * value.size),
    )(value, *done)


def runs(ms):
    found = []
    for at, m in enumerate(ms):
        if found and found[-1][0] + found[-1][2] == m:
            found[-1][2] += 1
        else:
            found.append([m, at, 1])
    return found


def cut_slot(cut, order, kinds, slot):
    _, _, _, rows, width = slot.shape
    shapes = [jax.ShapeDtypeStruct((len(order), rows, width), slot.dtype) for _ in kinds]
    spans = runs(order)

    def kernel(source, *refs):
        outs, sems = refs[:-1], refs[-1]
        me = lax.axis_index("cols")
        core = me & 1
        bit0 = (me >> cut[0]) & 1
        bit1 = (me >> cut[1]) & 1
        mine = jnp.where(core == 0, bit0, bit1)
        other = jnp.where(core == 0, bit1, bit0)
        copies = []
        for (own, hold), out in zip(kinds, outs):
            half = core if own else 1 - core
            piece = mine if own else other
            piece = piece if hold else 1 - piece
            for first, at, n in spans:
                copies.append(
                    pltpu.make_async_copy(
                        source.at[pl.ds(first, n), half, piece],
                        out.at[pl.ds(at, n)],
                        sems.at[len(copies)],
                    )
                )
        copy_all(copies)

    return pl.pallas_call(
        kernel,
        out_shape=shapes,
        in_specs=[pl.BlockSpec(memory_space=pltpu.HBM)],
        out_specs=[ANY] * len(shapes),
        scratch_shapes=[pltpu.SemaphoreType.DMA((len(spans) * len(kinds),))],
        name="cut_slot",
        **small(bytes_accessed=len(kinds) * slot.size, limit=(48 if len(kinds) == 1 else 1) << 20),
    )(slot)


def place_kernel(cut, hold, got, other_hold, other_got, out, sems):
    me = lax.axis_index("cols")
    core = me & 1
    rows = hold.shape[1]
    bit0 = (me >> cut[0]) & 1
    bit1 = (me >> cut[1]) & 1
    mine = jnp.where(core == 0, bit0, bit1)
    other = jnp.where(core == 0, bit1, bit0)
    slots = (
        (hold, core * 2 + mine),
        (got, core * 2 + 1 - mine),
        (other_hold, (1 - core) * 2 + other),
        (other_got, (1 - core) * 2 + 1 - other),
    )
    copies = [
        pltpu.make_async_copy(
            piece, out.at[:, pl.ds(pl.multiple_of(at * rows, rows), rows), :], sems.at[k]
        )
        for k, (piece, at) in enumerate(slots)
    ]
    copy_all(copies)


def place(cut, hold, got, other_hold, other_got):
    n, rows, width = hold.shape
    return pl.pallas_call(
        lambda *refs: place_kernel(cut, *refs),
        out_shape=jax.ShapeDtypeStruct((n, 4 * rows, width), hold.dtype),
        in_specs=[ANY] * 4,
        out_specs=ANY,
        scratch_shapes=[pltpu.SemaphoreType.DMA((4,))],
        name="place",
        **small(bytes_accessed=2 * n * 4 * rows * width * 2),
    )(hold, got, other_hold, other_got)


class Spread:
    def __init__(self, slot, owners_here, order):
        count = lax.axis_size("cols")
        dims = count.bit_length() - 2
        self.me = lax.axis_index("cols")
        self.core = self.me & 1
        self.owners = owners_here
        self.cut = (1, dims)
        self.others = [(b, b - 1) for b in range(2, dims + 1)]
        (give_out,) = cut_slot(self.cut, order, [(False, False)], slot)
        own_out, give_hold, own_hold = cut_slot(
            self.cut, order, [(True, False), (False, True), (True, True)], slot
        )
        self.own = own_out, own_hold
        self.theirs = flip(give_out, (0, 0)), flip(give_hold, (0, 0))

    def bit(self, index, bits):
        return (index >> jnp.where(self.core == 0, bits[0], bits[1])) & 1

    def choose(self, rounds, test, yes, no):
        holds = [test(self.owners[r]) for r in rounds]
        mask = holds[0]
        for at in range(1, len(rounds)):
            if rounds[at] != rounds[at - 1]:
                row = lax.broadcasted_iota(jnp.int32, yes.shape, 0)
                mask = jnp.where(row < at, mask, holds[at])
        return jnp.where(mask, yes, no)

    def begin(self, rounds, rows, *first):
        out, hold = [
            self.choose(rounds, lambda owner: (owner & 1) == self.core, own[rows], theirs[rows])
            for own, theirs in zip(self.own, self.theirs)
        ]
        if first:
            out = after(out, *first)
        return rounds, hold, flip(out, self.cut)

    def keep(self, state, bits):
        rounds, hold, got = state
        mine = self.bit(self.me, bits)
        return self.choose(rounds, lambda owner: mine == self.bit(owner, bits), hold, got)

    def middle(self, state, *first):
        bits = self.cut
        for other in self.others:
            hold = self.keep(state, bits)
            if first:
                hold = after(hold, *first)
                first = ()
            state = (state[0], hold, flip(hold, other))
            bits = other
        return state

    def last(self, state, *first):
        hold = self.keep(state, self.others[-1])
        if first:
            hold = after(hold, *first)
        return hold, flip(hold, self.cut)

    def join(self, hold, got):
        return place(self.cut, hold, got, flip(hold, (0, 0)), flip(got, (0, 0)))

    def join_above(self, hold, got, *first):
        both = shifted(after(jnp.stack([hold, got]), *first), "rows", 1)
        other = flip(both, (0, 0))
        return place(self.cut, both[0], both[1], other[0], other[1])


def apply(q, x):
    product = lax.dot_general(q, x, (((0,), (0,)), ((), ())), preferred_element_type=jnp.float32)
    return product.astype(jnp.bfloat16)


def apply_many(q, x):
    product = jnp.einsum("nab,nac->nbc", q, x, preferred_element_type=jnp.float32)
    return product.astype(jnp.bfloat16)


def local(slab, transforms, owners):
    row_block = lax.axis_index("rows")
    last_block = lax.axis_size("rows") - 1
    window = transforms.shape[2]
    border = window // 2
    local_rows, local_cols = slab.shape
    wins = local_rows // window
    rounds = owners.shape[0]
    slot = transforms[0].reshape(2 * wins, 2, 2, window // 4, window)
    crossing = 2 * wins - 1
    middle_one, middle_two = list(range(1, wins - 1)), list(range(wins, crossing))
    order = [crossing, crossing, 0, wins - 1] + middle_one + middle_two
    spread = Spread(slot, owners[:, row_block], order)
    cut_one, cut_two = 4 + len(middle_one), len(order)

    matrix = slab
    crosses, above_crosses = {}, {}
    for r in range(rounds):
        across = ([r + 1] if r + 1 < rounds else []) + ([r] if r == 0 else [])
        n = len(across)
        if r == 0:
            head = spread.middle(spread.begin(across + [r, r], slice(2 - n, 4)))
            tail = spread.middle(spread.begin([r] * (cut_two - 4), slice(4, cut_two)))
        else:
            head = spread.begin(across + [r] * wins, slice(2 - n, cut_one), head[2])
            tail = spread.begin([r] * (cut_two - cut_one), slice(cut_one, cut_two), tail[2])
            head, tail = spread.middle(head), spread.middle(tail, head_rows, tail_rows)
        head_pair, tail_pair = spread.last(head), spread.last(tail)
        edges = spread.join(*head_pair)
        head_rows = apply(edges[n], matrix[:window])
        tail_rows = apply(edges[n + 1], matrix[local_rows - window :])
        if n:
            from_above = spread.join_above(
                head_pair[0][:n, :, border:], head_pair[1][:n, :, border:], head_rows, tail_rows
            )
            for k, q in enumerate(across):
                crosses[q], above_crosses[q] = edges[k], from_above[k]
        edges = edges[n:]
        prev, cross = above_crosses[r], crosses[r]
        begin, end = head_rows[:border], tail_rows[border:]
        above, below = swap_rows(begin, end)
        rest = spread.join(*tail_pair)
        if r == 0:
            ones, twos = rest[: wins - 2], rest[wins - 2 :]
        else:
            ones, twos = edges[2:], rest
        mid = apply_many(
            ones,
            matrix[window : local_rows - window].reshape(wins - 2, window, local_cols),
        ).reshape(local_rows - 2 * window, local_cols)
        centre = jnp.concatenate([head_rows[border:], mid, tail_rows[:border]], 0)
        inner = apply_many(twos, centre.reshape(wins - 1, window, local_cols)).reshape(
            local_rows - window, local_cols
        )
        low = apply(cross[:, :border], jnp.concatenate([end, below], 0))
        low = jnp.where(row_block == last_block, end, low)
        top = apply(prev, jnp.concatenate([above, begin], 0))
        top = jnp.where(row_block == 0, begin, top)
        matrix = jnp.concatenate([top, inner, low], 0)
    return matrix


def solution(mesh):
    return jax.shard_map(
        local,
        mesh=mesh,
        in_specs=(P("rows", "cols"), P("cols", "rows", None), P()),
        out_specs=P("rows", "cols"),
        check_vma=False,
    )
```

```python
import jax
import jax.numpy as jnp
from jax import lax
from jax.experimental import pallas as pl
from jax.experimental.pallas import tpu as pltpu
from jax.sharding import PartitionSpec as P


def shifted(value, axis, steps):
    count = lax.axis_size(axis)
    initial, last = (max(0, -steps), min(count, count - steps))
    return lax.ppermute(value, axis, [(source, source + steps) for source in range(initial, last)])


def swap_rows(up, down):
    count = lax.axis_size("rows")
    even = (lax.axis_index("rows") & 1) == 0

    def swap(value, start):
        pairs = [(low, low + 1) for low in range(start, count - 1, 2)]
        return lax.ppermute(value, "rows", pairs + [(b, a) for a, b in pairs])

    first = swap(jnp.where(even, down, up), 0)
    second = swap(jnp.where(even, up, down), 1)
    return jnp.where(even, second, first), jnp.where(even, first, second)


def flip(value, bits):
    count = lax.axis_size("cols")
    return lax.ppermute(value, "cols", [(d, d ^ (1 << bits[d & 1])) for d in range(count)])


def copy_all(copies):
    for copy in copies:
        copy.start()
    for copy in copies:
        copy.wait()


def small(flops=0, bytes_accessed=0, limit=1 << 20):
    return dict(
        compiler_params=pltpu.CompilerParams(vmem_limit_bytes=limit),
        cost_estimate=pl.CostEstimate(
            flops=flops, bytes_accessed=bytes_accessed, transcendentals=0
        ),
    )


ANY = pl.BlockSpec(memory_space=pl.ANY)


def after(value, *done):
    def kernel(source, *refs):
        copy_all([pltpu.make_async_copy(source, refs[-2], refs[-1])])

    return pl.pallas_call(
        kernel,
        out_shape=jax.ShapeDtypeStruct(value.shape, value.dtype),
        in_specs=[ANY] * (1 + len(done)),
        out_specs=ANY,
        scratch_shapes=[pltpu.SemaphoreType.DMA],
        name="after",
        **small(bytes_accessed=4 * value.size),
    )(value, *done)


def runs(ms):
    found = []
    for at, m in enumerate(ms):
        if found and found[-1][0] + found[-1][2] == m:
            found[-1][2] += 1
        else:
            found.append([m, at, 1])
    return found


def cut_slot(cut, order, kinds, slot):
    _, _, _, rows, width = slot.shape
    shapes = [jax.ShapeDtypeStruct((len(order), rows, width), slot.dtype) for _ in kinds]
    spans = runs(order)

    def kernel(source, *refs):
        outs, sems = refs[:-1], refs[-1]
        me = lax.axis_index("cols")
        core = me & 1
        bit0 = (me >> cut[0]) & 1
        bit1 = (me >> cut[1]) & 1
        mine = jnp.where(core == 0, bit0, bit1)
        other = jnp.where(core == 0, bit1, bit0)
        copies = []
        for (own, hold), out in zip(kinds, outs):
            half = core if own else 1 - core
            piece = mine if own else other
            piece = piece if hold else 1 - piece
            for first, at, n in spans:
                copies.append(
                    pltpu.make_async_copy(
                        source.at[pl.ds(first, n), half, piece],
                        out.at[pl.ds(at, n)],
                        sems.at[len(copies)],
                    )
                )
        copy_all(copies)

    return pl.pallas_call(
        kernel,
        out_shape=shapes,
        in_specs=[pl.BlockSpec(memory_space=pltpu.HBM)],
        out_specs=[ANY] * len(shapes),
        scratch_shapes=[pltpu.SemaphoreType.DMA((len(spans) * len(kinds),))],
        name="cut_slot",
        **small(bytes_accessed=len(kinds) * slot.size, limit=(48 if len(kinds) == 1 else 1) << 20),
    )(slot)


def place_kernel(cut, hold, got, other_hold, other_got, out, sems):
    me = lax.axis_index("cols")
    core = me & 1
    rows = hold.shape[1]
    bit0 = (me >> cut[0]) & 1
    bit1 = (me >> cut[1]) & 1
    mine = jnp.where(core == 0, bit0, bit1)
    other = jnp.where(core == 0, bit1, bit0)
    slots = (
        (hold, core * 2 + mine),
        (got, core * 2 + 1 - mine),
        (other_hold, (1 - core) * 2 + other),
        (other_got, (1 - core) * 2 + 1 - other),
    )
    copies = [
        pltpu.make_async_copy(
            piece, out.at[:, pl.ds(pl.multiple_of(at * rows, rows), rows), :], sems.at[k]
        )
        for k, (piece, at) in enumerate(slots)
    ]
    copy_all(copies)


def place(cut, hold, got, other_hold, other_got):
    n, rows, width = hold.shape
    return pl.pallas_call(
        lambda *refs: place_kernel(cut, *refs),
        out_shape=jax.ShapeDtypeStruct((n, 4 * rows, width), hold.dtype),
        in_specs=[ANY] * 4,
        out_specs=ANY,
        scratch_shapes=[pltpu.SemaphoreType.DMA((4,))],
        name="place",
        **small(bytes_accessed=2 * n * 4 * rows * width * 2),
    )(hold, got, other_hold, other_got)


class Spread:
    def __init__(self, slot, owners_here, order):
        count = lax.axis_size("cols")
        dims = count.bit_length() - 2
        self.me = lax.axis_index("cols")
        self.core = self.me & 1
        self.owners = owners_here
        self.cut = (1, dims)
        self.others = [(b, b - 1) for b in range(2, dims + 1)]
        (give_out,) = cut_slot(self.cut, order, [(False, False)], slot)
        own_out, give_hold, own_hold = cut_slot(
            self.cut, order, [(True, False), (False, True), (True, True)], slot
        )
        self.own = own_out, own_hold
        self.theirs = flip(give_out, (0, 0)), flip(give_hold, (0, 0))

    def bit(self, index, bits):
        return (index >> jnp.where(self.core == 0, bits[0], bits[1])) & 1

    def choose(self, rounds, test, yes, no):
        holds = [test(self.owners[r]) for r in rounds]
        mask = holds[0]
        for at in range(1, len(rounds)):
            if rounds[at] != rounds[at - 1]:
                row = lax.broadcasted_iota(jnp.int32, yes.shape, 0)
                mask = jnp.where(row < at, mask, holds[at])
        return jnp.where(mask, yes, no)

    def begin(self, rounds, rows, *first):
        out, hold = [
            self.choose(rounds, lambda owner: (owner & 1) == self.core, own[rows], theirs[rows])
            for own, theirs in zip(self.own, self.theirs)
        ]
        if first:
            out = after(out, *first)
        return rounds, hold, flip(out, self.cut)

    def keep(self, state, bits):
        rounds, hold, got = state
        mine = self.bit(self.me, bits)
        return self.choose(rounds, lambda owner: mine == self.bit(owner, bits), hold, got)

    def middle(self, state, *first):
        bits = self.cut
        for other in self.others:
            hold = self.keep(state, bits)
            if first:
                hold = after(hold, *first)
                first = ()
            state = (state[0], hold, flip(hold, other))
            bits = other
        return state

    def last(self, state, *first):
        hold = self.keep(state, self.others[-1])
        if first:
            hold = after(hold, *first)
        return hold, flip(hold, self.cut)

    def join(self, hold, got):
        return place(self.cut, hold, got, flip(hold, (0, 0)), flip(got, (0, 0)))

    def join_above(self, hold, got):
        both = shifted(jnp.stack([hold, got]), "rows", 1)
        other = flip(both, (0, 0))
        return place(self.cut, both[0], both[1], other[0], other[1])


def apply(q, x):
    product = lax.dot_general(q, x, (((0,), (0,)), ((), ())), preferred_element_type=jnp.float32)
    return product.astype(jnp.bfloat16)


def apply_many(q, x):
    product = jnp.einsum("nab,nac->nbc", q, x, preferred_element_type=jnp.float32)
    return product.astype(jnp.bfloat16)


def write_inner(inner, border):
    rows, cols = inner.shape

    def kernel(source, out):
        out[...] = source[...]

    return pl.pallas_call(
        kernel,
        grid=(rows // border,),
        out_shape=jax.ShapeDtypeStruct((rows + 2 * border, cols), inner.dtype),
        in_specs=[pl.BlockSpec((border, cols), lambda i: (i, 0))],
        out_specs=pl.BlockSpec((border, cols), lambda i: (i + 1, 0)),
        compiler_params=pltpu.CompilerParams(vmem_limit_bytes=8 << 20),
        cost_estimate=pl.CostEstimate(flops=0, bytes_accessed=4 * inner.size, transcendentals=0),
        name="write_inner",
    )(inner)


def write_outer(whole, top, low):
    border, cols = top.shape
    last = whole.shape[0] // border - 1

    def kernel(_, first, final, out):
        @pl.when(pl.program_id(0) == 0)
        def _():
            out[...] = first[...]

        @pl.when(pl.program_id(0) == 1)
        def _():
            out[...] = final[...]

    block = pl.BlockSpec((border, cols), lambda i: (0, 0))
    return pl.pallas_call(
        kernel,
        grid=(2,),
        out_shape=jax.ShapeDtypeStruct(whole.shape, whole.dtype),
        in_specs=[ANY, block, block],
        out_specs=pl.BlockSpec((border, cols), lambda i: (i * last, 0)),
        input_output_aliases={0: 0},
        compiler_params=pltpu.CompilerParams(vmem_limit_bytes=8 << 20),
        cost_estimate=pl.CostEstimate(flops=0, bytes_accessed=8 * top.size, transcendentals=0),
        name="write_outer",
    )(whole, top, low)


def local(slab, transforms, owners):
    row_block = lax.axis_index("rows")
    last_block = lax.axis_size("rows") - 1
    window = transforms.shape[2]
    border = window // 2
    local_rows, local_cols = slab.shape
    wins = local_rows // window
    rounds = owners.shape[0]
    slot = transforms[0].reshape(2 * wins, 2, 2, window // 4, window)
    crossing = 2 * wins - 1
    middle_one, middle_two = list(range(1, wins - 1)), list(range(wins, crossing))
    order = [crossing, crossing, 0, wins - 1] + middle_one + middle_two
    spread = Spread(slot, owners[:, row_block], order)
    cut_one, cut_two = 4 + len(middle_one), len(order)

    heads, tails = [], []
    for r in range(rounds):
        across = ([r + 1] if r + 1 < rounds else []) + ([r] if r == 0 else [])
        if r == 0:
            head = spread.begin(across + [r, r], slice(2 - len(across), 4))
            tail = spread.begin([r] * (cut_two - 4), slice(4, cut_two))
        else:
            head = spread.begin(across + [r] * wins, slice(2 - len(across), cut_one), head[2])
            tail = spread.begin([r] * (cut_two - cut_one), slice(cut_one, cut_two), tail[2])
        head, tail = spread.middle(head), spread.middle(tail)
        heads.append(spread.last(head))
        tails.append(spread.last(tail))

    matrix = slab
    crosses, above_crosses = {}, {}
    for r in range(rounds):
        head, tail = heads[r], tails[r]
        edges = spread.join(*head)
        across = ([r + 1] if r + 1 < rounds else []) + ([r] if r == 0 else [])
        if across:
            n = len(across)
            from_above = spread.join_above(head[0][:n, :, border:], head[1][:n, :, border:])
            for k, q in enumerate(across):
                crosses[q], above_crosses[q] = edges[k], from_above[k]
            edges = edges[n:]
        prev, cross = above_crosses[r], crosses[r]
        outer = apply_many(
            edges[:2], jnp.stack([matrix[:window], matrix[local_rows - window :]])
        )
        head_rows, tail_rows = outer[0], outer[1]
        begin, end = head_rows[:border], tail_rows[border:]
        above, below = swap_rows(begin, end)
        rest = spread.join(*tail)
        if r == 0:
            ones, twos = rest[: wins - 2], rest[wins - 2 :]
        else:
            ones, twos = edges[2:], rest
        mid = apply_many(
            ones,
            matrix[window : local_rows - window].reshape(wins - 2, window, local_cols),
        ).reshape(local_rows - 2 * window, local_cols)
        centre = jnp.concatenate([head_rows[border:], mid, tail_rows[:border]], 0)
        inner = apply_many(twos, centre.reshape(wins - 1, window, local_cols)).reshape(
            local_rows - window, local_cols
        )
        low = apply(cross[:, :border], jnp.concatenate([end, below], 0))
        low = jnp.where(row_block == last_block, end, low)
        top = apply(prev, jnp.concatenate([above, begin], 0))
        top = jnp.where(row_block == 0, begin, top)
        if r < rounds - 1:
            matrix = jnp.concatenate([top, inner, low], 0)
    return write_outer(write_inner(inner, border), top, low)


def solution(mesh):
    return jax.shard_map(
        local,
        mesh=mesh,
        in_specs=(P("rows", "cols"), P("cols", "rows", None), P()),
        out_specs=P("rows", "cols"),
        check_vma=False,
    )
```

```python
import jax
import jax.numpy as jnp
from jax import lax
from jax.experimental import pallas as pl
from jax.experimental.pallas import tpu as pltpu
from jax.sharding import PartitionSpec as P


def shifted(value, axis, steps):
    count = lax.axis_size(axis)
    initial, last = (max(0, -steps), min(count, count - steps))
    return lax.ppermute(value, axis, [(source, source + steps) for source in range(initial, last)])


def swap_rows(up, down):
    count = lax.axis_size("rows")
    even = (lax.axis_index("rows") & 1) == 0

    def swap(value, start):
        pairs = [(low, low + 1) for low in range(start, count - 1, 2)]
        return lax.ppermute(value, "rows", pairs + [(b, a) for a, b in pairs])

    first = swap(jnp.where(even, down, up), 0)
    second = swap(jnp.where(even, up, down), 1)
    return jnp.where(even, second, first), jnp.where(even, first, second)


def flip(value, bits):
    count = lax.axis_size("cols")
    return lax.ppermute(value, "cols", [(d, d ^ (1 << bits[d & 1])) for d in range(count)])


def copy_all(copies):
    for copy in copies:
        copy.start()
    for copy in copies:
        copy.wait()


def small(flops=0, bytes_accessed=0, limit=1 << 20):
    return dict(
        compiler_params=pltpu.CompilerParams(vmem_limit_bytes=limit),
        cost_estimate=pl.CostEstimate(
            flops=flops, bytes_accessed=bytes_accessed, transcendentals=0
        ),
    )


ANY = pl.BlockSpec(memory_space=pl.ANY)


def after(value, *done):
    def kernel(source, *refs):
        copy_all([pltpu.make_async_copy(source, refs[-2], refs[-1])])

    return pl.pallas_call(
        kernel,
        out_shape=jax.ShapeDtypeStruct(value.shape, value.dtype),
        in_specs=[ANY] * (1 + len(done)),
        out_specs=ANY,
        scratch_shapes=[pltpu.SemaphoreType.DMA],
        name="after",
        **small(bytes_accessed=4 * value.size),
    )(value, *done)


def runs(ms):
    found = []
    for at, m in enumerate(ms):
        if found and found[-1][0] + found[-1][2] == m:
            found[-1][2] += 1
        else:
            found.append([m, at, 1])
    return found


def cut_slot(cut, order, kinds, slot):
    _, _, _, rows, width = slot.shape
    shapes = [jax.ShapeDtypeStruct((len(order), rows, width), slot.dtype) for _ in kinds]
    spans = runs(order)

    def kernel(source, *refs):
        outs, sems = refs[:-1], refs[-1]
        me = lax.axis_index("cols")
        core = me & 1
        bit0 = (me >> cut[0]) & 1
        bit1 = (me >> cut[1]) & 1
        mine = jnp.where(core == 0, bit0, bit1)
        other = jnp.where(core == 0, bit1, bit0)
        copies = []
        for (own, hold), out in zip(kinds, outs):
            half = core if own else 1 - core
            piece = mine if own else other
            piece = piece if hold else 1 - piece
            for first, at, n in spans:
                copies.append(
                    pltpu.make_async_copy(
                        source.at[pl.ds(first, n), half, piece],
                        out.at[pl.ds(at, n)],
                        sems.at[len(copies)],
                    )
                )
        copy_all(copies)

    return pl.pallas_call(
        kernel,
        out_shape=shapes,
        in_specs=[pl.BlockSpec(memory_space=pltpu.HBM)],
        out_specs=[ANY] * len(shapes),
        scratch_shapes=[pltpu.SemaphoreType.DMA((len(spans) * len(kinds),))],
        name="cut_slot",
        **small(bytes_accessed=len(kinds) * slot.size, limit=(48 if len(kinds) == 1 else 1) << 20),
    )(slot)


def place_kernel(cut, hold, got, other_hold, other_got, out, sems):
    me = lax.axis_index("cols")
    core = me & 1
    rows = hold.shape[1]
    bit0 = (me >> cut[0]) & 1
    bit1 = (me >> cut[1]) & 1
    mine = jnp.where(core == 0, bit0, bit1)
    other = jnp.where(core == 0, bit1, bit0)
    slots = (
        (hold, core * 2 + mine),
        (got, core * 2 + 1 - mine),
        (other_hold, (1 - core) * 2 + other),
        (other_got, (1 - core) * 2 + 1 - other),
    )
    copies = [
        pltpu.make_async_copy(
            piece, out.at[:, pl.ds(pl.multiple_of(at * rows, rows), rows), :], sems.at[k]
        )
        for k, (piece, at) in enumerate(slots)
    ]
    copy_all(copies)


def place(cut, hold, got, other_hold, other_got):
    n, rows, width = hold.shape
    return pl.pallas_call(
        lambda *refs: place_kernel(cut, *refs),
        out_shape=jax.ShapeDtypeStruct((n, 4 * rows, width), hold.dtype),
        in_specs=[ANY] * 4,
        out_specs=ANY,
        scratch_shapes=[pltpu.SemaphoreType.DMA((4,))],
        name="place",
        **small(bytes_accessed=2 * n * 4 * rows * width * 2),
    )(hold, got, other_hold, other_got)


class Spread:
    def __init__(self, slot, owners_here, order):
        count = lax.axis_size("cols")
        dims = count.bit_length() - 2
        self.me = lax.axis_index("cols")
        self.core = self.me & 1
        self.owners = owners_here
        self.cut = (1, dims)
        self.others = [(b, b - 1) for b in range(2, dims + 1)]
        (give_out,) = cut_slot(self.cut, order, [(False, False)], slot)
        own_out, give_hold, own_hold = cut_slot(
            self.cut, order, [(True, False), (False, True), (True, True)], slot
        )
        self.own = own_out, own_hold
        self.theirs = flip(give_out, (0, 0)), flip(give_hold, (0, 0))

    def bit(self, index, bits):
        return (index >> jnp.where(self.core == 0, bits[0], bits[1])) & 1

    def choose(self, rounds, test, yes, no):
        holds = [test(self.owners[r]) for r in rounds]
        mask = holds[0]
        for at in range(1, len(rounds)):
            if rounds[at] != rounds[at - 1]:
                row = lax.broadcasted_iota(jnp.int32, yes.shape, 0)
                mask = jnp.where(row < at, mask, holds[at])
        return jnp.where(mask, yes, no)

    def begin(self, rounds, rows, *first):
        out, hold = [
            self.choose(rounds, lambda owner: (owner & 1) == self.core, own[rows], theirs[rows])
            for own, theirs in zip(self.own, self.theirs)
        ]
        if first:
            out = after(out, *first)
        return rounds, hold, flip(out, self.cut)

    def keep(self, state, bits):
        rounds, hold, got = state
        mine = self.bit(self.me, bits)
        return self.choose(rounds, lambda owner: mine == self.bit(owner, bits), hold, got)

    def middle(self, state, *first):
        bits = self.cut
        for other in self.others:
            hold = self.keep(state, bits)
            if first:
                hold = after(hold, *first)
                first = ()
            state = (state[0], hold, flip(hold, other))
            bits = other
        return state

    def last(self, state, *first):
        hold = self.keep(state, self.others[-1])
        if first:
            hold = after(hold, *first)
        return hold, flip(hold, self.cut)

    def swap(self, pair):
        return (*pair, *[flip(piece, (0, 0)) for piece in pair])

    def join(self, pieces):
        return place(self.cut, *pieces)

    def join_above(self, hold, got):
        both = shifted(jnp.stack([hold, got]), "rows", 1)
        other = flip(both, (0, 0))
        return place(self.cut, both[0], both[1], other[0], other[1])


def apply(q, x):
    product = lax.dot_general(q, x, (((0,), (0,)), ((), ())), preferred_element_type=jnp.float32)
    return product.astype(jnp.bfloat16)


def apply_many(q, x):
    product = jnp.einsum("nab,nac->nbc", q, x, preferred_element_type=jnp.float32)
    return product.astype(jnp.bfloat16)


def write_inner(inner, border):
    rows, cols = inner.shape

    def kernel(source, out):
        out[...] = source[...]

    return pl.pallas_call(
        kernel,
        grid=(rows // border,),
        out_shape=jax.ShapeDtypeStruct((rows + 2 * border, cols), inner.dtype),
        in_specs=[pl.BlockSpec((border, cols), lambda i: (i, 0))],
        out_specs=pl.BlockSpec((border, cols), lambda i: (i + 1, 0)),
        compiler_params=pltpu.CompilerParams(vmem_limit_bytes=8 << 20),
        cost_estimate=pl.CostEstimate(flops=0, bytes_accessed=4 * inner.size, transcendentals=0),
        name="write_inner",
    )(inner)


def write_outer(whole, top, low):
    border, cols = top.shape
    last = whole.shape[0] // border - 1

    def kernel(_, first, final, out):
        @pl.when(pl.program_id(0) == 0)
        def _():
            out[...] = first[...]

        @pl.when(pl.program_id(0) == 1)
        def _():
            out[...] = final[...]

    block = pl.BlockSpec((border, cols), lambda i: (0, 0))
    return pl.pallas_call(
        kernel,
        grid=(2,),
        out_shape=jax.ShapeDtypeStruct(whole.shape, whole.dtype),
        in_specs=[ANY, block, block],
        out_specs=pl.BlockSpec((border, cols), lambda i: (i * last, 0)),
        input_output_aliases={0: 0},
        compiler_params=pltpu.CompilerParams(vmem_limit_bytes=8 << 20),
        cost_estimate=pl.CostEstimate(flops=0, bytes_accessed=8 * top.size, transcendentals=0),
        name="write_outer",
    )(whole, top, low)


def local(slab, transforms, owners):
    row_block = lax.axis_index("rows")
    last_block = lax.axis_size("rows") - 1
    window = transforms.shape[2]
    border = window // 2
    local_rows, local_cols = slab.shape
    wins = local_rows // window
    rounds = owners.shape[0]
    slot = transforms[0].reshape(2 * wins, 2, 2, window // 4, window)
    crossing = 2 * wins - 1
    middle_one, middle_two = list(range(1, wins - 1)), list(range(wins, crossing))
    order = [crossing, crossing, 0, wins - 1] + middle_one + middle_two
    spread = Spread(slot, owners[:, row_block], order)
    cut_one, cut_two = 4 + len(middle_one), len(order)

    heads, tails = [], []
    for r in range(rounds):
        across = ([r + 1] if r + 1 < rounds else []) + ([r] if r == 0 else [])
        if r == 0:
            head = spread.begin(across + [r, r], slice(2 - len(across), 4))
            tail = spread.begin([r] * (cut_two - 4), slice(4, cut_two))
        else:
            head = spread.begin(across + [r] * wins, slice(2 - len(across), cut_one), head[2])
            tail = spread.begin([r] * (cut_two - cut_one), slice(cut_one, cut_two), tail[2])
        head = spread.middle(head, *([] if r == 0 else [heads[r - 1][3]]))
        tail = spread.middle(tail)
        heads.append(spread.swap(spread.last(head)))
        tails.append(spread.swap(spread.last(tail)))

    matrix = slab
    crosses, above_crosses = {}, {}
    for r in range(rounds):
        head, tail = heads[r], tails[r]
        edges = spread.join(head)
        across = ([r + 1] if r + 1 < rounds else []) + ([r] if r == 0 else [])
        if across:
            n = len(across)
            from_above = spread.join_above(head[0][:n, :, border:], head[1][:n, :, border:])
            for k, q in enumerate(across):
                crosses[q], above_crosses[q] = edges[k], from_above[k]
            edges = edges[n:]
        prev, cross = above_crosses[r], crosses[r]
        outer = apply_many(
            edges[:2], jnp.stack([matrix[:window], matrix[local_rows - window :]])
        )
        head_rows, tail_rows = outer[0], outer[1]
        begin, end = head_rows[:border], tail_rows[border:]
        above, below = swap_rows(begin, end)
        rest = spread.join(tail)
        if r == 0:
            ones, twos = rest[: wins - 2], rest[wins - 2 :]
        else:
            ones, twos = edges[2:], rest
        mid = apply_many(
            ones,
            matrix[window : local_rows - window].reshape(wins - 2, window, local_cols),
        ).reshape(local_rows - 2 * window, local_cols)
        centre = jnp.concatenate([head_rows[border:], mid, tail_rows[:border]], 0)
        inner = apply_many(twos, centre.reshape(wins - 1, window, local_cols)).reshape(
            local_rows - window, local_cols
        )
        low = apply(cross[:, :border], jnp.concatenate([end, below], 0))
        low = jnp.where(row_block == last_block, end, low)
        top = apply(prev, jnp.concatenate([above, begin], 0))
        top = jnp.where(row_block == 0, begin, top)
        if r < rounds - 1:
            matrix = jnp.concatenate([top, inner, low], 0)
    return write_outer(write_inner(inner, border), top, low)


def solution(mesh):
    return jax.shard_map(
        local,
        mesh=mesh,
        in_specs=(P("rows", "cols"), P("cols", "rows", None), P()),
        out_specs=P("rows", "cols"),
        check_vma=False,
    )
```

```python
import jax
import jax.numpy as jnp
from jax import lax
from jax.experimental import pallas as pl
from jax.experimental.pallas import tpu as pltpu
from jax.sharding import PartitionSpec as P


def shifted(value, axis, steps):
    count = lax.axis_size(axis)
    initial, last = (max(0, -steps), min(count, count - steps))
    return lax.ppermute(value, axis, [(source, source + steps) for source in range(initial, last)])


def swap_rows(up, down):
    count = lax.axis_size("rows")
    even = (lax.axis_index("rows") & 1) == 0

    def swap(value, start):
        pairs = [(low, low + 1) for low in range(start, count - 1, 2)]
        return lax.ppermute(value, "rows", pairs + [(b, a) for a, b in pairs])

    first = swap(jnp.where(even, down, up), 0)
    second = swap(jnp.where(even, up, down), 1)
    return jnp.where(even, second, first), jnp.where(even, first, second)


def flip(value, bits):
    count = lax.axis_size("cols")
    return lax.ppermute(value, "cols", [(d, d ^ (1 << bits[d & 1])) for d in range(count)])


def copy_all(copies):
    for copy in copies:
        copy.start()
    for copy in copies:
        copy.wait()


def small(flops=0, bytes_accessed=0, limit=1 << 20):
    return dict(
        compiler_params=pltpu.CompilerParams(vmem_limit_bytes=limit),
        cost_estimate=pl.CostEstimate(
            flops=flops, bytes_accessed=bytes_accessed, transcendentals=0
        ),
    )


ANY = pl.BlockSpec(memory_space=pl.ANY)


def after(value, *done):
    def kernel(source, *refs):
        copy_all([pltpu.make_async_copy(source, refs[-2], refs[-1])])

    return pl.pallas_call(
        kernel,
        out_shape=jax.ShapeDtypeStruct(value.shape, value.dtype),
        in_specs=[ANY] * (1 + len(done)),
        out_specs=ANY,
        scratch_shapes=[pltpu.SemaphoreType.DMA],
        name="after",
        **small(bytes_accessed=4 * value.size),
    )(value, *done)


def runs(ms):
    found = []
    for at, m in enumerate(ms):
        if found and found[-1][0] + found[-1][2] == m:
            found[-1][2] += 1
        else:
            found.append([m, at, 1])
    return found


def cut_slot(cut, order, kinds, slot):
    _, _, _, rows, width = slot.shape
    shapes = [jax.ShapeDtypeStruct((len(order), rows, width), slot.dtype) for _ in kinds]
    spans = runs(order)

    def kernel(source, *refs):
        outs, sems = refs[:-1], refs[-1]
        me = lax.axis_index("cols")
        core = me & 1
        bit0 = (me >> cut[0]) & 1
        bit1 = (me >> cut[1]) & 1
        mine = jnp.where(core == 0, bit0, bit1)
        other = jnp.where(core == 0, bit1, bit0)
        copies = []
        for (own, hold), out in zip(kinds, outs):
            half = core if own else 1 - core
            piece = mine if own else other
            piece = piece if hold else 1 - piece
            for first, at, n in spans:
                copies.append(
                    pltpu.make_async_copy(
                        source.at[pl.ds(first, n), half, piece],
                        out.at[pl.ds(at, n)],
                        sems.at[len(copies)],
                    )
                )
        copy_all(copies)

    return pl.pallas_call(
        kernel,
        out_shape=shapes,
        in_specs=[pl.BlockSpec(memory_space=pltpu.HBM)],
        out_specs=[ANY] * len(shapes),
        scratch_shapes=[pltpu.SemaphoreType.DMA((len(spans) * len(kinds),))],
        name="cut_slot",
        **small(bytes_accessed=len(kinds) * slot.size, limit=(48 if len(kinds) == 1 else 1) << 20),
    )(slot)


def place_kernel(cut, hold, got, other_hold, other_got, out, sems):
    me = lax.axis_index("cols")
    core = me & 1
    rows = hold.shape[1]
    bit0 = (me >> cut[0]) & 1
    bit1 = (me >> cut[1]) & 1
    mine = jnp.where(core == 0, bit0, bit1)
    other = jnp.where(core == 0, bit1, bit0)
    slots = (
        (hold, core * 2 + mine),
        (got, core * 2 + 1 - mine),
        (other_hold, (1 - core) * 2 + other),
        (other_got, (1 - core) * 2 + 1 - other),
    )
    copies = [
        pltpu.make_async_copy(
            piece, out.at[:, pl.ds(pl.multiple_of(at * rows, rows), rows), :], sems.at[k]
        )
        for k, (piece, at) in enumerate(slots)
    ]
    copy_all(copies)


def place(cut, hold, got, other_hold, other_got):
    n, rows, width = hold.shape
    return pl.pallas_call(
        lambda *refs: place_kernel(cut, *refs),
        out_shape=jax.ShapeDtypeStruct((n, 4 * rows, width), hold.dtype),
        in_specs=[ANY] * 4,
        out_specs=ANY,
        scratch_shapes=[pltpu.SemaphoreType.DMA((4,))],
        name="place",
        **small(bytes_accessed=2 * n * 4 * rows * width * 2),
    )(hold, got, other_hold, other_got)


class Spread:
    def __init__(self, slot, owners_here, order):
        count = lax.axis_size("cols")
        dims = count.bit_length() - 2
        self.me = lax.axis_index("cols")
        self.core = self.me & 1
        self.owners = owners_here
        self.cut = (1, dims)
        self.others = [(b, b - 1) for b in range(2, dims + 1)]
        (give_out,) = cut_slot(self.cut, order, [(False, False)], slot)
        own_out, give_hold, own_hold = cut_slot(
            self.cut, order, [(True, False), (False, True), (True, True)], slot
        )
        self.own = own_out, own_hold
        self.theirs = flip(give_out, (0, 0)), flip(give_hold, (0, 0))

    def bit(self, index, bits):
        return (index >> jnp.where(self.core == 0, bits[0], bits[1])) & 1

    def choose(self, rounds, test, yes, no):
        holds = [test(self.owners[r]) for r in rounds]
        mask = holds[0]
        for at in range(1, len(rounds)):
            if rounds[at] != rounds[at - 1]:
                row = lax.broadcasted_iota(jnp.int32, yes.shape, 0)
                mask = jnp.where(row < at, mask, holds[at])
        return jnp.where(mask, yes, no)

    def begin(self, rounds, rows, *first):
        out, hold = [
            self.choose(rounds, lambda owner: (owner & 1) == self.core, own[rows], theirs[rows])
            for own, theirs in zip(self.own, self.theirs)
        ]
        if first:
            out = after(out, *first)
        return rounds, hold, flip(out, self.cut)

    def keep(self, state, bits):
        rounds, hold, got = state
        mine = self.bit(self.me, bits)
        return self.choose(rounds, lambda owner: mine == self.bit(owner, bits), hold, got)

    def middle(self, state, *first):
        bits = self.cut
        for other in self.others:
            hold = self.keep(state, bits)
            if first:
                hold = after(hold, *first)
                first = ()
            state = (state[0], hold, flip(hold, other))
            bits = other
        return state

    def last(self, state, *first):
        hold = self.keep(state, self.others[-1])
        if first:
            hold = after(hold, *first)
        return hold, flip(hold, self.cut)

    def join(self, hold, got):
        return place(self.cut, hold, got, flip(hold, (0, 0)), flip(got, (0, 0)))

    def join_above(self, hold, got):
        both = shifted(jnp.stack([hold, got]), "rows", 1)
        other = flip(both, (0, 0))
        return place(self.cut, both[0], both[1], other[0], other[1])


def apply(q, x):
    product = lax.dot_general(q, x, (((0,), (0,)), ((), ())), preferred_element_type=jnp.float32)
    return product.astype(jnp.bfloat16)


def apply_many(q, x):
    product = jnp.einsum("nab,nac->nbc", q, x, preferred_element_type=jnp.float32)
    return product.astype(jnp.bfloat16)


def write_inner(inner, border):
    rows, cols = inner.shape

    def kernel(source, out):
        out[...] = source[...]

    return pl.pallas_call(
        kernel,
        grid=(rows // border,),
        out_shape=jax.ShapeDtypeStruct((rows + 2 * border, cols), inner.dtype),
        in_specs=[pl.BlockSpec((border, cols), lambda i: (i, 0))],
        out_specs=pl.BlockSpec((border, cols), lambda i: (i + 1, 0)),
        compiler_params=pltpu.CompilerParams(vmem_limit_bytes=8 << 20),
        cost_estimate=pl.CostEstimate(flops=0, bytes_accessed=4 * inner.size, transcendentals=0),
        name="write_inner",
    )(inner)


def write_outer(whole, top, low):
    border, cols = top.shape
    last = whole.shape[0] // border - 1

    def kernel(_, first, final, out):
        @pl.when(pl.program_id(0) == 0)
        def _():
            out[...] = first[...]

        @pl.when(pl.program_id(0) == 1)
        def _():
            out[...] = final[...]

    block = pl.BlockSpec((border, cols), lambda i: (0, 0))
    return pl.pallas_call(
        kernel,
        grid=(2,),
        out_shape=jax.ShapeDtypeStruct(whole.shape, whole.dtype),
        in_specs=[ANY, block, block],
        out_specs=pl.BlockSpec((border, cols), lambda i: (i * last, 0)),
        input_output_aliases={0: 0},
        compiler_params=pltpu.CompilerParams(vmem_limit_bytes=8 << 20),
        cost_estimate=pl.CostEstimate(flops=0, bytes_accessed=8 * top.size, transcendentals=0),
        name="write_outer",
    )(whole, top, low)


def local(slab, transforms, owners):
    row_block = lax.axis_index("rows")
    last_block = lax.axis_size("rows") - 1
    window = transforms.shape[2]
    border = window // 2
    local_rows, local_cols = slab.shape
    wins = local_rows // window
    rounds = owners.shape[0]
    slot = transforms[0].reshape(2 * wins, 2, 2, window // 4, window)
    crossing = 2 * wins - 1
    middle_one, middle_two = list(range(1, wins - 1)), list(range(wins, crossing))
    order = [crossing, crossing, 0, wins - 1] + middle_one + middle_two
    spread = Spread(slot, owners[:, row_block], order)
    streams = []
    for r in range(rounds):
        across = ([r + 1] if r + 1 < rounds else []) + ([r] if r == 0 else [])
        first = 2 - len(across)
        if r == 0:
            streams.append(spread.middle(spread.begin(across + [r, r], slice(first, 4))))
            streams.append(spread.middle(spread.begin([r] * (len(order) - 4), slice(4, len(order)))))
        else:
            begun = spread.begin(across + [r] * crossing, slice(first, len(order)), streams[r - 1][2])
            streams.append(spread.middle(begun))
    pairs = [spread.last(stream) for stream in streams]

    matrix = slab
    crosses, above_crosses = {}, {}
    for r in range(rounds):
        head = pairs[0] if r == 0 else pairs[r + 1]
        edges = spread.join(*head)
        across = ([r + 1] if r + 1 < rounds else []) + ([r] if r == 0 else [])
        if across:
            n = len(across)
            from_above = spread.join_above(head[0][:n, :, border:], head[1][:n, :, border:])
            for k, q in enumerate(across):
                crosses[q], above_crosses[q] = edges[k], from_above[k]
            edges = edges[n:]
        prev, cross = above_crosses[r], crosses[r]
        outer = apply_many(
            edges[:2], jnp.stack([matrix[:window], matrix[local_rows - window :]])
        )
        head_rows, tail_rows = outer[0], outer[1]
        begin, end = head_rows[:border], tail_rows[border:]
        above, below = swap_rows(begin, end)
        rest = spread.join(*pairs[1]) if r == 0 else edges[2:]
        ones, twos = rest[: wins - 2], rest[wins - 2 :]
        mid = apply_many(
            ones,
            matrix[window : local_rows - window].reshape(wins - 2, window, local_cols),
        ).reshape(local_rows - 2 * window, local_cols)
        centre = jnp.concatenate([head_rows[border:], mid, tail_rows[:border]], 0)
        inner = apply_many(twos, centre.reshape(wins - 1, window, local_cols)).reshape(
            local_rows - window, local_cols
        )
        low = apply(cross[:, :border], jnp.concatenate([end, below], 0))
        low = jnp.where(row_block == last_block, end, low)
        top = apply(prev, jnp.concatenate([above, begin], 0))
        top = jnp.where(row_block == 0, begin, top)
        if r < rounds - 1:
            matrix = jnp.concatenate([top, inner, low], 0)
    return write_outer(write_inner(inner, border), top, low)


def solution(mesh):
    return jax.shard_map(
        local,
        mesh=mesh,
        in_specs=(P("rows", "cols"), P("cols", "rows", None), P()),
        out_specs=P("rows", "cols"),
        check_vma=False,
    )
```

```python
import jax
import jax.numpy as jnp
from jax import lax
from jax.experimental import pallas as pl
from jax.experimental.pallas import tpu as pltpu
from jax.sharding import PartitionSpec as P


def shifted(value, axis, steps):
    count = lax.axis_size(axis)
    initial, last = (max(0, -steps), min(count, count - steps))
    return lax.ppermute(value, axis, [(source, source + steps) for source in range(initial, last)])


def swap_rows(up, down):
    count = lax.axis_size("rows")
    even = (lax.axis_index("rows") & 1) == 0

    def swap(value, start):
        pairs = [(low, low + 1) for low in range(start, count - 1, 2)]
        return lax.ppermute(value, "rows", pairs + [(b, a) for a, b in pairs])

    first = swap(jnp.where(even, down, up), 0)
    second = swap(jnp.where(even, up, down), 1)
    return jnp.where(even, second, first), jnp.where(even, first, second)


def flip(value, bits):
    count = lax.axis_size("cols")
    return lax.ppermute(value, "cols", [(d, d ^ (1 << bits[d & 1])) for d in range(count)])


def copy_all(copies):
    for copy in copies:
        copy.start()
    for copy in copies:
        copy.wait()


def small(flops=0, bytes_accessed=0, limit=1 << 20):
    return dict(
        compiler_params=pltpu.CompilerParams(vmem_limit_bytes=limit),
        cost_estimate=pl.CostEstimate(
            flops=flops, bytes_accessed=bytes_accessed, transcendentals=0
        ),
    )


ANY = pl.BlockSpec(memory_space=pl.ANY)


def after(value, *done):
    def kernel(source, *refs):
        copy_all([pltpu.make_async_copy(source, refs[-2], refs[-1])])

    return pl.pallas_call(
        kernel,
        out_shape=jax.ShapeDtypeStruct(value.shape, value.dtype),
        in_specs=[ANY] * (1 + len(done)),
        out_specs=ANY,
        scratch_shapes=[pltpu.SemaphoreType.DMA],
        name="after",
        **small(bytes_accessed=4 * value.size),
    )(value, *done)


def runs(ms):
    found = []
    for at, m in enumerate(ms):
        if found and found[-1][0] + found[-1][2] == m:
            found[-1][2] += 1
        else:
            found.append([m, at, 1])
    return found


def cut_slot(cut, order, kinds, slot):
    _, _, _, rows, width = slot.shape
    shapes = [jax.ShapeDtypeStruct((len(order), rows, width), slot.dtype) for _ in kinds]
    spans = runs(order)

    def kernel(source, *refs):
        outs, sems = refs[:-1], refs[-1]
        me = lax.axis_index("cols")
        core = me & 1
        bit0 = (me >> cut[0]) & 1
        bit1 = (me >> cut[1]) & 1
        mine = jnp.where(core == 0, bit0, bit1)
        other = jnp.where(core == 0, bit1, bit0)
        copies = []
        for (own, hold), out in zip(kinds, outs):
            half = core if own else 1 - core
            piece = mine if own else other
            piece = piece if hold else 1 - piece
            for first, at, n in spans:
                copies.append(
                    pltpu.make_async_copy(
                        source.at[pl.ds(first, n), half, piece],
                        out.at[pl.ds(at, n)],
                        sems.at[len(copies)],
                    )
                )
        copy_all(copies)

    return pl.pallas_call(
        kernel,
        out_shape=shapes,
        in_specs=[pl.BlockSpec(memory_space=pltpu.HBM)],
        out_specs=[ANY] * len(shapes),
        scratch_shapes=[pltpu.SemaphoreType.DMA((len(spans) * len(kinds),))],
        name="cut_slot",
        **small(bytes_accessed=len(kinds) * slot.size, limit=(48 if len(kinds) == 1 else 1) << 20),
    )(slot)


def place_kernel(cut, hold, got, other_hold, other_got, out, sems):
    me = lax.axis_index("cols")
    core = me & 1
    rows = hold.shape[1]
    bit0 = (me >> cut[0]) & 1
    bit1 = (me >> cut[1]) & 1
    mine = jnp.where(core == 0, bit0, bit1)
    other = jnp.where(core == 0, bit1, bit0)
    slots = (
        (hold, core * 2 + mine),
        (got, core * 2 + 1 - mine),
        (other_hold, (1 - core) * 2 + other),
        (other_got, (1 - core) * 2 + 1 - other),
    )
    copies = [
        pltpu.make_async_copy(
            piece, out.at[:, pl.ds(pl.multiple_of(at * rows, rows), rows), :], sems.at[k]
        )
        for k, (piece, at) in enumerate(slots)
    ]
    copy_all(copies)


def place(cut, hold, got, other_hold, other_got):
    n, rows, width = hold.shape
    return pl.pallas_call(
        lambda *refs: place_kernel(cut, *refs),
        out_shape=jax.ShapeDtypeStruct((n, 4 * rows, width), hold.dtype),
        in_specs=[ANY] * 4,
        out_specs=ANY,
        scratch_shapes=[pltpu.SemaphoreType.DMA((4,))],
        name="place",
        **small(bytes_accessed=2 * n * 4 * rows * width * 2),
    )(hold, got, other_hold, other_got)


class Spread:
    def __init__(self, slot, owners_here, order):
        count = lax.axis_size("cols")
        dims = count.bit_length() - 2
        self.me = lax.axis_index("cols")
        self.core = self.me & 1
        self.owners = owners_here
        self.cut = (1, dims)
        self.others = [(b, b - 1) for b in range(2, dims + 1)]
        (give_out,) = cut_slot(self.cut, order, [(False, False)], slot)
        own_out, give_hold, own_hold = cut_slot(
            self.cut, order, [(True, False), (False, True), (True, True)], slot
        )
        self.own = own_out, own_hold
        self.theirs = flip(give_out, (0, 0)), flip(give_hold, (0, 0))

    def bit(self, index, bits):
        return (index >> jnp.where(self.core == 0, bits[0], bits[1])) & 1

    def choose(self, rounds, test, yes, no):
        holds = [test(self.owners[r]) for r in rounds]
        mask = holds[0]
        for at in range(1, len(rounds)):
            if rounds[at] != rounds[at - 1]:
                row = lax.broadcasted_iota(jnp.int32, yes.shape, 0)
                mask = jnp.where(row < at, mask, holds[at])
        return jnp.where(mask, yes, no)

    def begin(self, rounds, rows, *first):
        out, hold = [
            self.choose(rounds, lambda owner: (owner & 1) == self.core, own[rows], theirs[rows])
            for own, theirs in zip(self.own, self.theirs)
        ]
        if first:
            out = after(out, *first)
        return rounds, hold, flip(out, self.cut)

    def keep(self, state, bits):
        rounds, hold, got = state
        mine = self.bit(self.me, bits)
        return self.choose(rounds, lambda owner: mine == self.bit(owner, bits), hold, got)

    def middle(self, state, *first):
        bits = self.cut
        for other in self.others:
            hold = self.keep(state, bits)
            if first:
                hold = after(hold, *first)
                first = ()
            state = (state[0], hold, flip(hold, other))
            bits = other
        return state

    def last(self, state, *first):
        hold = self.keep(state, self.others[-1])
        if first:
            hold = after(hold, *first)
        return hold, flip(hold, self.cut)

    def join(self, hold, got):
        return place(self.cut, hold, got, flip(hold, (0, 0)), flip(got, (0, 0)))

    def join_above(self, hold, got, *later):
        both = jnp.stack([hold, got])
        both = shifted(after(both, *later) if later else both, "rows", 1)
        other = flip(both, (0, 0))
        return place(self.cut, both[0], both[1], other[0], other[1])


def apply(q, x):
    product = lax.dot_general(q, x, (((0,), (0,)), ((), ())), preferred_element_type=jnp.float32)
    return product.astype(jnp.bfloat16)


def apply_many(q, x):
    product = jnp.einsum("nab,nac->nbc", q, x, preferred_element_type=jnp.float32)
    return product.astype(jnp.bfloat16)


def write_inner(inner, border):
    rows, cols = inner.shape

    def kernel(source, out):
        out[...] = source[...]

    return pl.pallas_call(
        kernel,
        grid=(rows // border,),
        out_shape=jax.ShapeDtypeStruct((rows + 2 * border, cols), inner.dtype),
        in_specs=[pl.BlockSpec((border, cols), lambda i: (i, 0))],
        out_specs=pl.BlockSpec((border, cols), lambda i: (i + 1, 0)),
        compiler_params=pltpu.CompilerParams(vmem_limit_bytes=8 << 20),
        cost_estimate=pl.CostEstimate(flops=0, bytes_accessed=4 * inner.size, transcendentals=0),
        name="write_inner",
    )(inner)


def write_outer(whole, top, low):
    border, cols = top.shape
    last = whole.shape[0] // border - 1

    def kernel(_, first, final, out):
        @pl.when(pl.program_id(0) == 0)
        def _():
            out[...] = first[...]

        @pl.when(pl.program_id(0) == 1)
        def _():
            out[...] = final[...]

    block = pl.BlockSpec((border, cols), lambda i: (0, 0))
    return pl.pallas_call(
        kernel,
        grid=(2,),
        out_shape=jax.ShapeDtypeStruct(whole.shape, whole.dtype),
        in_specs=[ANY, block, block],
        out_specs=pl.BlockSpec((border, cols), lambda i: (i * last, 0)),
        input_output_aliases={0: 0},
        compiler_params=pltpu.CompilerParams(vmem_limit_bytes=8 << 20),
        cost_estimate=pl.CostEstimate(flops=0, bytes_accessed=8 * top.size, transcendentals=0),
        name="write_outer",
    )(whole, top, low)


def local(slab, transforms, owners):
    row_block = lax.axis_index("rows")
    last_block = lax.axis_size("rows") - 1
    window = transforms.shape[2]
    border = window // 2
    local_rows, local_cols = slab.shape
    wins = local_rows // window
    rounds = owners.shape[0]
    slot = transforms[0].reshape(2 * wins, 2, 2, window // 4, window)
    crossing = 2 * wins - 1
    middle_one, middle_two = list(range(1, wins - 1)), list(range(wins, crossing))
    order = [crossing, crossing, 0, wins - 1] + middle_one + middle_two
    spread = Spread(slot, owners[:, row_block], order)
    streams, opening = [], None
    for r in range(rounds):
        across = ([r + 1] if r + 1 < rounds else []) + ([r] if r == 0 else [])
        first = 2 - len(across)
        if r == 0:
            streams.append(spread.middle(spread.begin(across + [r, r], slice(first, 4))))
            opening = spread.begin([r] * (len(order) - 4), slice(4, len(order)))
            streams.append(spread.middle(opening))
        else:
            begun = spread.begin(across + [r] * crossing, slice(first, len(order)), opening[2])
            streams.append(spread.middle(begun))
            opening = begun
    pairs = [spread.last(stream) for stream in streams]

    matrix = slab
    crosses, above_crosses = {}, {}
    for r in range(rounds):
        head = pairs[0] if r == 0 else pairs[r + 1]
        edges = spread.join(*head)
        across = ([r + 1] if r + 1 < rounds else []) + ([r] if r == 0 else [])
        if across:
            n = len(across)
            later = [streams[r + 2][1]] if r + 2 < len(streams) else []
            from_above = spread.join_above(
                head[0][:n, :, border:], head[1][:n, :, border:], *later
            )
            for k, q in enumerate(across):
                crosses[q], above_crosses[q] = edges[k], from_above[k]
            edges = edges[n:]
        prev, cross = above_crosses[r], crosses[r]
        outer = apply_many(
            edges[:2], jnp.stack([matrix[:window], matrix[local_rows - window :]])
        )
        head_rows, tail_rows = outer[0], outer[1]
        begin, end = head_rows[:border], tail_rows[border:]
        above, below = swap_rows(begin, end)
        rest = spread.join(*pairs[1]) if r == 0 else edges[2:]
        ones, twos = rest[: wins - 2], rest[wins - 2 :]
        mid = apply_many(
            ones,
            matrix[window : local_rows - window].reshape(wins - 2, window, local_cols),
        ).reshape(local_rows - 2 * window, local_cols)
        centre = jnp.concatenate([head_rows[border:], mid, tail_rows[:border]], 0)
        inner = apply_many(twos, centre.reshape(wins - 1, window, local_cols)).reshape(
            local_rows - window, local_cols
        )
        low = apply(cross[:, :border], jnp.concatenate([end, below], 0))
        low = jnp.where(row_block == last_block, end, low)
        top = apply(prev, jnp.concatenate([above, begin], 0))
        top = jnp.where(row_block == 0, begin, top)
        if r < rounds - 1:
            matrix = jnp.concatenate([top, inner, low], 0)
    return write_outer(write_inner(inner, border), top, low)


def solution(mesh):
    return jax.shard_map(
        local,
        mesh=mesh,
        in_specs=(P("rows", "cols"), P("cols", "rows", None), P()),
        out_specs=P("rows", "cols"),
        check_vma=False,
    )
```

```python
import jax
import jax.numpy as jnp
from jax import lax
from jax.experimental import pallas as pl
from jax.experimental.pallas import tpu as pltpu
from jax.sharding import PartitionSpec as P


def shifted(value, axis, steps):
    count = lax.axis_size(axis)
    initial, last = (max(0, -steps), min(count, count - steps))
    return lax.ppermute(value, axis, [(source, source + steps) for source in range(initial, last)])


def swap_rows(up, down):
    count = lax.axis_size("rows")
    even = (lax.axis_index("rows") & 1) == 0

    def swap(value, start):
        pairs = [(low, low + 1) for low in range(start, count - 1, 2)]
        return lax.ppermute(value, "rows", pairs + [(b, a) for a, b in pairs])

    first = swap(jnp.where(even, down, up), 0)
    second = swap(jnp.where(even, up, down), 1)
    return jnp.where(even, second, first), jnp.where(even, first, second)


def flip(value, bits):
    count = lax.axis_size("cols")
    return lax.ppermute(value, "cols", [(d, d ^ (1 << bits[d & 1])) for d in range(count)])


def copy_all(copies):
    for copy in copies:
        copy.start()
    for copy in copies:
        copy.wait()


def small(flops=0, bytes_accessed=0, limit=1 << 20):
    return dict(
        compiler_params=pltpu.CompilerParams(vmem_limit_bytes=limit),
        cost_estimate=pl.CostEstimate(
            flops=flops, bytes_accessed=bytes_accessed, transcendentals=0
        ),
    )


ANY = pl.BlockSpec(memory_space=pl.ANY)


def after(value, *done):
    def kernel(source, *refs):
        copy_all([pltpu.make_async_copy(source, refs[-2], refs[-1])])

    return pl.pallas_call(
        kernel,
        out_shape=jax.ShapeDtypeStruct(value.shape, value.dtype),
        in_specs=[ANY] * (1 + len(done)),
        out_specs=ANY,
        scratch_shapes=[pltpu.SemaphoreType.DMA],
        name="after",
        **small(bytes_accessed=4 * value.size),
    )(value, *done)


def runs(ms):
    found = []
    for at, m in enumerate(ms):
        if found and found[-1][0] + found[-1][2] == m:
            found[-1][2] += 1
        else:
            found.append([m, at, 1])
    return found


def cut_slot(cut, order, kinds, slot):
    _, _, _, rows, width = slot.shape
    shapes = [jax.ShapeDtypeStruct((len(order), rows, width), slot.dtype) for _ in kinds]
    spans = runs(order)

    def kernel(source, *refs):
        outs, sems = refs[:-1], refs[-1]
        me = lax.axis_index("cols")
        core = me & 1
        bit0 = (me >> cut[0]) & 1
        bit1 = (me >> cut[1]) & 1
        mine = jnp.where(core == 0, bit0, bit1)
        other = jnp.where(core == 0, bit1, bit0)
        copies = []
        for (own, hold), out in zip(kinds, outs):
            half = core if own else 1 - core
            piece = mine if own else other
            piece = piece if hold else 1 - piece
            for first, at, n in spans:
                copies.append(
                    pltpu.make_async_copy(
                        source.at[pl.ds(first, n), half, piece],
                        out.at[pl.ds(at, n)],
                        sems.at[len(copies)],
                    )
                )
        copy_all(copies)

    return pl.pallas_call(
        kernel,
        out_shape=shapes,
        in_specs=[pl.BlockSpec(memory_space=pltpu.HBM)],
        out_specs=[ANY] * len(shapes),
        scratch_shapes=[pltpu.SemaphoreType.DMA((len(spans) * len(kinds),))],
        name="cut_slot",
        **small(bytes_accessed=len(kinds) * slot.size, limit=(48 if len(kinds) == 1 else 1) << 20),
    )(slot)


def place_kernel(cut, hold, got, other_hold, other_got, out, sems):
    me = lax.axis_index("cols")
    core = me & 1
    rows = hold.shape[1]
    bit0 = (me >> cut[0]) & 1
    bit1 = (me >> cut[1]) & 1
    mine = jnp.where(core == 0, bit0, bit1)
    other = jnp.where(core == 0, bit1, bit0)
    slots = (
        (hold, core * 2 + mine),
        (got, core * 2 + 1 - mine),
        (other_hold, (1 - core) * 2 + other),
        (other_got, (1 - core) * 2 + 1 - other),
    )
    copies = [
        pltpu.make_async_copy(
            piece, out.at[:, pl.ds(pl.multiple_of(at * rows, rows), rows), :], sems.at[k]
        )
        for k, (piece, at) in enumerate(slots)
    ]
    copy_all(copies)


def place(cut, hold, got, other_hold, other_got):
    n, rows, width = hold.shape
    return pl.pallas_call(
        lambda *refs: place_kernel(cut, *refs),
        out_shape=jax.ShapeDtypeStruct((n, 4 * rows, width), hold.dtype),
        in_specs=[ANY] * 4,
        out_specs=ANY,
        scratch_shapes=[pltpu.SemaphoreType.DMA((4,))],
        name="place",
        **small(bytes_accessed=2 * n * 4 * rows * width * 2),
    )(hold, got, other_hold, other_got)


class Spread:
    def __init__(self, slot, owners_here, order):
        count = lax.axis_size("cols")
        dims = count.bit_length() - 2
        self.me = lax.axis_index("cols")
        self.core = self.me & 1
        self.owners = owners_here
        self.cut = (1, dims)
        self.others = [(b, b - 1) for b in range(2, dims + 1)]
        (give_out,) = cut_slot(self.cut, order, [(False, False)], slot)
        own_out, give_hold, own_hold = cut_slot(
            self.cut, order, [(True, False), (False, True), (True, True)], slot
        )
        self.own = own_out, own_hold
        self.theirs = flip(give_out, (0, 0)), flip(give_hold, (0, 0))

    def bit(self, index, bits):
        return (index >> jnp.where(self.core == 0, bits[0], bits[1])) & 1

    def choose(self, rounds, test, yes, no):
        holds = [test(self.owners[r]) for r in rounds]
        mask = holds[0]
        for at in range(1, len(rounds)):
            if rounds[at] != rounds[at - 1]:
                row = lax.broadcasted_iota(jnp.int32, yes.shape, 0)
                mask = jnp.where(row < at, mask, holds[at])
        return jnp.where(mask, yes, no)

    def begin(self, rounds, rows, *first):
        out, hold = [
            self.choose(rounds, lambda owner: (owner & 1) == self.core, own[rows], theirs[rows])
            for own, theirs in zip(self.own, self.theirs)
        ]
        if first:
            out = after(out, *first)
        return rounds, hold, flip(out, self.cut)

    def keep(self, state, bits):
        rounds, hold, got = state
        mine = self.bit(self.me, bits)
        return self.choose(rounds, lambda owner: mine == self.bit(owner, bits), hold, got)

    def middle(self, state, *first):
        bits = self.cut
        for other in self.others:
            hold = self.keep(state, bits)
            if first:
                hold = after(hold, *first)
                first = ()
            state = (state[0], hold, flip(hold, other))
            bits = other
        return state

    def last(self, state, *first):
        hold = self.keep(state, self.others[-1])
        if first:
            hold = after(hold, *first)
        return hold, flip(hold, self.cut)

    def join(self, hold, got):
        return place(self.cut, hold, got, flip(hold, (0, 0)), flip(got, (0, 0)))

    def join_above(self, hold, got, done):
        both = shifted(after(jnp.stack([hold, got]), done), "rows", 1)
        other = flip(both, (0, 0))
        return place(self.cut, both[0], both[1], other[0], other[1])


def apply(q, x):
    product = lax.dot_general(q, x, (((0,), (0,)), ((), ())), preferred_element_type=jnp.float32)
    return product.astype(jnp.bfloat16)


def apply_many(q, x):
    product = jnp.einsum("nab,nac->nbc", q, x, preferred_element_type=jnp.float32)
    return product.astype(jnp.bfloat16)


def write_inner(inner, border):
    rows, cols = inner.shape

    def kernel(source, out):
        out[...] = source[...]

    return pl.pallas_call(
        kernel,
        grid=(rows // border,),
        out_shape=jax.ShapeDtypeStruct((rows + 2 * border, cols), inner.dtype),
        in_specs=[pl.BlockSpec((border, cols), lambda i: (i, 0))],
        out_specs=pl.BlockSpec((border, cols), lambda i: (i + 1, 0)),
        compiler_params=pltpu.CompilerParams(vmem_limit_bytes=8 << 20),
        cost_estimate=pl.CostEstimate(flops=0, bytes_accessed=4 * inner.size, transcendentals=0),
        name="write_inner",
    )(inner)


def write_outer(whole, top, low):
    border, cols = top.shape
    last = whole.shape[0] // border - 1

    def kernel(_, first, final, out):
        @pl.when(pl.program_id(0) == 0)
        def _():
            out[...] = first[...]

        @pl.when(pl.program_id(0) == 1)
        def _():
            out[...] = final[...]

    block = pl.BlockSpec((border, cols), lambda i: (0, 0))
    return pl.pallas_call(
        kernel,
        grid=(2,),
        out_shape=jax.ShapeDtypeStruct(whole.shape, whole.dtype),
        in_specs=[ANY, block, block],
        out_specs=pl.BlockSpec((border, cols), lambda i: (i * last, 0)),
        input_output_aliases={0: 0},
        compiler_params=pltpu.CompilerParams(vmem_limit_bytes=8 << 20),
        cost_estimate=pl.CostEstimate(flops=0, bytes_accessed=8 * top.size, transcendentals=0),
        name="write_outer",
    )(whole, top, low)


def local(slab, transforms, owners):
    row_block = lax.axis_index("rows")
    last_block = lax.axis_size("rows") - 1
    window = transforms.shape[2]
    border = window // 2
    local_rows, local_cols = slab.shape
    wins = local_rows // window
    rounds = owners.shape[0]
    slot = transforms[0].reshape(2 * wins, 2, 2, window // 4, window)
    crossing = 2 * wins - 1
    middle_one, middle_two = list(range(1, wins - 1)), list(range(wins, crossing))
    order = [crossing, crossing, 0, wins - 1] + middle_one + middle_two
    spread = Spread(slot, owners[:, row_block], order)
    streams = []
    for r in range(rounds):
        across = ([r + 1] if r + 1 < rounds else []) + ([r] if r == 0 else [])
        first = 2 - len(across)
        if r == 0:
            streams.append(spread.middle(spread.begin(across + [r, r], slice(first, 4))))
            streams.append(spread.middle(spread.begin([r] * (len(order) - 4), slice(4, len(order)))))
        else:
            begun = spread.begin(across + [r] * crossing, slice(first, len(order)), streams[r - 1][2])
            streams.append(spread.middle(begun))
    pairs = [spread.last(stream) for stream in streams]

    matrix = slab
    crosses, above_crosses = {}, {}
    for r in range(rounds):
        head = pairs[0] if r == 0 else pairs[r + 1]
        edges = spread.join(*head)
        across = ([r + 1] if r + 1 < rounds else []) + ([r] if r == 0 else [])
        n = len(across)
        for k, q in enumerate(across):
            crosses[q] = edges[k]
        edges = edges[n:]
        outer = apply_many(
            edges[:2], jnp.stack([matrix[:window], matrix[local_rows - window :]])
        )
        head_rows, tail_rows = outer[0], outer[1]
        begin, end = head_rows[:border], tail_rows[border:]
        above, below = swap_rows(begin, end)
        rest = spread.join(*pairs[1]) if r == 0 else edges[2:]
        ones, twos = rest[: wins - 2], rest[wins - 2 :]
        mid = apply_many(
            ones,
            matrix[window : local_rows - window].reshape(wins - 2, window, local_cols),
        ).reshape(local_rows - 2 * window, local_cols)
        centre = jnp.concatenate([head_rows[border:], mid, tail_rows[:border]], 0)
        inner = apply_many(twos, centre.reshape(wins - 1, window, local_cols)).reshape(
            local_rows - window, local_cols
        )
        if n:
            from_above = spread.join_above(
                head[0][:n, :, border:], head[1][:n, :, border:], inner
            )
            for k, q in enumerate(across):
                above_crosses[q] = from_above[k]
        prev, cross = above_crosses[r], crosses[r]
        low = apply(cross[:, :border], jnp.concatenate([end, below], 0))
        low = jnp.where(row_block == last_block, end, low)
        top = apply(prev, jnp.concatenate([above, begin], 0))
        top = jnp.where(row_block == 0, begin, top)
        if r < rounds - 1:
            matrix = jnp.concatenate([top, inner, low], 0)
    return write_outer(write_inner(inner, border), top, low)


def solution(mesh):
    return jax.shard_map(
        local,
        mesh=mesh,
        in_specs=(P("rows", "cols"), P("cols", "rows", None), P()),
        out_specs=P("rows", "cols"),
        check_vma=False,
    )
```

```python
import jax
import jax.numpy as jnp
from jax import lax
from jax.experimental import pallas as pl
from jax.experimental.pallas import tpu as pltpu
from jax.sharding import PartitionSpec as P


def shifted(value, axis, steps):
    count = lax.axis_size(axis)
    initial, last = (max(0, -steps), min(count, count - steps))
    return lax.ppermute(value, axis, [(source, source + steps) for source in range(initial, last)])


def swap_rows(up, down):
    count = lax.axis_size("rows")
    even = (lax.axis_index("rows") & 1) == 0

    def swap(value, start):
        pairs = [(low, low + 1) for low in range(start, count - 1, 2)]
        return lax.ppermute(value, "rows", pairs + [(b, a) for a, b in pairs])

    first = swap(jnp.where(even, down, up), 0)
    second = swap(jnp.where(even, up, down), 1)
    return jnp.where(even, second, first), jnp.where(even, first, second)


def flip(value, bits):
    count = lax.axis_size("cols")
    return lax.ppermute(value, "cols", [(d, d ^ (1 << bits[d & 1])) for d in range(count)])


def copy_all(copies):
    for copy in copies:
        copy.start()
    for copy in copies:
        copy.wait()


def small(flops=0, bytes_accessed=0, limit=1 << 20):
    return dict(
        compiler_params=pltpu.CompilerParams(vmem_limit_bytes=limit),
        cost_estimate=pl.CostEstimate(
            flops=flops, bytes_accessed=bytes_accessed, transcendentals=0
        ),
    )


ANY = pl.BlockSpec(memory_space=pl.ANY)


def after(value, *done):
    def kernel(source, *refs):
        copy_all([pltpu.make_async_copy(source, refs[-2], refs[-1])])

    return pl.pallas_call(
        kernel,
        out_shape=jax.ShapeDtypeStruct(value.shape, value.dtype),
        in_specs=[ANY] * (1 + len(done)),
        out_specs=ANY,
        scratch_shapes=[pltpu.SemaphoreType.DMA],
        name="after",
        **small(bytes_accessed=4 * value.size),
    )(value, *done)


def runs(ms):
    found = []
    for at, m in enumerate(ms):
        if found and found[-1][0] + found[-1][2] == m:
            found[-1][2] += 1
        else:
            found.append([m, at, 1])
    return found


def cut_slot(cut, order, kinds, slot):
    _, _, _, rows, width = slot.shape
    shapes = [jax.ShapeDtypeStruct((len(order), rows, width), slot.dtype) for _ in kinds]
    spans = runs(order)

    def kernel(source, *refs):
        outs, sems = refs[:-1], refs[-1]
        me = lax.axis_index("cols")
        core = me & 1
        bit0 = (me >> cut[0]) & 1
        bit1 = (me >> cut[1]) & 1
        mine = jnp.where(core == 0, bit0, bit1)
        other = jnp.where(core == 0, bit1, bit0)
        copies = []
        for (own, hold), out in zip(kinds, outs):
            half = core if own else 1 - core
            piece = mine if own else other
            piece = piece if hold else 1 - piece
            for first, at, n in spans:
                copies.append(
                    pltpu.make_async_copy(
                        source.at[pl.ds(first, n), half, piece],
                        out.at[pl.ds(at, n)],
                        sems.at[len(copies)],
                    )
                )
        copy_all(copies)

    return pl.pallas_call(
        kernel,
        out_shape=shapes,
        in_specs=[pl.BlockSpec(memory_space=pltpu.HBM)],
        out_specs=[ANY] * len(shapes),
        scratch_shapes=[pltpu.SemaphoreType.DMA((len(spans) * len(kinds),))],
        name="cut_slot",
        **small(bytes_accessed=len(kinds) * slot.size, limit=(48 if len(kinds) == 1 else 1) << 20),
    )(slot)


def place_kernel(cut, hold, got, other_hold, other_got, out, sems):
    me = lax.axis_index("cols")
    core = me & 1
    rows = hold.shape[1]
    bit0 = (me >> cut[0]) & 1
    bit1 = (me >> cut[1]) & 1
    mine = jnp.where(core == 0, bit0, bit1)
    other = jnp.where(core == 0, bit1, bit0)
    slots = (
        (hold, core * 2 + mine),
        (got, core * 2 + 1 - mine),
        (other_hold, (1 - core) * 2 + other),
        (other_got, (1 - core) * 2 + 1 - other),
    )
    copies = [
        pltpu.make_async_copy(
            piece, out.at[:, pl.ds(pl.multiple_of(at * rows, rows), rows), :], sems.at[k]
        )
        for k, (piece, at) in enumerate(slots)
    ]
    copy_all(copies)


def place(cut, hold, got, other_hold, other_got):
    n, rows, width = hold.shape
    return pl.pallas_call(
        lambda *refs: place_kernel(cut, *refs),
        out_shape=jax.ShapeDtypeStruct((n, 4 * rows, width), hold.dtype),
        in_specs=[ANY] * 4,
        out_specs=ANY,
        scratch_shapes=[pltpu.SemaphoreType.DMA((4,))],
        name="place",
        **small(bytes_accessed=2 * n * 4 * rows * width * 2),
    )(hold, got, other_hold, other_got)


class Spread:
    def __init__(self, slot, owners_here, order):
        count = lax.axis_size("cols")
        dims = count.bit_length() - 2
        self.me = lax.axis_index("cols")
        self.core = self.me & 1
        self.owners = owners_here
        self.cut = (1, dims)
        self.others = [(b, b - 1) for b in range(2, dims + 1)]
        (give_out,) = cut_slot(self.cut, order, [(False, False)], slot)
        own_out, give_hold, own_hold = cut_slot(
            self.cut, order, [(True, False), (False, True), (True, True)], slot
        )
        self.own = own_out, own_hold
        self.theirs = flip(give_out, (0, 0)), flip(give_hold, (0, 0))

    def bit(self, index, bits):
        return (index >> jnp.where(self.core == 0, bits[0], bits[1])) & 1

    def choose(self, rounds, test, yes, no):
        holds = [test(self.owners[r]) for r in rounds]
        mask = holds[0]
        for at in range(1, len(rounds)):
            if rounds[at] != rounds[at - 1]:
                row = lax.broadcasted_iota(jnp.int32, yes.shape, 0)
                mask = jnp.where(row < at, mask, holds[at])
        return jnp.where(mask, yes, no)

    def begin(self, rounds, rows, *first):
        out, hold = [
            self.choose(rounds, lambda owner: (owner & 1) == self.core, own[rows], theirs[rows])
            for own, theirs in zip(self.own, self.theirs)
        ]
        if first:
            out = after(out, *first)
        return rounds, hold, flip(out, self.cut)

    def keep(self, state, bits):
        rounds, hold, got = state
        mine = self.bit(self.me, bits)
        return self.choose(rounds, lambda owner: mine == self.bit(owner, bits), hold, got)

    def middle(self, state, *first):
        bits = self.cut
        for other in self.others:
            hold = self.keep(state, bits)
            if first:
                hold = after(hold, *first)
                first = ()
            state = (state[0], hold, flip(hold, other))
            bits = other
        return state

    def last(self, state, *first):
        hold = self.keep(state, self.others[-1])
        if first:
            hold = after(hold, *first)
        return hold, flip(hold, self.cut)

    def last_two(self, state, count):
        hold = self.keep(state, self.others[-1])
        return [(part, flip(part, self.cut)) for part in (hold[:count], hold[count:])]

    def join(self, hold, got):
        return place(self.cut, hold, got, flip(hold, (0, 0)), flip(got, (0, 0)))

    def join_above(self, hold, got):
        both = shifted(jnp.stack([hold, got]), "rows", 1)
        other = flip(both, (0, 0))
        return place(self.cut, both[0], both[1], other[0], other[1])


def apply(q, x):
    product = lax.dot_general(q, x, (((0,), (0,)), ((), ())), preferred_element_type=jnp.float32)
    return product.astype(jnp.bfloat16)


def apply_many(q, x):
    product = jnp.einsum("nab,nac->nbc", q, x, preferred_element_type=jnp.float32)
    return product.astype(jnp.bfloat16)


def write_inner(inner, border):
    rows, cols = inner.shape

    def kernel(source, out):
        out[...] = source[...]

    return pl.pallas_call(
        kernel,
        grid=(rows // border,),
        out_shape=jax.ShapeDtypeStruct((rows + 2 * border, cols), inner.dtype),
        in_specs=[pl.BlockSpec((border, cols), lambda i: (i, 0))],
        out_specs=pl.BlockSpec((border, cols), lambda i: (i + 1, 0)),
        compiler_params=pltpu.CompilerParams(vmem_limit_bytes=8 << 20),
        cost_estimate=pl.CostEstimate(flops=0, bytes_accessed=4 * inner.size, transcendentals=0),
        name="write_inner",
    )(inner)


def write_outer(whole, top, low):
    border, cols = top.shape
    last = whole.shape[0] // border - 1

    def kernel(_, first, final, out):
        @pl.when(pl.program_id(0) == 0)
        def _():
            out[...] = first[...]

        @pl.when(pl.program_id(0) == 1)
        def _():
            out[...] = final[...]

    block = pl.BlockSpec((border, cols), lambda i: (0, 0))
    return pl.pallas_call(
        kernel,
        grid=(2,),
        out_shape=jax.ShapeDtypeStruct(whole.shape, whole.dtype),
        in_specs=[ANY, block, block],
        out_specs=pl.BlockSpec((border, cols), lambda i: (i * last, 0)),
        input_output_aliases={0: 0},
        compiler_params=pltpu.CompilerParams(vmem_limit_bytes=8 << 20),
        cost_estimate=pl.CostEstimate(flops=0, bytes_accessed=8 * top.size, transcendentals=0),
        name="write_outer",
    )(whole, top, low)


def local(slab, transforms, owners):
    row_block = lax.axis_index("rows")
    last_block = lax.axis_size("rows") - 1
    window = transforms.shape[2]
    border = window // 2
    local_rows, local_cols = slab.shape
    wins = local_rows // window
    rounds = owners.shape[0]
    slot = transforms[0].reshape(2 * wins, 2, 2, window // 4, window)
    crossing = 2 * wins - 1
    middle_one, middle_two = list(range(1, wins - 1)), list(range(wins, crossing))
    order = [crossing, crossing, 0, wins - 1] + middle_one + middle_two
    spread = Spread(slot, owners[:, row_block], order)
    streams = []
    for r in range(rounds):
        across = ([r + 1] if r + 1 < rounds else []) + ([r] if r == 0 else [])
        first = 2 - len(across)
        if r == 0:
            streams.append(spread.middle(spread.begin(across + [r, r], slice(first, 4))))
            streams.append(spread.middle(spread.begin([r] * (len(order) - 4), slice(4, len(order)))))
        else:
            begun = spread.begin(across + [r] * crossing, slice(first, len(order)), streams[r - 1][2])
            streams.append(spread.middle(begun))
    pairs = [spread.last(stream) for stream in streams[:2]]
    for r in range(1, rounds):
        pairs += spread.last_two(streams[r + 1], 3 if r + 1 < rounds else 2)

    matrix = slab
    crosses, above_crosses = {}, {}
    for r in range(rounds):
        head, tail = pairs[2 * r], pairs[2 * r + 1]
        edges = spread.join(*head)
        across = ([r + 1] if r + 1 < rounds else []) + ([r] if r == 0 else [])
        if across:
            n = len(across)
            from_above = spread.join_above(head[0][:n, :, border:], head[1][:n, :, border:])
            for k, q in enumerate(across):
                crosses[q], above_crosses[q] = edges[k], from_above[k]
            edges = edges[n:]
        prev, cross = above_crosses[r], crosses[r]
        outer = apply_many(
            edges[:2], jnp.stack([matrix[:window], matrix[local_rows - window :]])
        )
        head_rows, tail_rows = outer[0], outer[1]
        begin, end = head_rows[:border], tail_rows[border:]
        above, below = swap_rows(begin, end)
        rest = spread.join(*tail)
        ones, twos = rest[: wins - 2], rest[wins - 2 :]
        mid = apply_many(
            ones,
            matrix[window : local_rows - window].reshape(wins - 2, window, local_cols),
        ).reshape(local_rows - 2 * window, local_cols)
        centre = jnp.concatenate([head_rows[border:], mid, tail_rows[:border]], 0)
        inner = apply_many(twos, centre.reshape(wins - 1, window, local_cols)).reshape(
            local_rows - window, local_cols
        )
        low = apply(cross[:, :border], jnp.concatenate([end, below], 0))
        low = jnp.where(row_block == last_block, end, low)
        top = apply(prev, jnp.concatenate([above, begin], 0))
        top = jnp.where(row_block == 0, begin, top)
        if r < rounds - 1:
            matrix = jnp.concatenate([top, inner, low], 0)
    return write_outer(write_inner(inner, border), top, low)


def solution(mesh):
    return jax.shard_map(
        local,
        mesh=mesh,
        in_specs=(P("rows", "cols"), P("cols", "rows", None), P()),
        out_specs=P("rows", "cols"),
        check_vma=False,
    )
```

```python
import jax
import jax.numpy as jnp
from jax import lax
from jax.experimental import pallas as pl
from jax.experimental.pallas import tpu as pltpu
from jax.sharding import PartitionSpec as P


def shifted(value, axis, steps):
    count = lax.axis_size(axis)
    initial, last = (max(0, -steps), min(count, count - steps))
    return lax.ppermute(value, axis, [(source, source + steps) for source in range(initial, last)])


def swap_rows(up, down):
    count = lax.axis_size("rows")
    even = (lax.axis_index("rows") & 1) == 0

    def swap(value, start):
        pairs = [(low, low + 1) for low in range(start, count - 1, 2)]
        return lax.ppermute(value, "rows", pairs + [(b, a) for a, b in pairs])

    first = swap(jnp.where(even, down, up), 0)
    second = swap(jnp.where(even, up, down), 1)
    return jnp.where(even, second, first), jnp.where(even, first, second)


def flip(value, bits):
    count = lax.axis_size("cols")
    return lax.ppermute(value, "cols", [(d, d ^ (1 << bits[d & 1])) for d in range(count)])


def copy_all(copies):
    for copy in copies:
        copy.start()
    for copy in copies:
        copy.wait()


def small(flops=0, bytes_accessed=0, limit=1 << 20):
    return dict(
        compiler_params=pltpu.CompilerParams(vmem_limit_bytes=limit),
        cost_estimate=pl.CostEstimate(
            flops=flops, bytes_accessed=bytes_accessed, transcendentals=0
        ),
    )


ANY = pl.BlockSpec(memory_space=pl.ANY)


def after(value, *done):
    def kernel(source, *refs):
        copy_all([pltpu.make_async_copy(source, refs[-2], refs[-1])])

    return pl.pallas_call(
        kernel,
        out_shape=jax.ShapeDtypeStruct(value.shape, value.dtype),
        in_specs=[ANY] * (1 + len(done)),
        out_specs=ANY,
        scratch_shapes=[pltpu.SemaphoreType.DMA],
        name="after",
        **small(bytes_accessed=4 * value.size),
    )(value, *done)


def runs(ms):
    found = []
    for at, m in enumerate(ms):
        if found and found[-1][0] + found[-1][2] == m:
            found[-1][2] += 1
        else:
            found.append([m, at, 1])
    return found


def cut_slot(cut, order, kinds, slot):
    _, _, _, rows, width = slot.shape
    shapes = [jax.ShapeDtypeStruct((len(order), rows, width), slot.dtype) for _ in kinds]
    spans = runs(order)

    def kernel(source, *refs):
        outs, sems = refs[:-1], refs[-1]
        me = lax.axis_index("cols")
        core = me & 1
        bit0 = (me >> cut[0]) & 1
        bit1 = (me >> cut[1]) & 1
        mine = jnp.where(core == 0, bit0, bit1)
        other = jnp.where(core == 0, bit1, bit0)
        copies = []
        for (own, hold), out in zip(kinds, outs):
            half = core if own else 1 - core
            piece = mine if own else other
            piece = piece if hold else 1 - piece
            for first, at, n in spans:
                copies.append(
                    pltpu.make_async_copy(
                        source.at[pl.ds(first, n), half, piece],
                        out.at[pl.ds(at, n)],
                        sems.at[len(copies)],
                    )
                )
        copy_all(copies)

    return pl.pallas_call(
        kernel,
        out_shape=shapes,
        in_specs=[pl.BlockSpec(memory_space=pltpu.HBM)],
        out_specs=[ANY] * len(shapes),
        scratch_shapes=[pltpu.SemaphoreType.DMA((len(spans) * len(kinds),))],
        name="cut_slot",
        **small(bytes_accessed=len(kinds) * slot.size, limit=(48 if len(kinds) == 1 else 1) << 20),
    )(slot)


def place_kernel(cut, hold, got, other_hold, other_got, out, sems):
    me = lax.axis_index("cols")
    core = me & 1
    rows = hold.shape[1]
    bit0 = (me >> cut[0]) & 1
    bit1 = (me >> cut[1]) & 1
    mine = jnp.where(core == 0, bit0, bit1)
    other = jnp.where(core == 0, bit1, bit0)
    slots = (
        (hold, core * 2 + mine),
        (got, core * 2 + 1 - mine),
        (other_hold, (1 - core) * 2 + other),
        (other_got, (1 - core) * 2 + 1 - other),
    )
    copies = [
        pltpu.make_async_copy(
            piece, out.at[:, pl.ds(pl.multiple_of(at * rows, rows), rows), :], sems.at[k]
        )
        for k, (piece, at) in enumerate(slots)
    ]
    copy_all(copies)


def place(cut, hold, got, other_hold, other_got):
    n, rows, width = hold.shape
    return pl.pallas_call(
        lambda *refs: place_kernel(cut, *refs),
        out_shape=jax.ShapeDtypeStruct((n, 4 * rows, width), hold.dtype),
        in_specs=[ANY] * 4,
        out_specs=ANY,
        scratch_shapes=[pltpu.SemaphoreType.DMA((4,))],
        name="place",
        **small(bytes_accessed=2 * n * 4 * rows * width * 2),
    )(hold, got, other_hold, other_got)


class Spread:
    def __init__(self, slot, owners_here, order):
        count = lax.axis_size("cols")
        dims = count.bit_length() - 2
        self.me = lax.axis_index("cols")
        self.core = self.me & 1
        self.owners = owners_here
        self.cut = (1, dims)
        self.others = [(b, b - 1) for b in range(2, dims + 1)]
        (give_out,) = cut_slot(self.cut, order, [(False, False)], slot)
        own_out, give_hold, own_hold = cut_slot(
            self.cut, order, [(True, False), (False, True), (True, True)], slot
        )
        self.own = own_out, own_hold
        self.theirs = flip(give_out, (0, 0)), flip(give_hold, (0, 0))

    def bit(self, index, bits):
        return (index >> jnp.where(self.core == 0, bits[0], bits[1])) & 1

    def choose(self, rounds, test, yes, no):
        holds = [test(self.owners[r]) for r in rounds]
        mask = holds[0]
        for at in range(1, len(rounds)):
            if rounds[at] != rounds[at - 1]:
                row = lax.broadcasted_iota(jnp.int32, yes.shape, 0)
                mask = jnp.where(row < at, mask, holds[at])
        return jnp.where(mask, yes, no)

    def begin(self, rounds, rows, *first):
        out, hold = [
            self.choose(rounds, lambda owner: (owner & 1) == self.core, own[rows], theirs[rows])
            for own, theirs in zip(self.own, self.theirs)
        ]
        if first:
            out = after(out, *first)
        return rounds, hold, flip(out, self.cut)

    def keep(self, state, bits):
        rounds, hold, got = state
        mine = self.bit(self.me, bits)
        return self.choose(rounds, lambda owner: mine == self.bit(owner, bits), hold, got)

    def middle(self, state, *first):
        bits = self.cut
        for other in self.others:
            hold = self.keep(state, bits)
            if first:
                hold = after(hold, *first)
                first = ()
            state = (state[0], hold, flip(hold, other))
            bits = other
        return state

    def last(self, state, *first):
        hold = self.keep(state, self.others[-1])
        if first:
            hold = after(hold, *first)
        return hold, flip(hold, self.cut)

    def last_two(self, state, count):
        hold = self.keep(state, self.others[-1])
        return [(part, flip(part, self.cut)) for part in (hold[:count], hold[count:])]

    def join(self, hold, got):
        return place(self.cut, hold, got, flip(hold, (0, 0)), flip(got, (0, 0)))

    def join_above(self, hold, got):
        both = shifted(jnp.stack([hold, got]), "rows", 1)
        other = flip(both, (0, 0))
        return place(self.cut, both[0], both[1], other[0], other[1])


def apply(q, x):
    product = lax.dot_general(q, x, (((0,), (0,)), ((), ())), preferred_element_type=jnp.float32)
    return product.astype(jnp.bfloat16)


def apply_many(q, x):
    product = jnp.einsum("nab,nac->nbc", q, x, preferred_element_type=jnp.float32)
    return product.astype(jnp.bfloat16)


def write_inner(inner, border):
    rows, cols = inner.shape

    def kernel(source, out):
        out[...] = source[...]

    return pl.pallas_call(
        kernel,
        grid=(rows // border,),
        out_shape=jax.ShapeDtypeStruct((rows + 2 * border, cols), inner.dtype),
        in_specs=[pl.BlockSpec((border, cols), lambda i: (i, 0))],
        out_specs=pl.BlockSpec((border, cols), lambda i: (i + 1, 0)),
        compiler_params=pltpu.CompilerParams(vmem_limit_bytes=8 << 20),
        cost_estimate=pl.CostEstimate(flops=0, bytes_accessed=4 * inner.size, transcendentals=0),
        name="write_inner",
    )(inner)


def write_outer(whole, top, low):
    border, cols = top.shape
    last = whole.shape[0] // border - 1

    def kernel(_, first, final, out):
        @pl.when(pl.program_id(0) == 0)
        def _():
            out[...] = first[...]

        @pl.when(pl.program_id(0) == 1)
        def _():
            out[...] = final[...]

    block = pl.BlockSpec((border, cols), lambda i: (0, 0))
    return pl.pallas_call(
        kernel,
        grid=(2,),
        out_shape=jax.ShapeDtypeStruct(whole.shape, whole.dtype),
        in_specs=[ANY, block, block],
        out_specs=pl.BlockSpec((border, cols), lambda i: (i * last, 0)),
        input_output_aliases={0: 0},
        compiler_params=pltpu.CompilerParams(vmem_limit_bytes=8 << 20),
        cost_estimate=pl.CostEstimate(flops=0, bytes_accessed=8 * top.size, transcendentals=0),
        name="write_outer",
    )(whole, top, low)


def local(slab, transforms, owners):
    row_block = lax.axis_index("rows")
    last_block = lax.axis_size("rows") - 1
    window = transforms.shape[2]
    border = window // 2
    local_rows, local_cols = slab.shape
    wins = local_rows // window
    rounds = owners.shape[0]
    slot = transforms[0].reshape(2 * wins, 2, 2, window // 4, window)
    crossing = 2 * wins - 1
    middle_one, middle_two = list(range(1, wins - 1)), list(range(wins, crossing))
    order = [crossing, crossing, 0, wins - 1] + middle_one + middle_two
    spread = Spread(slot, owners[:, row_block], order)
    streams = []
    for r in range(rounds):
        across = ([r + 1] if r + 1 < rounds else []) + ([r] if r == 0 else [])
        first = 2 - len(across)
        if r == 0:
            streams.append(spread.middle(spread.begin(across + [r, r], slice(first, 4))))
            streams.append(spread.middle(spread.begin([r] * (len(order) - 4), slice(4, len(order)))))
        else:
            begun = spread.begin(across + [r] * crossing, slice(first, len(order)), streams[r - 1][2])
            streams.append(spread.middle(begun))
    pairs = [spread.last(stream) for stream in streams[:2]]
    for r in range(1, rounds):
        pairs += spread.last_two(streams[r + 1], 3 if r + 1 < rounds else 2)

    matrix = slab
    crosses, above_crosses = {}, {}
    for r in range(rounds):
        head, tail = pairs[2 * r], pairs[2 * r + 1]
        edges = spread.join(*head)
        across = ([r + 1] if r + 1 < rounds else []) + ([r] if r == 0 else [])
        if across:
            n = len(across)
            from_above = spread.join_above(head[0][:n, :, border:], head[1][:n, :, border:])
            for k, q in enumerate(across):
                crosses[q], above_crosses[q] = edges[k], from_above[k]
            edges = edges[n:]
        prev, cross = above_crosses[r], crosses[r]
        outer = apply_many(
            edges[:2], jnp.stack([matrix[:window], matrix[local_rows - window :]])
        )
        head_rows, tail_rows = outer[0], outer[1]
        begin, end = head_rows[:border], tail_rows[border:]
        above, below = swap_rows(begin, end)
        rest = spread.join(*tail)
        ones, twos = rest[: wins - 2], rest[wins - 2 :]
        mid = apply_many(
            ones,
            matrix[window : local_rows - window].reshape(wins - 2, window, local_cols),
        ).reshape(local_rows - 2 * window, local_cols)
        centre = jnp.concatenate([head_rows[border:], mid, tail_rows[:border]], 0)
        inner = apply_many(twos, centre.reshape(wins - 1, window, local_cols)).reshape(
            local_rows - window, local_cols
        )
        if r == rounds - 1:
            whole = write_inner(inner, border)
            prev, cross = after(prev, whole), after(cross, whole)
        low = apply(cross[:, :border], jnp.concatenate([end, below], 0))
        low = jnp.where(row_block == last_block, end, low)
        top = apply(prev, jnp.concatenate([above, begin], 0))
        top = jnp.where(row_block == 0, begin, top)
        if r < rounds - 1:
            matrix = jnp.concatenate([top, inner, low], 0)
    return write_outer(whole, top, low)


def solution(mesh):
    return jax.shard_map(
        local,
        mesh=mesh,
        in_specs=(P("rows", "cols"), P("cols", "rows", None), P()),
        out_specs=P("rows", "cols"),
        check_vma=False,
    )
```

```python
import jax
import jax.numpy as jnp
from jax import lax
from jax.experimental import pallas as pl
from jax.experimental.pallas import tpu as pltpu
from jax.sharding import PartitionSpec as P


def shifted(value, axis, steps):
    count = lax.axis_size(axis)
    initial, last = (max(0, -steps), min(count, count - steps))
    return lax.ppermute(value, axis, [(source, source + steps) for source in range(initial, last)])


def swap_rows(up, down):
    count = lax.axis_size("rows")
    even = (lax.axis_index("rows") & 1) == 0

    def swap(value, start):
        pairs = [(low, low + 1) for low in range(start, count - 1, 2)]
        return lax.ppermute(value, "rows", pairs + [(b, a) for a, b in pairs])

    first = swap(jnp.where(even, down, up), 0)
    second = swap(jnp.where(even, up, down), 1)
    return jnp.where(even, second, first), jnp.where(even, first, second)


def flip(value, bits):
    count = lax.axis_size("cols")
    return lax.ppermute(value, "cols", [(d, d ^ (1 << bits[d & 1])) for d in range(count)])


def copy_all(copies):
    for copy in copies:
        copy.start()
    for copy in copies:
        copy.wait()


def small(flops=0, bytes_accessed=0, limit=1 << 20):
    return dict(
        compiler_params=pltpu.CompilerParams(vmem_limit_bytes=limit),
        cost_estimate=pl.CostEstimate(
            flops=flops, bytes_accessed=bytes_accessed, transcendentals=0
        ),
    )


ANY = pl.BlockSpec(memory_space=pl.ANY)


def after(value, *done):
    def kernel(source, *refs):
        copy_all([pltpu.make_async_copy(source, refs[-2], refs[-1])])

    return pl.pallas_call(
        kernel,
        out_shape=jax.ShapeDtypeStruct(value.shape, value.dtype),
        in_specs=[ANY] * (1 + len(done)),
        out_specs=ANY,
        scratch_shapes=[pltpu.SemaphoreType.DMA],
        name="after",
        **small(bytes_accessed=4 * value.size),
    )(value, *done)


def runs(ms):
    found = []
    for at, m in enumerate(ms):
        if found and found[-1][0] + found[-1][2] == m:
            found[-1][2] += 1
        else:
            found.append([m, at, 1])
    return found


def cut_slot(cut, order, kinds, slot):
    _, _, _, rows, width = slot.shape
    shapes = [jax.ShapeDtypeStruct((len(order), rows, width), slot.dtype) for _ in kinds]
    spans = runs(order)

    def kernel(source, *refs):
        outs, sems = refs[:-1], refs[-1]
        me = lax.axis_index("cols")
        core = me & 1
        bit0 = (me >> cut[0]) & 1
        bit1 = (me >> cut[1]) & 1
        mine = jnp.where(core == 0, bit0, bit1)
        other = jnp.where(core == 0, bit1, bit0)
        copies = []
        for (own, hold), out in zip(kinds, outs):
            half = core if own else 1 - core
            piece = mine if own else other
            piece = piece if hold else 1 - piece
            for first, at, n in spans:
                copies.append(
                    pltpu.make_async_copy(
                        source.at[pl.ds(first, n), half, piece],
                        out.at[pl.ds(at, n)],
                        sems.at[len(copies)],
                    )
                )
        copy_all(copies)

    return pl.pallas_call(
        kernel,
        out_shape=shapes,
        in_specs=[pl.BlockSpec(memory_space=pltpu.HBM)],
        out_specs=[ANY] * len(shapes),
        scratch_shapes=[pltpu.SemaphoreType.DMA((len(spans) * len(kinds),))],
        name="cut_slot",
        **small(bytes_accessed=len(kinds) * slot.size, limit=(48 if len(kinds) == 1 else 1) << 20),
    )(slot)


def place_kernel(cut, hold, got, other_hold, other_got, out, sems):
    me = lax.axis_index("cols")
    core = me & 1
    rows = hold.shape[1]
    bit0 = (me >> cut[0]) & 1
    bit1 = (me >> cut[1]) & 1
    mine = jnp.where(core == 0, bit0, bit1)
    other = jnp.where(core == 0, bit1, bit0)
    slots = (
        (hold, core * 2 + mine),
        (got, core * 2 + 1 - mine),
        (other_hold, (1 - core) * 2 + other),
        (other_got, (1 - core) * 2 + 1 - other),
    )
    copies = [
        pltpu.make_async_copy(
            piece, out.at[:, pl.ds(pl.multiple_of(at * rows, rows), rows), :], sems.at[k]
        )
        for k, (piece, at) in enumerate(slots)
    ]
    copy_all(copies)


def place(cut, hold, got, other_hold, other_got):
    n, rows, width = hold.shape
    return pl.pallas_call(
        lambda *refs: place_kernel(cut, *refs),
        out_shape=jax.ShapeDtypeStruct((n, 4 * rows, width), hold.dtype),
        in_specs=[ANY] * 4,
        out_specs=ANY,
        scratch_shapes=[pltpu.SemaphoreType.DMA((4,))],
        name="place",
        **small(bytes_accessed=2 * n * 4 * rows * width * 2),
    )(hold, got, other_hold, other_got)


class Spread:
    def __init__(self, slot, owners_here, order):
        count = lax.axis_size("cols")
        dims = count.bit_length() - 2
        self.me = lax.axis_index("cols")
        self.core = self.me & 1
        self.owners = owners_here
        self.cut = (1, dims)
        self.others = [(b, b - 1) for b in range(2, dims + 1)]
        (give_out,) = cut_slot(self.cut, order, [(False, False)], slot)
        own_out, give_hold, own_hold = cut_slot(
            self.cut, order, [(True, False), (False, True), (True, True)], slot
        )
        self.own = own_out, own_hold
        self.theirs = flip(give_out, (0, 0)), flip(give_hold, (0, 0))

    def bit(self, index, bits):
        return (index >> jnp.where(self.core == 0, bits[0], bits[1])) & 1

    def choose(self, rounds, test, yes, no):
        holds = [test(self.owners[r]) for r in rounds]
        mask = holds[0]
        for at in range(1, len(rounds)):
            if rounds[at] != rounds[at - 1]:
                row = lax.broadcasted_iota(jnp.int32, yes.shape, 0)
                mask = jnp.where(row < at, mask, holds[at])
        return jnp.where(mask, yes, no)

    def begin(self, rounds, rows, *first):
        out, hold = [
            self.choose(rounds, lambda owner: (owner & 1) == self.core, own[rows], theirs[rows])
            for own, theirs in zip(self.own, self.theirs)
        ]
        if first:
            out = after(out, *first)
        return rounds, hold, flip(out, self.cut)

    def keep(self, state, bits):
        rounds, hold, got = state
        mine = self.bit(self.me, bits)
        return self.choose(rounds, lambda owner: mine == self.bit(owner, bits), hold, got)

    def middle(self, state, *first):
        bits = self.cut
        for other in self.others:
            hold = self.keep(state, bits)
            if first:
                hold = after(hold, *first)
                first = ()
            state = (state[0], hold, flip(hold, other))
            bits = other
        return state

    def last(self, state, *first):
        hold = self.keep(state, self.others[-1])
        if first:
            hold = after(hold, *first)
        return hold, flip(hold, self.cut)

    def last_two(self, state, count):
        hold = self.keep(state, self.others[-1])
        return [(part, flip(part, self.cut)) for part in (hold[:count], hold[count:])]

    def join(self, hold, got):
        return place(self.cut, hold, got, flip(hold, (0, 0)), flip(got, (0, 0)))

    def join_above(self, hold, got):
        both = shifted(jnp.stack([hold, got]), "rows", 1)
        other = flip(both, (0, 0))
        return place(self.cut, both[0], both[1], other[0], other[1])


def apply(q, x):
    product = lax.dot_general(q, x, (((0,), (0,)), ((), ())), preferred_element_type=jnp.float32)
    return product.astype(jnp.bfloat16)


def apply_many(q, x):
    product = jnp.einsum("nab,nac->nbc", q, x, preferred_element_type=jnp.float32)
    return product.astype(jnp.bfloat16)


def local(slab, transforms, owners):
    row_block = lax.axis_index("rows")
    last_block = lax.axis_size("rows") - 1
    window = transforms.shape[2]
    border = window // 2
    local_rows, local_cols = slab.shape
    wins = local_rows // window
    rounds = owners.shape[0]
    slot = transforms[0].reshape(2 * wins, 2, 2, window // 4, window)
    crossing = 2 * wins - 1
    middle_one, middle_two = list(range(1, wins - 1)), list(range(wins, crossing))
    order = [crossing, crossing, 0, wins - 1] + middle_one + middle_two
    spread = Spread(slot, owners[:, row_block], order)
    streams = []
    for r in range(rounds):
        across = ([r + 1] if r + 1 < rounds else []) + ([r] if r == 0 else [])
        first = 2 - len(across)
        if r == 0:
            streams.append(spread.middle(spread.begin(across + [r, r], slice(first, 4))))
            streams.append(spread.middle(spread.begin([r] * (len(order) - 4), slice(4, len(order)))))
        else:
            begun = spread.begin(across + [r] * crossing, slice(first, len(order)), streams[r - 1][2])
            streams.append(spread.middle(begun))
    pairs = [spread.last(stream) for stream in streams[:2]]
    for r in range(1, rounds):
        pairs += spread.last_two(streams[r + 1], 3 if r + 1 < rounds else 2)

    matrix = slab
    crosses, above_crosses = {}, {}
    for r in range(rounds):
        head, tail = pairs[2 * r], pairs[2 * r + 1]
        edges = spread.join(*head)
        across = ([r + 1] if r + 1 < rounds else []) + ([r] if r == 0 else [])
        if across:
            n = len(across)
            from_above = spread.join_above(head[0][:n, :, border:], head[1][:n, :, border:])
            for k, q in enumerate(across):
                crosses[q], above_crosses[q] = edges[k], from_above[k]
            edges = edges[n:]
        prev, cross = above_crosses[r], crosses[r]
        outer = apply_many(
            edges[:2], jnp.stack([matrix[:window], matrix[local_rows - window :]])
        )
        head_rows, tail_rows = outer[0], outer[1]
        begin, end = head_rows[:border], tail_rows[border:]
        above, below = swap_rows(begin, end)
        rest = spread.join(*tail)
        ones, twos = rest[: wins - 2], rest[wins - 2 :]
        mid = apply_many(
            ones,
            matrix[window : local_rows - window].reshape(wins - 2, window, local_cols),
        ).reshape(local_rows - 2 * window, local_cols)
        centre = jnp.concatenate([head_rows[border:], mid, tail_rows[:border]], 0)
        inner = apply_many(twos, centre.reshape(wins - 1, window, local_cols)).reshape(
            local_rows - window, local_cols
        )
        low = apply(cross[:, :border], jnp.concatenate([end, below], 0))
        low = jnp.where(row_block == last_block, end, low)
        top = apply(prev, jnp.concatenate([above, begin], 0))
        top = jnp.where(row_block == 0, begin, top)
        matrix = jnp.concatenate([top, inner, low], 0)
    return matrix


def solution(mesh):
    return jax.shard_map(
        local,
        mesh=mesh,
        in_specs=(P("rows", "cols"), P("cols", "rows", None), P()),
        out_specs=P("rows", "cols"),
        check_vma=False,
    )
```

```python
import jax
import jax.numpy as jnp
from jax import lax
from jax.experimental import pallas as pl
from jax.experimental.pallas import tpu as pltpu
from jax.sharding import PartitionSpec as P


def shifted(value, axis, steps):
    count = lax.axis_size(axis)
    initial, last = (max(0, -steps), min(count, count - steps))
    return lax.ppermute(value, axis, [(source, source + steps) for source in range(initial, last)])


def swap_rows(up, down):
    count = lax.axis_size("rows")
    even = (lax.axis_index("rows") & 1) == 0

    def swap(value, start):
        pairs = [(low, low + 1) for low in range(start, count - 1, 2)]
        return lax.ppermute(value, "rows", pairs + [(b, a) for a, b in pairs])

    first = swap(jnp.where(even, down, up), 0)
    second = swap(jnp.where(even, up, down), 1)
    return jnp.where(even, second, first), jnp.where(even, first, second)


def flip(value, bits):
    count = lax.axis_size("cols")
    return lax.ppermute(value, "cols", [(d, d ^ (1 << bits[d & 1])) for d in range(count)])


def copy_all(copies):
    for copy in copies:
        copy.start()
    for copy in copies:
        copy.wait()


def small(flops=0, bytes_accessed=0, limit=1 << 20):
    return dict(
        compiler_params=pltpu.CompilerParams(vmem_limit_bytes=limit),
        cost_estimate=pl.CostEstimate(
            flops=flops, bytes_accessed=bytes_accessed, transcendentals=0
        ),
    )


ANY = pl.BlockSpec(memory_space=pl.ANY)


def after(value, *done):
    def kernel(source, *refs):
        copy_all([pltpu.make_async_copy(source, refs[-2], refs[-1])])

    return pl.pallas_call(
        kernel,
        out_shape=jax.ShapeDtypeStruct(value.shape, value.dtype),
        in_specs=[ANY] * (1 + len(done)),
        out_specs=ANY,
        scratch_shapes=[pltpu.SemaphoreType.DMA],
        name="after",
        **small(bytes_accessed=4 * value.size),
    )(value, *done)


def runs(ms):
    found = []
    for at, m in enumerate(ms):
        if found and found[-1][0] + found[-1][2] == m:
            found[-1][2] += 1
        else:
            found.append([m, at, 1])
    return found


def cut_slot(cut, order, kinds, slot):
    _, _, _, rows, width = slot.shape
    shapes = [jax.ShapeDtypeStruct((len(order), rows, width), slot.dtype) for _ in kinds]
    spans = runs(order)

    def kernel(source, *refs):
        outs, sems = refs[:-1], refs[-1]
        me = lax.axis_index("cols")
        core = me & 1
        bit0 = (me >> cut[0]) & 1
        bit1 = (me >> cut[1]) & 1
        mine = jnp.where(core == 0, bit0, bit1)
        other = jnp.where(core == 0, bit1, bit0)
        copies = []
        for (own, hold), out in zip(kinds, outs):
            half = core if own else 1 - core
            piece = mine if own else other
            piece = piece if hold else 1 - piece
            for first, at, n in spans:
                copies.append(
                    pltpu.make_async_copy(
                        source.at[pl.ds(first, n), half, piece],
                        out.at[pl.ds(at, n)],
                        sems.at[len(copies)],
                    )
                )
        copy_all(copies)

    return pl.pallas_call(
        kernel,
        out_shape=shapes,
        in_specs=[pl.BlockSpec(memory_space=pltpu.HBM)],
        out_specs=[ANY] * len(shapes),
        scratch_shapes=[pltpu.SemaphoreType.DMA((len(spans) * len(kinds),))],
        name="cut_slot",
        **small(bytes_accessed=len(kinds) * slot.size, limit=(48 if len(kinds) == 1 else 1) << 20),
    )(slot)


def place_kernel(cut, hold, got, other_hold, other_got, out, sems):
    me = lax.axis_index("cols")
    core = me & 1
    rows = hold.shape[1]
    bit0 = (me >> cut[0]) & 1
    bit1 = (me >> cut[1]) & 1
    mine = jnp.where(core == 0, bit0, bit1)
    other = jnp.where(core == 0, bit1, bit0)
    slots = (
        (hold, core * 2 + mine),
        (got, core * 2 + 1 - mine),
        (other_hold, (1 - core) * 2 + other),
        (other_got, (1 - core) * 2 + 1 - other),
    )
    copies = [
        pltpu.make_async_copy(
            piece, out.at[:, pl.ds(pl.multiple_of(at * rows, rows), rows), :], sems.at[k]
        )
        for k, (piece, at) in enumerate(slots)
    ]
    copy_all(copies)


def place(cut, hold, got, other_hold, other_got):
    n, rows, width = hold.shape
    return pl.pallas_call(
        lambda *refs: place_kernel(cut, *refs),
        out_shape=jax.ShapeDtypeStruct((n, 4 * rows, width), hold.dtype),
        in_specs=[ANY] * 4,
        out_specs=ANY,
        scratch_shapes=[pltpu.SemaphoreType.DMA((4,))],
        name="place",
        **small(bytes_accessed=2 * n * 4 * rows * width * 2),
    )(hold, got, other_hold, other_got)


class Spread:
    def __init__(self, slot, owners_here, order):
        count = lax.axis_size("cols")
        dims = count.bit_length() - 2
        self.me = lax.axis_index("cols")
        self.core = self.me & 1
        self.owners = owners_here
        self.cut = (1, dims)
        self.others = [(b, b - 1) for b in range(2, dims + 1)]
        (give_out,) = cut_slot(self.cut, order, [(False, False)], slot)
        own_out, give_hold, own_hold = cut_slot(
            self.cut, order, [(True, False), (False, True), (True, True)], slot
        )
        self.own = own_out, own_hold
        self.theirs = flip(give_out, (0, 0)), flip(give_hold, (0, 0))

    def bit(self, index, bits):
        return (index >> jnp.where(self.core == 0, bits[0], bits[1])) & 1

    def choose(self, rounds, test, yes, no):
        holds = [test(self.owners[r]) for r in rounds]
        mask = holds[0]
        for at in range(1, len(rounds)):
            if rounds[at] != rounds[at - 1]:
                row = lax.broadcasted_iota(jnp.int32, yes.shape, 0)
                mask = jnp.where(row < at, mask, holds[at])
        return jnp.where(mask, yes, no)

    def begin(self, rounds, rows, *first):
        out, hold = [
            self.choose(rounds, lambda owner: (owner & 1) == self.core, own[rows], theirs[rows])
            for own, theirs in zip(self.own, self.theirs)
        ]
        if first:
            out = after(out, *first)
        return rounds, hold, flip(out, self.cut)

    def keep(self, state, bits):
        rounds, hold, got = state
        mine = self.bit(self.me, bits)
        return self.choose(rounds, lambda owner: mine == self.bit(owner, bits), hold, got)

    def middle(self, state, *first):
        bits = self.cut
        for other in self.others:
            hold = self.keep(state, bits)
            if first:
                hold = after(hold, *first)
                first = ()
            state = (state[0], hold, flip(hold, other))
            bits = other
        return state

    def last(self, state, *first):
        hold = self.keep(state, self.others[-1])
        if first:
            hold = after(hold, *first)
        return hold, flip(hold, self.cut)

    def last_two(self, state, count):
        hold = self.keep(state, self.others[-1])
        return [(part, flip(part, self.cut)) for part in (hold[:count], hold[count:])]

    def join(self, hold, got):
        return place(self.cut, hold, got, flip(hold, (0, 0)), flip(got, (0, 0)))

    def join_above(self, hold, got):
        both = shifted(jnp.stack([hold, got]), "rows", 1)
        other = flip(both, (0, 0))
        return place(self.cut, both[0], both[1], other[0], other[1])


def apply(q, x):
    product = lax.dot_general(q, x, (((0,), (0,)), ((), ())), preferred_element_type=jnp.float32)
    return product.astype(jnp.bfloat16)


def apply_many(q, x):
    product = jnp.einsum("nab,nac->nbc", q, x, preferred_element_type=jnp.float32)
    return product.astype(jnp.bfloat16)


def write_inner(inner, border):
    rows, cols = inner.shape

    def kernel(source, out):
        out[...] = source[...]

    return pl.pallas_call(
        kernel,
        grid=(rows // border,),
        out_shape=jax.ShapeDtypeStruct((rows + 2 * border, cols), inner.dtype),
        in_specs=[pl.BlockSpec((border, cols), lambda i: (i, 0))],
        out_specs=pl.BlockSpec((border, cols), lambda i: (i + 1, 0)),
        compiler_params=pltpu.CompilerParams(vmem_limit_bytes=8 << 20),
        cost_estimate=pl.CostEstimate(flops=0, bytes_accessed=4 * inner.size, transcendentals=0),
        name="write_inner",
    )(inner)


def write_outer(whole, top, low):
    border, cols = top.shape
    last = whole.shape[0] // border - 1

    def kernel(_, first, final, out):
        @pl.when(pl.program_id(0) == 0)
        def _():
            out[...] = first[...]

        @pl.when(pl.program_id(0) == 1)
        def _():
            out[...] = final[...]

    block = pl.BlockSpec((border, cols), lambda i: (0, 0))
    return pl.pallas_call(
        kernel,
        grid=(2,),
        out_shape=jax.ShapeDtypeStruct(whole.shape, whole.dtype),
        in_specs=[ANY, block, block],
        out_specs=pl.BlockSpec((border, cols), lambda i: (i * last, 0)),
        input_output_aliases={0: 0},
        compiler_params=pltpu.CompilerParams(vmem_limit_bytes=8 << 20),
        cost_estimate=pl.CostEstimate(flops=0, bytes_accessed=8 * top.size, transcendentals=0),
        name="write_outer",
    )(whole, top, low)


def local(slab, transforms, owners):
    row_block = lax.axis_index("rows")
    last_block = lax.axis_size("rows") - 1
    window = transforms.shape[2]
    border = window // 2
    local_rows, local_cols = slab.shape
    wins = local_rows // window
    rounds = owners.shape[0]
    slot = transforms[0].reshape(2 * wins, 2, 2, window // 4, window)
    crossing = 2 * wins - 1
    middle_one, middle_two = list(range(1, wins - 1)), list(range(wins, crossing))
    order = [crossing, crossing, 0, wins - 1] + middle_one + middle_two
    spread = Spread(slot, owners[:, row_block], order)
    streams = []
    for r in range(rounds):
        across = ([r + 1] if r + 1 < rounds else []) + ([r] if r == 0 else [])
        first = 2 - len(across)
        if r == 0:
            streams.append(spread.middle(spread.begin(across + [r, r], slice(first, 4))))
            streams.append(spread.middle(spread.begin([r] * (len(order) - 4), slice(4, len(order)))))
        else:
            begun = spread.begin(across + [r] * crossing, slice(first, len(order)), streams[r - 1][2])
            streams.append(spread.middle(begun))
    pairs = [spread.last(stream) for stream in streams[:2]]
    for r in range(1, rounds):
        pairs += spread.last_two(streams[r + 1], wins + (1 if r + 1 < rounds else 0))

    matrix = slab
    crosses, above_crosses = {}, {}
    for r in range(rounds):
        head, tail = pairs[2 * r], pairs[2 * r + 1]
        edges = spread.join(*head)
        across = ([r + 1] if r + 1 < rounds else []) + ([r] if r == 0 else [])
        if across:
            n = len(across)
            from_above = spread.join_above(head[0][:n, :, border:], head[1][:n, :, border:])
            for k, q in enumerate(across):
                crosses[q], above_crosses[q] = edges[k], from_above[k]
            edges = edges[n:]
        prev, cross = above_crosses[r], crosses[r]
        outer = apply_many(
            edges[:2], jnp.stack([matrix[:window], matrix[local_rows - window :]])
        )
        head_rows, tail_rows = outer[0], outer[1]
        begin, end = head_rows[:border], tail_rows[border:]
        above, below = swap_rows(begin, end)
        rest = spread.join(*tail)
        if r == 0:
            ones, twos = rest[: wins - 2], rest[wins - 2 :]
        else:
            ones, twos = edges[2:], rest
        mid = apply_many(
            ones,
            matrix[window : local_rows - window].reshape(wins - 2, window, local_cols),
        ).reshape(local_rows - 2 * window, local_cols)
        centre = jnp.concatenate([head_rows[border:], mid, tail_rows[:border]], 0)
        inner = apply_many(twos, centre.reshape(wins - 1, window, local_cols)).reshape(
            local_rows - window, local_cols
        )
        low = apply(cross[:, :border], jnp.concatenate([end, below], 0))
        low = jnp.where(row_block == last_block, end, low)
        top = apply(prev, jnp.concatenate([above, begin], 0))
        top = jnp.where(row_block == 0, begin, top)
        if r < rounds - 1:
            matrix = jnp.concatenate([top, inner, low], 0)
    return write_outer(write_inner(inner, border), top, low)


def solution(mesh):
    return jax.shard_map(
        local,
        mesh=mesh,
        in_specs=(P("rows", "cols"), P("cols", "rows", None), P()),
        out_specs=P("rows", "cols"),
        check_vma=False,
    )
```

```python
import jax
import jax.numpy as jnp
from jax import lax
from jax.experimental import pallas as pl
from jax.experimental.pallas import tpu as pltpu
from jax.sharding import PartitionSpec as P


def shifted(value, axis, steps):
    count = lax.axis_size(axis)
    initial, last = (max(0, -steps), min(count, count - steps))
    return lax.ppermute(value, axis, [(source, source + steps) for source in range(initial, last)])


def swap_rows(up, down):
    count = lax.axis_size("rows")
    even = (lax.axis_index("rows") & 1) == 0

    def swap(value, start):
        pairs = [(low, low + 1) for low in range(start, count - 1, 2)]
        return lax.ppermute(value, "rows", pairs + [(b, a) for a, b in pairs])

    first = swap(jnp.where(even, down, up), 0)
    second = swap(jnp.where(even, up, down), 1)
    return jnp.where(even, second, first), jnp.where(even, first, second)


def flip(value, bits):
    count = lax.axis_size("cols")
    return lax.ppermute(value, "cols", [(d, d ^ (1 << bits[d & 1])) for d in range(count)])


def copy_all(copies):
    for copy in copies:
        copy.start()
    for copy in copies:
        copy.wait()


def small(flops=0, bytes_accessed=0, limit=1 << 20):
    return dict(
        compiler_params=pltpu.CompilerParams(vmem_limit_bytes=limit),
        cost_estimate=pl.CostEstimate(
            flops=flops, bytes_accessed=bytes_accessed, transcendentals=0
        ),
    )


ANY = pl.BlockSpec(memory_space=pl.ANY)


def after(value, *done):
    def kernel(source, *refs):
        copy_all([pltpu.make_async_copy(source, refs[-2], refs[-1])])

    return pl.pallas_call(
        kernel,
        out_shape=jax.ShapeDtypeStruct(value.shape, value.dtype),
        in_specs=[ANY] * (1 + len(done)),
        out_specs=ANY,
        scratch_shapes=[pltpu.SemaphoreType.DMA],
        name="after",
        **small(bytes_accessed=4 * value.size),
    )(value, *done)


def runs(ms):
    found = []
    for at, m in enumerate(ms):
        if found and found[-1][0] + found[-1][2] == m:
            found[-1][2] += 1
        else:
            found.append([m, at, 1])
    return found


def cut_slot(cut, order, kinds, slot):
    _, _, _, rows, width = slot.shape
    shapes = [jax.ShapeDtypeStruct((len(order), rows, width), slot.dtype) for _ in kinds]
    spans = runs(order)

    def kernel(source, *refs):
        outs, sems = refs[:-1], refs[-1]
        me = lax.axis_index("cols")
        core = me & 1
        bit0 = (me >> cut[0]) & 1
        bit1 = (me >> cut[1]) & 1
        mine = jnp.where(core == 0, bit0, bit1)
        other = jnp.where(core == 0, bit1, bit0)
        copies = []
        for (own, hold), out in zip(kinds, outs):
            half = core if own else 1 - core
            piece = mine if own else other
            piece = piece if hold else 1 - piece
            for first, at, n in spans:
                copies.append(
                    pltpu.make_async_copy(
                        source.at[pl.ds(first, n), half, piece],
                        out.at[pl.ds(at, n)],
                        sems.at[len(copies)],
                    )
                )
        copy_all(copies)

    return pl.pallas_call(
        kernel,
        out_shape=shapes,
        in_specs=[pl.BlockSpec(memory_space=pltpu.HBM)],
        out_specs=[ANY] * len(shapes),
        scratch_shapes=[pltpu.SemaphoreType.DMA((len(spans) * len(kinds),))],
        name="cut_slot",
        **small(bytes_accessed=len(kinds) * slot.size, limit=(48 if len(kinds) == 1 else 1) << 20),
    )(slot)


def place_kernel(cut, hold, got, other_hold, other_got, out, sems):
    me = lax.axis_index("cols")
    core = me & 1
    rows = hold.shape[1]
    bit0 = (me >> cut[0]) & 1
    bit1 = (me >> cut[1]) & 1
    mine = jnp.where(core == 0, bit0, bit1)
    other = jnp.where(core == 0, bit1, bit0)
    slots = (
        (hold, core * 2 + mine),
        (got, core * 2 + 1 - mine),
        (other_hold, (1 - core) * 2 + other),
        (other_got, (1 - core) * 2 + 1 - other),
    )
    copies = [
        pltpu.make_async_copy(
            piece, out.at[:, pl.ds(pl.multiple_of(at * rows, rows), rows), :], sems.at[k]
        )
        for k, (piece, at) in enumerate(slots)
    ]
    copy_all(copies)


def place(cut, hold, got, other_hold, other_got):
    n, rows, width = hold.shape
    return pl.pallas_call(
        lambda *refs: place_kernel(cut, *refs),
        out_shape=jax.ShapeDtypeStruct((n, 4 * rows, width), hold.dtype),
        in_specs=[ANY] * 4,
        out_specs=ANY,
        scratch_shapes=[pltpu.SemaphoreType.DMA((4,))],
        name="place",
        **small(bytes_accessed=2 * n * 4 * rows * width * 2),
    )(hold, got, other_hold, other_got)


class Spread:
    def __init__(self, slot, owners_here, order):
        count = lax.axis_size("cols")
        dims = count.bit_length() - 2
        self.me = lax.axis_index("cols")
        self.core = self.me & 1
        self.owners = owners_here
        self.cut = (1, dims)
        self.others = [(b, b - 1) for b in range(2, dims + 1)]
        (give_out,) = cut_slot(self.cut, order, [(False, False)], slot)
        own_out, give_hold, own_hold = cut_slot(
            self.cut, order, [(True, False), (False, True), (True, True)], slot
        )
        self.own = own_out, own_hold
        self.theirs = flip(give_out, (0, 0)), flip(give_hold, (0, 0))

    def bit(self, index, bits):
        return (index >> jnp.where(self.core == 0, bits[0], bits[1])) & 1

    def choose(self, rounds, test, yes, no):
        holds = [test(self.owners[r]) for r in rounds]
        mask = holds[0]
        for at in range(1, len(rounds)):
            if rounds[at] != rounds[at - 1]:
                row = lax.broadcasted_iota(jnp.int32, yes.shape, 0)
                mask = jnp.where(row < at, mask, holds[at])
        return jnp.where(mask, yes, no)

    def begin(self, rounds, rows, *first):
        out, hold = [
            self.choose(rounds, lambda owner: (owner & 1) == self.core, own[rows], theirs[rows])
            for own, theirs in zip(self.own, self.theirs)
        ]
        if first:
            out = after(out, *first)
        return rounds, hold, flip(out, self.cut)

    def keep(self, state, bits):
        rounds, hold, got = state
        mine = self.bit(self.me, bits)
        return self.choose(rounds, lambda owner: mine == self.bit(owner, bits), hold, got)

    def middle(self, state, *first):
        bits = self.cut
        for other in self.others:
            hold = self.keep(state, bits)
            if first:
                hold = after(hold, *first)
                first = ()
            state = (state[0], hold, flip(hold, other))
            bits = other
        return state

    def last(self, state, *first):
        hold = self.keep(state, self.others[-1])
        if first:
            hold = after(hold, *first)
        return hold, flip(hold, self.cut)

    def last_two(self, state, count):
        hold = self.keep(state, self.others[-1])
        return [(part, flip(part, self.cut)) for part in (hold[:count], hold[count:])]

    def join(self, hold, got):
        return place(self.cut, hold, got, flip(hold, (0, 0)), flip(got, (0, 0)))

    def join_above(self, hold, got):
        both = shifted(jnp.stack([hold, got]), "rows", 1)
        other = flip(both, (0, 0))
        return place(self.cut, both[0], both[1], other[0], other[1])


def apply(q, x):
    product = lax.dot_general(q, x, (((0,), (0,)), ((), ())), preferred_element_type=jnp.float32)
    return product.astype(jnp.bfloat16)


def apply_many(q, x):
    product = jnp.einsum("nab,nac->nbc", q, x, preferred_element_type=jnp.float32)
    return product.astype(jnp.bfloat16)


def write_inner(inner, border):
    rows, cols = inner.shape

    def kernel(source, out):
        out[...] = source[...]

    return pl.pallas_call(
        kernel,
        grid=(rows // border,),
        out_shape=jax.ShapeDtypeStruct((rows + 2 * border, cols), inner.dtype),
        in_specs=[pl.BlockSpec((border, cols), lambda i: (i, 0))],
        out_specs=pl.BlockSpec((border, cols), lambda i: (i + 1, 0)),
        compiler_params=pltpu.CompilerParams(vmem_limit_bytes=8 << 20),
        cost_estimate=pl.CostEstimate(flops=0, bytes_accessed=4 * inner.size, transcendentals=0),
        name="write_inner",
    )(inner)


def write_outer(whole, top, low):
    border, cols = top.shape
    last = whole.shape[0] // border - 1

    def kernel(_, first, final, out):
        @pl.when(pl.program_id(0) == 0)
        def _():
            out[...] = first[...]

        @pl.when(pl.program_id(0) == 1)
        def _():
            out[...] = final[...]

    block = pl.BlockSpec((border, cols), lambda i: (0, 0))
    return pl.pallas_call(
        kernel,
        grid=(2,),
        out_shape=jax.ShapeDtypeStruct(whole.shape, whole.dtype),
        in_specs=[ANY, block, block],
        out_specs=pl.BlockSpec((border, cols), lambda i: (i * last, 0)),
        input_output_aliases={0: 0},
        compiler_params=pltpu.CompilerParams(vmem_limit_bytes=8 << 20),
        cost_estimate=pl.CostEstimate(flops=0, bytes_accessed=8 * top.size, transcendentals=0),
        name="write_outer",
    )(whole, top, low)


def local(slab, transforms, owners):
    row_block = lax.axis_index("rows")
    last_block = lax.axis_size("rows") - 1
    window = transforms.shape[2]
    border = window // 2
    local_rows, local_cols = slab.shape
    wins = local_rows // window
    rounds = owners.shape[0]
    slot = transforms[0].reshape(2 * wins, 2, 2, window // 4, window)
    crossing = 2 * wins - 1
    middle_one, middle_two = list(range(1, wins - 1)), list(range(wins, crossing))
    order = [crossing, crossing, 0, wins - 1] + middle_one + middle_two
    spread = Spread(slot, owners[:, row_block], order)
    streams, opening = [], None
    for r in range(rounds):
        across = ([r + 1] if r + 1 < rounds else []) + ([r] if r == 0 else [])
        first = 2 - len(across)
        if r == 0:
            streams.append(spread.middle(spread.begin(across + [r, r], slice(first, 4))))
            opening = spread.begin([r] * (len(order) - 4), slice(4, len(order)))
            streams.append(spread.middle(opening))
        else:
            begun = spread.begin(across + [r] * crossing, slice(first, len(order)), opening[2])
            streams.append(spread.middle(begun))
            opening = begun
    pairs = [spread.last(stream) for stream in streams[:2]]
    for r in range(1, rounds):
        pairs += spread.last_two(streams[r + 1], 3 if r + 1 < rounds else 2)

    matrix = slab
    crosses, above_crosses = {}, {}
    for r in range(rounds):
        head, tail = pairs[2 * r], pairs[2 * r + 1]
        edges = spread.join(*head)
        across = ([r + 1] if r + 1 < rounds else []) + ([r] if r == 0 else [])
        if across:
            n = len(across)
            from_above = spread.join_above(head[0][:n, :, border:], head[1][:n, :, border:])
            for k, q in enumerate(across):
                crosses[q], above_crosses[q] = edges[k], from_above[k]
            edges = edges[n:]
        prev, cross = above_crosses[r], crosses[r]
        outer = apply_many(
            edges[:2], jnp.stack([matrix[:window], matrix[local_rows - window :]])
        )
        head_rows, tail_rows = outer[0], outer[1]
        begin, end = head_rows[:border], tail_rows[border:]
        above, below = swap_rows(begin, end)
        rest = spread.join(*tail)
        ones, twos = rest[: wins - 2], rest[wins - 2 :]
        mid = apply_many(
            ones,
            matrix[window : local_rows - window].reshape(wins - 2, window, local_cols),
        ).reshape(local_rows - 2 * window, local_cols)
        centre = jnp.concatenate([head_rows[border:], mid, tail_rows[:border]], 0)
        inner = apply_many(twos, centre.reshape(wins - 1, window, local_cols)).reshape(
            local_rows - window, local_cols
        )
        low = apply(cross[:, :border], jnp.concatenate([end, below], 0))
        low = jnp.where(row_block == last_block, end, low)
        top = apply(prev, jnp.concatenate([above, begin], 0))
        top = jnp.where(row_block == 0, begin, top)
        if r < rounds - 1:
            matrix = jnp.concatenate([top, inner, low], 0)
    return write_outer(write_inner(inner, border), top, low)


def solution(mesh):
    return jax.shard_map(
        local,
        mesh=mesh,
        in_specs=(P("rows", "cols"), P("cols", "rows", None), P()),
        out_specs=P("rows", "cols"),
        check_vma=False,
    )
```
